128 devices in a mesh: shard: 8 (over z_hi, x), rep: 16 (over y, z_lo, core).
Axes of the slice: x: 4, y: 4, z: 4 (z_hi: 2, z_lo: 2; z = z_hi * 2 + z_lo), core: 2. Of those that a mesh axis runs over, the one named last changes fastest.
Arguments:
- latents: bfloat16 [1024, 256, 384], P(('shard', 'rep')), may hold values from -6 to 6
- conditions: bfloat16 [1024, 384], P(('shard', 'rep')), may hold values from -6 to 6
- counts: int32 [128], P(('shard', 'rep')), may hold values from 0 to 8, as said below
- mod_weight: bfloat16 [384, 2304], P('shard'), may hold values from -0.3125 to 0.3125
- mod_bias: bfloat16 [2304], P('shard'), may hold values from -3 to 3
- qkv_weight: bfloat16 [384, 1152], P('shard'), may hold values from -0.3125 to 0.3125
- qv_bias: bfloat16 [768], P('shard'), may hold values from -3 to 3
- proj_weight: bfloat16 [384, 384], P('shard'), may hold values from -1.25 to 1.25
- proj_bias: bfloat16 [384], P('shard'), may hold values from -3 to 3
- up_weight: bfloat16 [384, 1536], P('shard'), may hold values from -0.3125 to 0.3125
- up_bias: bfloat16 [1536], P('shard'), may hold values from -3 to 3
- down_weight: bfloat16 [1536, 384], P('shard'), may hold values from -0.15625 to 0.15625
- down_bias: bfloat16 [384], P('shard'), may hold values from -3 to 3
- grad_out: bfloat16 [1024, 256, 384], P(('shard', 'rep')), may hold values from -6 to 6
Outputs:
- output: bfloat16 [1024, 256, 384], P(('shard', 'rep'))
- grad_latents: bfloat16 [1024, 256, 384], P(('shard', 'rep'))
- grad_conditions: bfloat16 [1024, 384], P(('shard', 'rep'))
- grad_mod_weight: float32 [384, 2304], P('shard')
- grad_mod_bias: float32 [2304], P('shard')
- grad_qkv_weight: float32 [384, 1152], P('shard')
- grad_qv_bias: float32 [768], P('shard')
- grad_proj_weight: float32 [384, 384], P('shard')
- grad_proj_bias: float32 [384], P('shard')
- grad_up_weight: float32 [384, 1536], P('shard')
- grad_up_bias: float32 [1536], P('shard')
- grad_down_weight: float32 [1536, 384], P('shard')
- grad_down_bias: float32 [384], P('shard')
The draws below stay inside these ranges and needn't reach their ends.
Inputs may be any that keep to these rules, and one draw needn't show every extreme that they name: Device d (shard index slowest, then rep) holds its latents in its first counts[d] of 8 slots; the other slots are padding. Some device holds 8 latents and some holds none.
All inputs are finite; a program needn't handle non-finite values.
Results may differ from the reference program's by a relative error of at most 0.023.
Values may be sent and summed in bfloat16 or wider, within the bound.
No kernel may reach another device: no remote copies, remote signals or barrier semaphores. Data moves between devices by JAX's collectives and lax.ppermute only.
A program may use at most 192 MiB of HBM per device.

```python
import jax
import jax.numpy as jnp
from jax import lax

D = 384
HEADS = 6
HEAD_DIM = 64
FF = 1536
LAT_TOK = 256
CAP = 8
SLOTS = 1024


def draw_counts(key, part):
    key = jax.random.fold_in(key, 7)
    first, second = jax.random.split(key)
    number = SLOTS // CAP
    base = jax.random.randint(first, (number,), 0, CAP + 1)
    order = jax.random.permutation(second, number)
    base = base.at[order[0]].set(CAP)
    base = base.at[order[1]].set(0)
    return base.astype(jnp.int32)


def block_levels(rng, shape, cuts, least, largest):
    loudness, own = 1.0, jax.random.fold_in(rng, 6)
    for dim, parts in cuts:
        heights = jnp.exp(jax.random.uniform(jax.random.fold_in(own, dim), (parts,), jnp.float32, least / len(cuts), largest / len(cuts)))
        loudness = loudness * jnp.repeat(heights, shape[dim] // parts).reshape([-1 if axis == dim else 1 for axis in range(len(shape))])
    return loudness


def gaussian(key, shape, deviation, bound, cuts=(), held_as=jnp.bfloat16):
    entries = jax.random.normal(key, shape, jnp.float32) * deviation
    if len(cuts) > 0:
        entries = block_levels(key, shape, cuts, -0.22, 0.18) * entries
    return jnp.clip(entries, min=-bound, max=bound).astype(held_as)


def setup_inputs(seed: int = 0) -> dict:
    key_of = jax.random.split(jax.random.key(seed), 15)
    return {
        "latents": gaussian(key_of[0], (SLOTS, LAT_TOK, D), 1.0, 6.0, ((0, 128),)),
        "conditions": gaussian(key_of[1], (SLOTS, D), 1.0, 6.0, ((0, 128),)),
        "counts": draw_counts(jax.random.fold_in(key_of[14], 71), 0),
        "mod_weight": gaussian(key_of[3], (D, 6 * D), D ** -0.5, 0.3125, ((0, 8),)),
        "mod_bias": gaussian(key_of[4], (6 * D,), 0.5, 3.0, ((0, 8),)),
        "qkv_weight": gaussian(key_of[5], (D, 3 * D), D ** -0.5, 0.3125, ((0, 8),)),
        "qv_bias": gaussian(key_of[6], (2 * D,), 0.5, 3.0, ((0, 8),)),
        "proj_weight": gaussian(key_of[7], (D, D), (D // 16) ** -0.5, 1.25, ((0, 8),)),
        "proj_bias": gaussian(key_of[8], (D,), 0.5, 3.0, ((0, 8),)),
        "up_weight": gaussian(key_of[9], (D, FF), D ** -0.5, 0.3125, ((0, 8),)),
        "up_bias": gaussian(key_of[10], (FF,), 0.5, 3.0, ((0, 8),)),
        "down_weight": gaussian(key_of[11], (FF, D), FF ** -0.5, 0.15625, ((0, 8),)),
        "down_bias": gaussian(key_of[12], (D,), 0.5, 3.0, ((0, 8),)),
        "grad_out": gaussian(key_of[13], (SLOTS, LAT_TOK, D), 1.0, 6.0, ((0, 128),)),
    }


@jax.custom_vjp
def low(v):
    return lax.optimization_barrier(v.astype(jnp.bfloat16)).astype(jnp.float32)

@jax.custom_vjp
def low_back(v):
    return v

def low_keep(v):
    return (low(v), None)

def low_pass(kept, grad):
    return (grad,)

def back_keep(v):
    return (v, None)

def back_low(kept, grad):
    return (low(grad),)
low.defvjp(low_keep, low_pass)
low_back.defvjp(back_keep, back_low)

def matmul(left, right):
    return jnp.dot(left, right, precision=lax.Precision.HIGHEST)

def normalize(value):
    center = lax.optimization_barrier(jnp.mean(value, axis=-1, keepdims=True))
    centered = value - center
    spread = lax.optimization_barrier(jnp.mean(centered * centered, axis=-1, keepdims=True))
    return centered * lax.rsqrt(spread + 1e-06)

def forward(params, latents, conditions, valid):
    mod_weight, mod_bias, qkv_weight, qv_bias, proj_weight, proj_bias, up_weight, up_bias, down_weight, down_bias = params
    group = latents.shape[0]
    rows = group * LAT_TOK
    modulation = low_back(matmul(low(jax.nn.silu(conditions)), mod_weight) + mod_bias)
    pieces = jnp.split(modulation, 6, axis=-1)
    shift_one, scale_one, gate_one, shift_two, scale_two, gate_two = [piece[:, None, :] for piece in pieces]
    hidden_one = low(normalize(latents) * (1.0 + scale_one) + shift_one)
    full_bias = jnp.concatenate([qv_bias[:D], jnp.zeros((D,), jnp.float32), qv_bias[D:]])
    qkv = low(low_back(matmul(hidden_one.reshape(rows, D), qkv_weight) + full_bias))
    qkv = qkv.reshape(group, LAT_TOK, 3, HEADS, HEAD_DIM)
    queries, keys, values = (qkv[:, :, 0], qkv[:, :, 1], qkv[:, :, 2])
    scores = low_back(jnp.einsum('gqhd,gkhd->ghqk', queries, keys, precision=lax.Precision.HIGHEST) * HEAD_DIM ** (-0.5))
    probs = low(jax.nn.softmax(scores, axis=-1))
    mixed = jnp.einsum('ghqk,gkhd->gqhd', probs, values, precision=lax.Precision.HIGHEST)
    mixed = low(low_back(mixed)).reshape(rows, D)
    branch_one = low_back(matmul(mixed, proj_weight) + proj_bias).reshape(group, LAT_TOK, D)
    middle = latents + gate_one * branch_one
    hidden_two = low(normalize(middle) * (1.0 + scale_two) + shift_two).reshape(rows, D)
    upward = low_back(matmul(hidden_two, up_weight) + up_bias)
    act_low = low(jax.nn.gelu(upward, approximate=True))
    branch_two = low_back(matmul(act_low, down_weight) + down_bias).reshape(group, LAT_TOK, D)
    return (middle + gate_two * branch_two) * valid[:, None, None]

def reference(latents, conditions, counts, mod_weight, mod_bias, qkv_weight, qv_bias, proj_weight, proj_bias, up_weight, up_bias, down_weight, down_bias, grad_out):
    params = tuple((w.astype(jnp.float32) for w in (mod_weight, mod_bias, qkv_weight, qv_bias, proj_weight, proj_bias, up_weight, up_bias, down_weight, down_bias)))
    slot = jnp.arange(SLOTS, dtype=jnp.int32)
    valid = (slot % CAP < counts[slot // CAP]).astype(jnp.float32)
    group = 16
    steps_count = SLOTS // group
    lat_blocks = latents.astype(jnp.float32).reshape(steps_count, group, LAT_TOK, D)
    cond_blocks = conditions.astype(jnp.float32).reshape(steps_count, group, D)
    valid_blocks = valid.reshape(steps_count, group)
    cot_blocks = grad_out.astype(jnp.float32).reshape(steps_count, group, LAT_TOK, D)

    def step(totals, block):
        lat, cond, flags, cot = block
        result, pull = jax.vjp(lambda p, a, b: forward(p, a, b, flags), params, lat, cond)
        grad_params, grad_lat, grad_cond = pull(cot)
        totals = tuple((a + b for a, b in zip(totals, grad_params)))
        return (totals, (result.astype(jnp.bfloat16), grad_lat.astype(jnp.bfloat16), grad_cond.astype(jnp.bfloat16)))
    start = tuple((jnp.zeros_like(p) for p in params))
    totals, (outputs, grad_lats, grad_conds) = lax.scan(step, start, (lat_blocks, cond_blocks, valid_blocks, cot_blocks))
    return (outputs.reshape(SLOTS, LAT_TOK, D), grad_lats.reshape(SLOTS, LAT_TOK, D), grad_conds.reshape(SLOTS, D), totals[0], totals[1], totals[2], totals[3], totals[4], totals[5], totals[6], totals[7], totals[8], totals[9])
```

```python
import functools

import jax
import jax.numpy as jnp
from jax import lax
from jax.experimental import pallas as pl
from jax.experimental.pallas import tpu as pltpu
from jax.sharding import PartitionSpec as P

D = 384
HEADS = 6
HEAD_DIM = 64
FF = 1536
TOK = 256
CAP = 8
STEP = 1
TWIN = 128
BF = jnp.bfloat16
F32 = jnp.float32
VMEM_BYTES = 56 * 1024 * 1024

LANES_ONE = 2048
QKV_W = 3 * D
MOD_ONE = 2 * D
BIAS_ONE = QKV_W + MOD_ONE
LANES_TWO = 5120
MOD_TWO = 4 * D
AT_MOD = FF
AT_PROJ = AT_MOD + MOD_TWO
AT_DOWN = AT_PROJ + D
BIAS_TWO = AT_DOWN + FF
ROW_QKV, ROW_MOD, ROW_PROJ, ROW_UP, ROW_DOWN = 0, 9, 27, 30, 42


def dot(left, right):
    return jnp.dot(left, right, preferred_element_type=F32)


def dot_tn(left, right):
    return lax.dot_general(left, right, (((0,), (0,)), ((), ())), preferred_element_type=F32)


def dot_nt(left, right):
    return lax.dot_general(left, right, (((1,), (1,)), ((), ())), preferred_element_type=F32)


def normalize(value):
    center = jnp.mean(value, axis=-1, keepdims=True)
    centered = value - center
    spread = jnp.mean(centered * centered, axis=-1, keepdims=True)
    inverse = lax.rsqrt(spread + 1e-06)
    return centered * inverse, inverse


def norm_back(grad, normed, inverse):
    first = jnp.mean(grad, axis=-1, keepdims=True)
    second = jnp.mean(grad * normed, axis=-1, keepdims=True)
    return inverse * (grad - first - normed * second)


def bias_row(bias, first, count):
    return jnp.concatenate([bias[first + i : first + i + 1, :] for i in range(count)], axis=1)


def silu(cond):
    return cond * (1.0 / (1.0 + jnp.exp(-cond)))


def assemble(info, pieces, full):
    column, z_high, core = info[1], info[2], info[3]
    for k in range(4):
        spot = lax.rem(column + k, 4) * 48
        mine = (z_high ^ core) * 192 + spot
        other = (1 - (z_high ^ core)) * 192 + spot
        full[pl.ds(pl.multiple_of(mine, 16), 48), :] = pieces[k][...]
        full[pl.ds(pl.multiple_of(other, 16), 48), :] = pieces[4 + k][...]


def forward_kernel(
    info, latents, conditions, p0, p1, p2, p3, p4, p5, p6, p7,
    weights, bias_out, mod_out, qkv_out, expo_out, mixed_out, rinv_out, hidden_out,
):
    step = pl.program_id(0)

    @pl.when(step == 0)
    def _():
        assemble(info, (p0, p1, p2, p3, p4, p5, p6, p7), weights)
        total = jnp.zeros((48, 128), F32)
        for k in range(8):
            total += weights[48 * k : 48 * k + 48, BIAS_ONE : BIAS_ONE + 128].astype(F32)
        bias_out[...] = total
        cond_low = silu(conditions[...].astype(F32)).astype(BF)
        mod_out[...] = dot(cond_low, weights[:, QKV_W : QKV_W + MOD_ONE]) + bias_row(
            total, ROW_MOD, 6
        )

    @pl.when(step < info[0])
    def _():
        mod = mod_out[pl.ds(step, 1), :]
        normed, _ = normalize(latents[0].astype(F32))
        hidden = (normed * (1.0 + mod[:, D : 2 * D]) + mod[:, :D]).astype(BF)
        hidden_out[0] = hidden
        full_bias = bias_row(bias_out[0:16, :], ROW_QKV, 9)
        qkv = (dot(hidden, weights[:, :QKV_W]) + full_bias).astype(BF)
        qkv_out[0] = qkv
        low = lax.broadcasted_iota(jnp.int32, (TOK, 128), 1) < HEAD_DIM
        ones = jnp.ones((TOK, 128), BF)
        for pair in range(HEADS // 2):
            at = 128 * pair
            query = qkv[:, at : at + 128] * jnp.asarray(HEAD_DIM**-0.5, BF)
            key = qkv[:, D + at : D + at + 128]
            value = jnp.concatenate([qkv[:, 2 * D + at : 2 * D + at + 128], ones], axis=1)
            parts = []
            for half in range(2):
                chosen = jnp.where(low if half == 0 else ~low, query, jnp.zeros_like(query))
                scores = dot_nt(chosen, key)
                expo = jnp.exp(scores - jnp.max(scores, axis=-1, keepdims=True)).astype(BF)
                expo_out[0, 2 * pair + half] = expo
                parts.append(dot(expo, value))
            total = jnp.where(low, parts[0][:, 128:], parts[1][:, 128:])
            inverse = 1.0 / total
            rinv_out[0, :, at : at + 128] = inverse
            mixed_out[0, :, at : at + 128] = (
                jnp.where(low, parts[0][:, :128], parts[1][:, :128]) * inverse
            ).astype(BF)


def middle_kernel(
    info, latents, conditions, mixed_in, grad_out, bias_in, p0, p1, p2, p3, p4, p5, p6, p7,
    weights, out, grad_mid_out, grad_mixed_out, grad_mod, keep, send,
    mod, acc_up, acc_down, acc_proj, acc_bias,
):
    step = pl.program_id(0)

    @pl.when(step == 0)
    def _():
        assemble(info, (p0, p1, p2, p3, p4, p5, p6, p7), weights)
        cond_low = silu(conditions[...].astype(F32)).astype(BF)
        mod[...] = dot(cond_low, weights[:, AT_MOD : AT_MOD + MOD_TWO]) + bias_row(
            bias_in[...], ROW_MOD + 6, 12
        )
        acc_up[...] = jnp.zeros_like(acc_up)
        acc_down[...] = jnp.zeros_like(acc_down)
        acc_proj[...] = jnp.zeros_like(acc_proj)
        acc_bias[...] = jnp.zeros_like(acc_bias)
        grad_mod[...] = jnp.zeros_like(grad_mod)

    @pl.when(step >= info[0])
    def _():
        out[0] = jnp.zeros((TOK, D), BF)

    @pl.when(step < info[0])
    def _():
        row = mod[pl.ds(step, 1), :]
        gate_one, shift_two = row[:, :D], row[:, D : 2 * D]
        scale_two, gate_two = row[:, 2 * D : 3 * D], row[:, 3 * D :]
        bias = bias_in[...]
        mixed = mixed_in[0]
        w_proj = weights[:, AT_PROJ : AT_PROJ + D]
        branch_one = dot(mixed, w_proj) + bias_row(bias, ROW_PROJ, 3)
        middle = latents[0].astype(F32) + gate_one * branch_one
        normed, inverse = normalize(middle)
        hidden = (normed * (1.0 + scale_two) + shift_two).astype(BF)
        cot = grad_out[0].astype(F32)
        g_two = (cot * gate_two).astype(BF)
        up_bias = bias_row(bias, ROW_UP, 12)
        branch_two = bias_row(bias, ROW_DOWN, 3)
        d_hidden = jnp.zeros((TOK, D), F32)
        root = 0.7978845608028654
        cube = root * 0.044715
        for chunk in range(4):
            at = D * chunk
            w_up = weights[:, at : at + D]
            w_down = jnp.concatenate(
                [
                    weights[48 * s : 48 * s + 48, AT_DOWN + D * q : AT_DOWN + D * q + D]
                    for s in (2 * chunk, 2 * chunk + 1)
                    for q in range(4)
                ],
                axis=0,
            )
            upward = dot(hidden, w_up) + up_bias[:, at : at + D]
            square = upward * upward
            bend = jnp.tanh(upward * (root + cube * square))
            half = 0.5 + 0.5 * bend
            act = upward * half
            slope = half + act * (1.0 - bend) * (root + (3.0 * cube) * square)
            act_low = act.astype(BF)
            branch_two = branch_two + dot(act_low, w_down)
            acc_down[at : at + D, :] += dot_tn(act_low, g_two)
            g_up = (slope * dot_nt(g_two, w_down)).astype(BF)
            acc_up[:, at : at + D] += dot_tn(hidden, g_up)
            acc_bias[0:1, at : at + D] += jnp.sum(g_up.astype(F32), axis=0, keepdims=True)
            d_hidden = d_hidden + dot_nt(g_up, w_up)
        out[0] = (middle + gate_two * branch_two).astype(BF)
        acc_bias[1:2, :D] += jnp.sum(g_two.astype(F32), axis=0, keepdims=True)
        grad_mod[pl.ds(step, 1), 3 * D :] = jnp.sum(cot * branch_two, axis=0, keepdims=True)
        grad_mod[pl.ds(step, 1), D : 2 * D] = jnp.sum(d_hidden, axis=0, keepdims=True)
        grad_mod[pl.ds(step, 1), 2 * D : 3 * D] = jnp.sum(
            d_hidden * normed, axis=0, keepdims=True
        )
        grad_mid = cot + norm_back(d_hidden * (1.0 + scale_two), normed, inverse)
        grad_mid_out[0] = grad_mid
        grad_mod[pl.ds(step, 1), :D] = jnp.sum(grad_mid * branch_one, axis=0, keepdims=True)
        g_one = (grad_mid * gate_one).astype(BF)
        acc_bias[2:3, :D] += jnp.sum(g_one.astype(F32), axis=0, keepdims=True)
        acc_proj[...] += dot_tn(mixed, g_one)
        grad_mixed_out[0] = dot_nt(g_one, w_proj).astype(BF)

    @pl.when(step == CAP - 1)
    def _():
        cond_low = silu(conditions[...].astype(F32)).astype(BF)
        g_mod = grad_mod[...].astype(BF)
        mod_grad = dot_tn(cond_low.astype(F32), g_mod.astype(F32)).astype(BF)
        z_high, core, column = info[2], info[3], info[1]
        sums = jnp.sum(g_mod.astype(F32), axis=0, keepdims=True)
        rows = [jnp.zeros((ROW_MOD + 6, 128), F32)]
        rows += [sums[:, 128 * i : 128 * i + 128] for i in range(12)]
        rows += [acc_bias[2:3, 128 * i : 128 * i + 128] for i in range(3)]
        rows += [acc_bias[0:1, 128 * i : 128 * i + 128] for i in range(12)]
        rows += [acc_bias[1:2, 128 * i : 128 * i + 128] for i in range(3)]
        rows += [jnp.zeros((3, 128), F32)]
        bias_block = jnp.concatenate(rows, axis=0).astype(BF)
        for owner in range(8):
            zh, xx = owner // 4, owner % 4
            spot = lax.rem(xx - column + 4, 4) * 48
            spot = pl.multiple_of(spot, 16)
            is_mine = (z_high ^ core) == zh
            lo = 48 * owner

            def put(ref, spot=spot, lo=lo, owner=owner):
                ref[pl.ds(spot, 48), :FF] = acc_up[lo : lo + 48, :].astype(BF)
                ref[pl.ds(spot, 48), AT_MOD : AT_MOD + MOD_TWO] = mod_grad[lo : lo + 48, :]
                ref[pl.ds(spot, 48), AT_PROJ : AT_PROJ + D] = acc_proj[lo : lo + 48, :].astype(BF)
                for q in range(4):
                    at = 192 * owner + 48 * q
                    ref[pl.ds(spot, 48), AT_DOWN + D * q : AT_DOWN + D * q + D] = acc_down[
                        at : at + 48, :
                    ].astype(BF)
                ref[pl.ds(spot, 48), BIAS_TWO : BIAS_TWO + 128] = bias_block

            pl.when(is_mine)(functools.partial(put, keep))
            pl.when(jnp.logical_not(is_mine))(functools.partial(put, send))


def backward_kernel(
    info, latents, conditions, qkv_in, expo_in, mixed_in, rinv_in, hidden_in, grad_mid_in,
    grad_mixed_in, mod_in, weights, weights_two, grad_mod_two,
    out, grad_cond, keep, send,
    acc_qkv, acc_bias, grad_mod,
):
    step = pl.program_id(0)

    @pl.when(step == 0)
    def _():
        acc_qkv[...] = jnp.zeros_like(acc_qkv)
        acc_bias[...] = jnp.zeros_like(acc_bias)
        grad_mod[...] = jnp.zeros_like(grad_mod)

    @pl.when(step >= info[0])
    def _():
        out[0] = jnp.zeros((TOK, D), BF)

    @pl.when(step < info[0])
    def _():
        row = mod_in[pl.ds(step, 1), :]
        normed, inverse = normalize(latents[0].astype(F32))
        qkv = qkv_in[0]
        hidden = hidden_in[0]
        scaled = (grad_mixed_in[0].astype(F32) * rinv_in[0]).astype(BF)
        product = scaled.astype(F32) * mixed_in[0].astype(F32)
        low = lax.broadcasted_iota(jnp.int32, (TOK, 128), 1) < HEAD_DIM
        low_wide = lax.broadcasted_iota(jnp.int32, (TOK, 128), 1) < HEAD_DIM
        factor = HEAD_DIM**-0.5
        g_query, g_key, g_value = [], [], []
        for pair in range(HEADS // 2):
            at = 128 * pair
            query = qkv[:, at : at + 128]
            key = qkv[:, D + at : D + at + 128]
            value = qkv[:, 2 * D + at : 2 * D + at + 128]
            grad = scaled[:, at : at + 128]
            weighed = product[:, at : at + 128]
            parts = []
            for half in range(2):
                mask = low if half == 0 else ~low
                chosen = jnp.where(mask, grad, jnp.zeros_like(grad))
                delta = jnp.sum(
                    jnp.where(low_wide if half == 0 else ~low_wide, weighed, 0.0),
                    axis=-1,
                    keepdims=True,
                )
                expo = expo_in[0, 2 * pair + half]
                g_probs = dot_nt(chosen, value)
                g_scores = (expo.astype(F32) * (g_probs - delta)).astype(BF)
                parts.append(
                    (dot(g_scores, key), dot_tn(g_scores, query), dot_tn(expo, grad))
                )
            g_query.append((jnp.where(low_wide, parts[0][0], parts[1][0]) * factor).astype(BF))
            g_key.append((jnp.where(low_wide, parts[0][1], parts[1][1]) * factor).astype(BF))
            g_value.append(jnp.where(low_wide, parts[0][2], parts[1][2]).astype(BF))
        g_qkv = jnp.concatenate(g_query + g_key + g_value, axis=1)
        acc_qkv[...] += dot_tn(hidden, g_qkv)
        acc_bias[0:1, :] += jnp.sum(g_qkv.astype(F32), axis=0, keepdims=True)
        d_hidden = dot_nt(g_qkv, weights[:, :QKV_W])
        grad_mod[pl.ds(step, 1), :D] = jnp.sum(d_hidden, axis=0, keepdims=True)
        grad_mod[pl.ds(step, 1), D:] = jnp.sum(d_hidden * normed, axis=0, keepdims=True)
        out[0] = (
            grad_mid_in[0] + norm_back(d_hidden * (1.0 + row[:, D : 2 * D]), normed, inverse)
        ).astype(BF)

    @pl.when(step == CAP - 1)
    def _():
        cond = conditions[...].astype(F32)
        sig = 1.0 / (1.0 + jnp.exp(-cond))
        cond_low = (cond * sig).astype(BF)
        g_mod = grad_mod[...].astype(BF)
        g_mod_two = grad_mod_two[...].astype(BF)
        g_cond = dot_nt(g_mod, weights[:, QKV_W : QKV_W + MOD_ONE])
        g_cond += dot_nt(g_mod_two, weights_two[:, AT_MOD : AT_MOD + MOD_TWO])
        grad_cond[...] = (g_cond * (sig * (1.0 + cond * (1.0 - sig)))).astype(BF)
        mod_grad = dot_tn(cond_low.astype(F32), g_mod.astype(F32)).astype(BF)
        sums = jnp.sum(g_mod.astype(F32), axis=0, keepdims=True)
        rows = [acc_bias[0:1, 128 * i : 128 * i + 128] for i in range(9)]
        rows += [sums[:, 128 * i : 128 * i + 128] for i in range(6)]
        rows += [jnp.zeros((33, 128), F32)]
        bias_block = jnp.concatenate(rows, axis=0).astype(BF)
        z_high, core, column = info[2], info[3], info[1]
        for owner in range(8):
            zh, xx = owner // 4, owner % 4
            spot = pl.multiple_of(lax.rem(xx - column + 4, 4) * 48, 16)
            is_mine = (z_high ^ core) == zh
            lo = 48 * owner

            def put(ref, spot=spot, lo=lo):
                ref[pl.ds(spot, 48), :QKV_W] = acc_qkv[lo : lo + 48, :].astype(BF)
                ref[pl.ds(spot, 48), QKV_W : QKV_W + MOD_ONE] = mod_grad[lo : lo + 48, :]
                ref[pl.ds(spot, 48), BIAS_ONE : BIAS_ONE + 128] = bias_block

            pl.when(is_mine)(functools.partial(put, keep))
            pl.when(jnp.logical_not(is_mine))(functools.partial(put, send))


def slot_spec(*shape):
    zeros = (0,) * len(shape)
    return pl.BlockSpec((1, *shape), lambda j, info: (jnp.minimum(j, jnp.maximum(info[0] - 1, 0)), *zeros))


def slot_out(*shape):
    zeros = (0,) * len(shape)
    return pl.BlockSpec((1, *shape), lambda j, info: (j, *zeros))


def whole(*shape):
    zeros = (0,) * len(shape)
    return pl.BlockSpec(shape, lambda j, info: zeros)


def params():
    return pltpu.CompilerParams(
        dimension_semantics=("arbitrary",), vmem_limit_bytes=VMEM_BYTES
    )


def run_forward(info, latents, conditions, pieces):
    return pl.pallas_call(
        forward_kernel,
        grid_spec=pltpu.PrefetchScalarGridSpec(
            num_scalar_prefetch=1,
            grid=(CAP,),
            in_specs=[slot_spec(TOK, D), whole(CAP, D)] + [whole(48, LANES_ONE)] * 8,
            out_specs=[
                whole(D, LANES_ONE),
                whole(48, 128),
                whole(CAP, MOD_ONE),
                slot_out(TOK, QKV_W),
                slot_out(HEADS, TOK, TOK),
                slot_out(TOK, D),
                slot_out(TOK, D),
                slot_out(TOK, D),
            ],
        ),
        out_shape=[
            jax.ShapeDtypeStruct((D, LANES_ONE), BF),
            jax.ShapeDtypeStruct((48, 128), F32),
            jax.ShapeDtypeStruct((CAP, MOD_ONE), F32),
            jax.ShapeDtypeStruct((CAP, TOK, QKV_W), BF),
            jax.ShapeDtypeStruct((CAP, HEADS, TOK, TOK), BF),
            jax.ShapeDtypeStruct((CAP, TOK, D), BF),
            jax.ShapeDtypeStruct((CAP, TOK, D), F32),
            jax.ShapeDtypeStruct((CAP, TOK, D), BF),
        ],
        compiler_params=params(),
        name="attention_forward",
        cost_estimate=pl.CostEstimate(
            flops=3_000_000_000, bytes_accessed=20_000_000, transcendentals=3_000_000
        ),
    )(info, latents, conditions, *pieces)


def run_middle(info, latents, conditions, mixed, grad_out, bias, pieces):
    return pl.pallas_call(
        middle_kernel,
        grid_spec=pltpu.PrefetchScalarGridSpec(
            num_scalar_prefetch=1,
            grid=(CAP,),
            in_specs=[
                slot_spec(TOK, D),
                whole(CAP, D),
                slot_spec(TOK, D),
                slot_spec(TOK, D),
                whole(48, 128),
            ]
            + [whole(48, LANES_TWO)] * 8,
            out_specs=[
                whole(D, LANES_TWO),
                slot_out(TOK, D),
                slot_out(TOK, D),
                slot_out(TOK, D),
                whole(CAP, MOD_TWO),
                whole(192, LANES_TWO),
                whole(192, LANES_TWO),
            ],
            scratch_shapes=[
                pltpu.VMEM((CAP, MOD_TWO), F32),
                pltpu.VMEM((D, FF), F32),
                pltpu.VMEM((FF, D), F32),
                pltpu.VMEM((D, D), F32),
                pltpu.VMEM((8, FF), F32),
            ],
        ),
        out_shape=[
            jax.ShapeDtypeStruct((D, LANES_TWO), BF),
            jax.ShapeDtypeStruct((CAP, TOK, D), BF),
            jax.ShapeDtypeStruct((CAP, TOK, D), F32),
            jax.ShapeDtypeStruct((CAP, TOK, D), BF),
            jax.ShapeDtypeStruct((CAP, MOD_TWO), F32),
            jax.ShapeDtypeStruct((192, LANES_TWO), BF),
            jax.ShapeDtypeStruct((192, LANES_TWO), BF),
        ],
        compiler_params=params(),
        name="feed_forward_both_ways",
        cost_estimate=pl.CostEstimate(
            flops=16_000_000_000, bytes_accessed=30_000_000, transcendentals=3_000_000
        ),
    )(info, latents, conditions, mixed, grad_out, bias, *pieces)


def run_backward(
    info, latents, conditions, qkv, expo, mixed, rinv, hidden, grad_mid, grad_mixed, mod,
    weights, weights_two, grad_mod_two,
):
    return pl.pallas_call(
        backward_kernel,
        grid_spec=pltpu.PrefetchScalarGridSpec(
            num_scalar_prefetch=1,
            grid=(CAP,),
            in_specs=[
                slot_spec(TOK, D),
                whole(CAP, D),
                slot_spec(TOK, QKV_W),
                slot_spec(HEADS, TOK, TOK),
                slot_spec(TOK, D),
                slot_spec(TOK, D),
                slot_spec(TOK, D),
                slot_spec(TOK, D),
                slot_spec(TOK, D),
                whole(CAP, MOD_ONE),
                whole(D, LANES_ONE),
                whole(D, LANES_TWO),
                whole(CAP, MOD_TWO),
            ],
            out_specs=[
                slot_out(TOK, D),
                whole(CAP, D),
                whole(192, LANES_ONE),
                whole(192, LANES_ONE),
            ],
            scratch_shapes=[
                pltpu.VMEM((D, QKV_W), F32),
                pltpu.VMEM((8, QKV_W), F32),
                pltpu.VMEM((CAP, MOD_ONE), F32),
            ],
        ),
        out_shape=[
            jax.ShapeDtypeStruct((CAP, TOK, D), BF),
            jax.ShapeDtypeStruct((CAP, D), BF),
            jax.ShapeDtypeStruct((192, LANES_ONE), BF),
            jax.ShapeDtypeStruct((192, LANES_ONE), BF),
        ],
        compiler_params=params(),
        name="attention_backward",
        cost_estimate=pl.CostEstimate(
            flops=9_000_000_000, bytes_accessed=30_000_000, transcendentals=1_000
        ),
    )(
        info, latents, conditions, qkv, expo, mixed, rinv, hidden, grad_mid, grad_mixed, mod,
        weights, weights_two, grad_mod_two,
    )


def place(index):
    shard, rep = divmod(index, 16)
    return shard // 4, shard % 4, rep // 4, (rep // 2) % 2, rep % 2


def index_of(z_high, x, y, z_low, core):
    return (z_high * 4 + x) * 16 + y * 4 + z_low * 2 + core


def routes(target_of):
    return [(i, target_of(*place(i))) for i in range(TWIN)]


def fetch(k):
    def source(zh, x, y, zl, c):
        if c == 0:
            return index_of(zh, (x + k) % 4, y, zl, c)
        return index_of(1 - zh, (x + k) % 4, y, 1 - zl, c)

    return [(source(*place(i)), i) for i in range(TWIN)]


CORE_SWAP = routes(lambda zh, x, y, zl, c: index_of(zh, x, y, zl, 1 - c))
ZLOW_SWAP = routes(lambda zh, x, y, zl, c: index_of(zh, x, y, 1 - zl, c))
BOTH = ("shard", "rep")


def move(value, pairs):
    return lax.ppermute(value, BOTH, pairs)


def y_route(k):
    return routes(lambda zh, x, y, zl, c: index_of(zh, x, (y + k) % 4, zl, c))


def gather(block):
    mine = [move(block, fetch(k)) for k in range(4)]
    other = [move(piece, CORE_SWAP) for piece in mine]
    return mine + other


def add(values, dtype=BF):
    return sum(v.astype(F32) for v in values).astype(dtype)


def reduce(keep, send):
    held = add([keep, move(send, CORE_SWAP)])
    arrived = []
    for k in range(4):
        back = [(target, source) for source, target in fetch(k)]
        arrived.append(move(held[48 * k : 48 * k + 48], back))
    total = add(arrived)
    total = add([total, move(total, CORE_SWAP)])
    total = add([total, move(total, ZLOW_SWAP)])
    return add([total] + [move(total, y_route(k)) for k in (1, 2, 3)], F32)


def pack_bias(shard, mod_bias, qv_bias, proj_bias, up_bias, down_bias):
    flat = jnp.zeros((48 * 128,), BF)
    qv_at = shard * 96 + jnp.where(shard >= 4, D, 0)
    flat = lax.dynamic_update_slice(flat, qv_bias, (qv_at,))
    flat = lax.dynamic_update_slice(flat, mod_bias, (ROW_MOD * 128 + shard * 288,))
    flat = lax.dynamic_update_slice(flat, proj_bias, (ROW_PROJ * 128 + shard * 48,))
    flat = lax.dynamic_update_slice(flat, up_bias, (ROW_UP * 128 + shard * 192,))
    flat = lax.dynamic_update_slice(flat, down_bias, (ROW_DOWN * 128 + shard * 48,))
    return flat.reshape(48, 128)


def on_device(
    latents, conditions, counts, mod_weight, mod_bias, qkv_weight, qv_bias, proj_weight,
    proj_bias, up_weight, up_bias, down_weight, down_bias, grad_out,
):
    shard = lax.axis_index("shard")
    rep = lax.axis_index("rep")
    info = jnp.stack([counts[0], shard % 4, shard // 4, rep % 2]).astype(jnp.int32)
    biases = pack_bias(shard, mod_bias, qv_bias, proj_bias, up_bias, down_bias)
    block_one = jnp.concatenate([qkv_weight, mod_weight[:, :MOD_ONE], biases], axis=1)
    block_two = jnp.concatenate(
        [up_weight, mod_weight[:, MOD_ONE:], proj_weight]
        + [down_weight[48 * q : 48 * q + 48] for q in range(4)]
        + [jnp.zeros((48, 128), BF)],
        axis=1,
    )
    pieces_one = gather(block_one)
    pieces_two = gather(block_two)
    weights, bias, mod, qkv, expo, mixed, rinv, hidden = run_forward(
        info, latents, conditions, pieces_one
    )
    weights_two, out, grad_mid, grad_mixed, grad_mod_two, keep_two, send_two = run_middle(
        info, latents, conditions, mixed, grad_out, bias, pieces_two
    )
    grad_latents, grad_cond, keep_one, send_one = run_backward(
        info, latents, conditions, qkv, expo, mixed, rinv, hidden, grad_mid, grad_mixed, mod,
        weights, weights_two, grad_mod_two,
    )
    two = reduce(keep_two, send_two)
    one = reduce(keep_one, send_one)
    grad_bias = (
        one[:, BIAS_ONE : BIAS_ONE + 128] + two[:, BIAS_TWO : BIAS_TWO + 128]
    ).reshape(-1)
    qv_at = shard * 96 + jnp.where(shard >= 4, D, 0)

    def part(first, size):
        return lax.dynamic_slice(grad_bias, (first,), (size,))

    return (
        out,
        grad_latents,
        grad_cond,
        jnp.concatenate([one[:, QKV_W : QKV_W + MOD_ONE], two[:, AT_MOD : AT_MOD + MOD_TWO]], 1),
        part(ROW_MOD * 128 + shard * 288, 288),
        one[:, :QKV_W],
        part(qv_at, 96),
        two[:, AT_PROJ : AT_PROJ + D],
        part(ROW_PROJ * 128 + shard * 48, 48),
        two[:, :FF],
        part(ROW_UP * 128 + shard * 192, 192),
        jnp.concatenate([two[:, AT_DOWN + D * q : AT_DOWN + D * q + D] for q in range(4)], 0),
        part(ROW_DOWN * 128 + shard * 48, 48),
    )


def solution(mesh):
    slots = P(("shard", "rep"), None, None)
    rows = P(("shard", "rep"), None)
    matrix, vector = P("shard", None), P("shard")
    in_specs = (slots, rows, P(("shard", "rep"))) + (matrix, vector) * 5 + (slots,)
    out_specs = (slots, slots, rows) + (matrix, vector) * 5
    return jax.shard_map(
        on_device, mesh=mesh, in_specs=in_specs, out_specs=out_specs, check_vma=False
    )
```

```python
import functools

import jax
import jax.numpy as jnp
from jax import lax
from jax.experimental import pallas as pl
from jax.experimental.pallas import tpu as pltpu
from jax.sharding import PartitionSpec as P

D = 384
HEADS = 6
HEAD_DIM = 64
FF = 1536
TOK = 256
CAP = 8
STEP = 1
TWIN = 128
BF = jnp.bfloat16
F32 = jnp.float32
VMEM_BYTES = 56 * 1024 * 1024

LANES_ONE = 2048
QKV_W = 3 * D
MOD_ONE = 2 * D
BIAS_ONE = QKV_W + MOD_ONE
LANES_TWO = 5120
MOD_TWO = 4 * D
AT_MOD = FF
AT_PROJ = AT_MOD + MOD_TWO
AT_DOWN = AT_PROJ + D
BIAS_TWO = AT_DOWN + FF
ROW_QKV, ROW_MOD, ROW_PROJ, ROW_UP, ROW_DOWN = 0, 9, 27, 30, 42


def dot(left, right):
    return jnp.dot(left, right, preferred_element_type=F32)


def dot_tn(left, right):
    return lax.dot_general(left, right, (((0,), (0,)), ((), ())), preferred_element_type=F32)


def dot_nt(left, right):
    return lax.dot_general(left, right, (((1,), (1,)), ((), ())), preferred_element_type=F32)


def normalize(value):
    center = jnp.mean(value, axis=-1, keepdims=True)
    centered = value - center
    spread = jnp.mean(centered * centered, axis=-1, keepdims=True)
    inverse = lax.rsqrt(spread + 1e-06)
    return centered * inverse, inverse


def norm_back(grad, normed, inverse):
    first = jnp.mean(grad, axis=-1, keepdims=True)
    second = jnp.mean(grad * normed, axis=-1, keepdims=True)
    return inverse * (grad - first - normed * second)


def spread(rows, size):
    width = 8 * size
    lane = lax.broadcasted_iota(jnp.int32, (8, width), 1)
    total = jnp.zeros((8, width), F32)
    for owner, row in enumerate(rows):
        padded = jnp.concatenate([row, jnp.zeros((1, width - row.shape[1]), F32)], axis=1)
        padded = jnp.where(lane < size, jnp.broadcast_to(padded, (8, width)), 0.0)
        total += pltpu.roll(padded, owner * size, 1) if owner else padded
    return total[0:1]


def all_biases(raw):
    def rows(first, count):
        return [
            jnp.concatenate([block[first + i : first + i + 1] for i in range(count)], axis=1)
            for block in raw
        ]

    qv = spread(rows(0, 1), 96)
    full = [qv[:, :D], jnp.zeros((1, D), F32), qv[:, D:]]
    full += [spread(rows(1, 3), 288), spread(rows(4, 1), 48)]
    full += [spread(rows(5, 2), 192), spread(rows(7, 1), 48)]
    full = jnp.concatenate(full, axis=1)
    cut = [full[:, 128 * i : 128 * i + 128] for i in range(45)]
    return jnp.concatenate(cut + [jnp.zeros((3, 128), F32)], axis=0)


def bias_row(bias, first, count):
    return jnp.concatenate([bias[first + i : first + i + 1, :] for i in range(count)], axis=1)


def silu(cond):
    return cond * (1.0 / (1.0 + jnp.exp(-cond)))


def assemble(info, pieces, full):
    column, z_high, core = info[1], info[2], info[3]
    for k in range(4):
        spot = lax.rem(column + k, 4) * 48
        mine = (z_high ^ core) * 192 + spot
        other = (1 - (z_high ^ core)) * 192 + spot
        full[pl.ds(pl.multiple_of(mine, 16), 48), :] = pieces[k][...]
        full[pl.ds(pl.multiple_of(other, 16), 48), :] = pieces[4 + k][...]


def forward_kernel(
    info, latents, conditions, p0, p1, p2, p3, p4, p5, p6, p7,
    weights, bias_out, mod_out, qkv_out, expo_out, mixed_out, rinv_out, hidden_out,
):
    step = pl.program_id(0)

    @pl.when(step == 0)
    def _():
        assemble(info, (p0, p1, p2, p3, p4, p5, p6, p7), weights)
        total = all_biases(
            [
                weights[48 * k : 48 * k + 16, BIAS_ONE : BIAS_ONE + 128].astype(F32)[:8]
                for k in range(8)
            ]
        )
        bias_out[...] = total
        cond_low = silu(conditions[...].astype(F32)).astype(BF)
        mod_out[...] = dot(cond_low, weights[:, QKV_W : QKV_W + MOD_ONE]) + bias_row(
            total, ROW_MOD, 6
        )

    @pl.when(step < info[0])
    def _():
        mod = mod_out[pl.ds(step, 1), :]
        normed, _ = normalize(latents[0].astype(F32))
        hidden = (normed * (1.0 + mod[:, D : 2 * D]) + mod[:, :D]).astype(BF)
        hidden_out[step] = hidden
        full_bias = bias_row(bias_out[0:16, :], ROW_QKV, 9)
        qkv = (dot(hidden, weights[:, :QKV_W]) + full_bias).astype(BF)
        qkv_out[step] = qkv
        low = lax.broadcasted_iota(jnp.int32, (TOK, 128), 1) < HEAD_DIM
        ones = jnp.ones((TOK, 128), BF)
        for pair in range(HEADS // 2):
            at = 128 * pair
            query = qkv[:, at : at + 128] * jnp.asarray(HEAD_DIM**-0.5, BF)
            key = qkv[:, D + at : D + at + 128]
            value = jnp.concatenate([qkv[:, 2 * D + at : 2 * D + at + 128], ones], axis=1)
            parts = []
            for half in range(2):
                chosen = jnp.where(low if half == 0 else ~low, query, jnp.zeros_like(query))
                scores = dot_nt(chosen, key)
                expo = jnp.exp(scores - jnp.max(scores, axis=-1, keepdims=True)).astype(BF)
                expo_out[step, 2 * pair + half] = expo
                parts.append(dot(expo, value))
            total = jnp.where(low, parts[0][:, 128:], parts[1][:, 128:])
            inverse = 1.0 / total
            rinv_out[step, :, at : at + 128] = inverse
            mixed_out[step, :, at : at + 128] = (
                jnp.where(low, parts[0][:, :128], parts[1][:, :128]) * inverse
            ).astype(BF)


def middle_kernel(
    info, latents, conditions, mixed_in, grad_out, bias_in, p0, p1, p2, p3, p4, p5, p6, p7,
    weights, out, grad_mid_out, grad_mixed_out, grad_mod, keep, send,
    mod, acc_up, acc_down, acc_proj, acc_bias,
):
    step = pl.program_id(0)

    @pl.when(step == 0)
    def _():
        assemble(info, (p0, p1, p2, p3, p4, p5, p6, p7), weights)
        cond_low = silu(conditions[...].astype(F32)).astype(BF)
        mod[...] = dot(cond_low, weights[:, AT_MOD : AT_MOD + MOD_TWO]) + bias_row(
            bias_in[...], ROW_MOD + 6, 12
        )
        acc_up[...] = jnp.zeros_like(acc_up)
        acc_down[...] = jnp.zeros_like(acc_down)
        acc_proj[...] = jnp.zeros_like(acc_proj)
        acc_bias[...] = jnp.zeros_like(acc_bias)
        grad_mod[...] = jnp.zeros_like(grad_mod)

    @pl.when(step >= info[0])
    def _():
        out[0] = jnp.zeros((TOK, D), BF)

    @pl.when(step < info[0])
    def _():
        row = mod[pl.ds(step, 1), :]
        gate_one, shift_two = row[:, :D], row[:, D : 2 * D]
        scale_two, gate_two = row[:, 2 * D : 3 * D], row[:, 3 * D :]
        bias = bias_in[...]
        mixed = mixed_in[step]
        w_proj = weights[:, AT_PROJ : AT_PROJ + D]
        branch_one = dot(mixed, w_proj) + bias_row(bias, ROW_PROJ, 3)
        middle = latents[0].astype(F32) + gate_one * branch_one
        normed, inverse = normalize(middle)
        hidden = (normed * (1.0 + scale_two) + shift_two).astype(BF)
        cot = grad_out[0].astype(F32)
        g_two = (cot * gate_two).astype(BF)
        up_bias = bias_row(bias, ROW_UP, 12)
        branch_two = bias_row(bias, ROW_DOWN, 3)
        d_hidden = jnp.zeros((TOK, D), F32)
        root = 0.7978845608028654
        cube = root * 0.044715
        for chunk in range(4):
            at = D * chunk
            w_up = weights[:, at : at + D]
            w_down = jnp.concatenate(
                [
                    weights[48 * s : 48 * s + 48, AT_DOWN + D * q : AT_DOWN + D * q + D]
                    for s in (2 * chunk, 2 * chunk + 1)
                    for q in range(4)
                ],
                axis=0,
            )
            upward = dot(hidden, w_up) + up_bias[:, at : at + D]
            square = upward * upward
            bend = jnp.tanh(upward * (root + cube * square))
            half = 0.5 + 0.5 * bend
            act = upward * half
            slope = half + act * (1.0 - bend) * (root + (3.0 * cube) * square)
            act_low = act.astype(BF)
            branch_two = branch_two + dot(act_low, w_down)
            acc_down[at : at + D, :] += dot_tn(act_low, g_two)
            g_up = (slope * dot_nt(g_two, w_down)).astype(BF)
            acc_up[:, at : at + D] += dot_tn(hidden, g_up)
            acc_bias[0:1, at : at + D] += jnp.sum(g_up.astype(F32), axis=0, keepdims=True)
            d_hidden = d_hidden + dot_nt(g_up, w_up)
        out[0] = (middle + gate_two * branch_two).astype(BF)
        acc_bias[1:2, :D] += jnp.sum(g_two.astype(F32), axis=0, keepdims=True)
        grad_mod[pl.ds(step, 1), 3 * D :] = jnp.sum(cot * branch_two, axis=0, keepdims=True)
        grad_mod[pl.ds(step, 1), D : 2 * D] = jnp.sum(d_hidden, axis=0, keepdims=True)
        grad_mod[pl.ds(step, 1), 2 * D : 3 * D] = jnp.sum(
            d_hidden * normed, axis=0, keepdims=True
        )
        grad_mid = cot + norm_back(d_hidden * (1.0 + scale_two), normed, inverse)
        grad_mid_out[step] = grad_mid
        grad_mod[pl.ds(step, 1), :D] = jnp.sum(grad_mid * branch_one, axis=0, keepdims=True)
        g_one = (grad_mid * gate_one).astype(BF)
        acc_bias[2:3, :D] += jnp.sum(g_one.astype(F32), axis=0, keepdims=True)
        acc_proj[...] += dot_tn(mixed, g_one)
        grad_mixed_out[step] = dot_nt(g_one, w_proj).astype(BF)

    @pl.when(step == CAP - 1)
    def _():
        cond_low = silu(conditions[...].astype(F32)).astype(BF)
        g_mod = grad_mod[...].astype(BF)
        mod_grad = dot_tn(cond_low.astype(F32), g_mod.astype(F32)).astype(BF)
        z_high, core, column = info[2], info[3], info[1]
        sums = jnp.sum(g_mod.astype(F32), axis=0, keepdims=True)
        rows = [jnp.zeros((ROW_MOD + 6, 128), F32)]
        rows += [sums[:, 128 * i : 128 * i + 128] for i in range(12)]
        rows += [acc_bias[2:3, 128 * i : 128 * i + 128] for i in range(3)]
        rows += [acc_bias[0:1, 128 * i : 128 * i + 128] for i in range(12)]
        rows += [acc_bias[1:2, 128 * i : 128 * i + 128] for i in range(3)]
        rows += [jnp.zeros((3, 128), F32)]
        bias_block = jnp.concatenate(rows, axis=0).astype(BF)
        for owner in range(8):
            zh, xx = owner // 4, owner % 4
            spot = lax.rem(xx - column + 4, 4) * 48
            spot = pl.multiple_of(spot, 16)
            is_mine = (z_high ^ core) == zh
            lo = 48 * owner

            def put(ref, spot=spot, lo=lo, owner=owner):
                ref[pl.ds(spot, 48), :FF] = acc_up[lo : lo + 48, :].astype(BF)
                ref[pl.ds(spot, 48), AT_MOD : AT_MOD + MOD_TWO] = mod_grad[lo : lo + 48, :]
                ref[pl.ds(spot, 48), AT_PROJ : AT_PROJ + D] = acc_proj[lo : lo + 48, :].astype(BF)
                for q in range(4):
                    at = 192 * owner + 48 * q
                    ref[pl.ds(spot, 48), AT_DOWN + D * q : AT_DOWN + D * q + D] = acc_down[
                        at : at + 48, :
                    ].astype(BF)
                ref[pl.ds(spot, 48), BIAS_TWO : BIAS_TWO + 128] = bias_block

            pl.when(is_mine)(functools.partial(put, keep))
            pl.when(jnp.logical_not(is_mine))(functools.partial(put, send))


def backward_kernel(
    first, last,
    info, latents, conditions, qkv_in, expo_in, mixed_in, rinv_in, hidden_in, grad_mid_in,
    grad_mixed_in, mod_in, weights, *refs,
):
    if last:
        weights_two, grad_mod_two, acc_in, bias_in, grad_mod_in, _, out, grad_cond, keep, send = refs[:10]
        acc_qkv, acc_bias, grad_mod = refs[10:]
    else:
        out, acc_qkv, acc_bias, grad_mod = refs
    step = pl.program_id(0)
    slot = step + first

    @pl.when(step == 0)
    def _():
        if last:
            acc_qkv[...] = acc_in[...]
            acc_bias[...] = bias_in[...]
            grad_mod[...] = grad_mod_in[...]
        else:
            acc_qkv[...] = jnp.zeros_like(acc_qkv)
            acc_bias[...] = jnp.zeros_like(acc_bias)
            grad_mod[...] = jnp.zeros_like(grad_mod)

    @pl.when(slot >= info[0])
    def _():
        out[0] = jnp.zeros((TOK, D), BF)

    @pl.when(slot < info[0])
    def _():
        row = mod_in[pl.ds(slot, 1), :]
        normed, inverse = normalize(latents[0].astype(F32))
        qkv = qkv_in[slot]
        hidden = hidden_in[slot]
        scaled = (grad_mixed_in[slot].astype(F32) * rinv_in[slot]).astype(BF)
        product = scaled.astype(F32) * mixed_in[slot].astype(F32)
        low = lax.broadcasted_iota(jnp.int32, (TOK, 128), 1) < HEAD_DIM
        low_wide = lax.broadcasted_iota(jnp.int32, (TOK, 128), 1) < HEAD_DIM
        factor = HEAD_DIM**-0.5
        g_query, g_key, g_value = [], [], []
        for pair in range(HEADS // 2):
            at = 128 * pair
            query = qkv[:, at : at + 128]
            key = qkv[:, D + at : D + at + 128]
            value = qkv[:, 2 * D + at : 2 * D + at + 128]
            grad = scaled[:, at : at + 128]
            weighed = product[:, at : at + 128]
            parts = []
            for half in range(2):
                mask = low if half == 0 else ~low
                chosen = jnp.where(mask, grad, jnp.zeros_like(grad))
                delta = jnp.sum(
                    jnp.where(low_wide if half == 0 else ~low_wide, weighed, 0.0),
                    axis=-1,
                    keepdims=True,
                )
                expo = expo_in[slot, 2 * pair + half]
                g_probs = dot_nt(chosen, value)
                g_scores = (expo.astype(F32) * (g_probs - delta)).astype(BF)
                parts.append(
                    (dot(g_scores, key), dot_tn(g_scores, query), dot_tn(expo, grad))
                )
            g_query.append((jnp.where(low_wide, parts[0][0], parts[1][0]) * factor).astype(BF))
            g_key.append((jnp.where(low_wide, parts[0][1], parts[1][1]) * factor).astype(BF))
            g_value.append(jnp.where(low_wide, parts[0][2], parts[1][2]).astype(BF))
        g_qkv = jnp.concatenate(g_query + g_key + g_value, axis=1)
        acc_qkv[...] += dot_tn(hidden, g_qkv)
        acc_bias[0:1, :] += jnp.sum(g_qkv.astype(F32), axis=0, keepdims=True)
        d_hidden = dot_nt(g_qkv, weights[:, :QKV_W])
        grad_mod[pl.ds(slot, 1), :D] = jnp.sum(d_hidden, axis=0, keepdims=True)
        grad_mod[pl.ds(slot, 1), D:] = jnp.sum(d_hidden * normed, axis=0, keepdims=True)
        out[0] = (
            grad_mid_in[slot] + norm_back(d_hidden * (1.0 + row[:, D : 2 * D]), normed, inverse)
        ).astype(BF)

    if not last:
        return

    @pl.when(step == CAP - 1 - first)
    def _():
        cond = conditions[...].astype(F32)
        sig = 1.0 / (1.0 + jnp.exp(-cond))
        cond_low = (cond * sig).astype(BF)
        g_mod = grad_mod[...].astype(BF)
        g_mod_two = grad_mod_two[...].astype(BF)
        g_cond = dot_nt(g_mod, weights[:, QKV_W : QKV_W + MOD_ONE])
        g_cond += dot_nt(g_mod_two, weights_two[:, AT_MOD : AT_MOD + MOD_TWO])
        grad_cond[...] = (g_cond * (sig * (1.0 + cond * (1.0 - sig)))).astype(BF)
        mod_grad = dot_tn(cond_low.astype(F32), g_mod.astype(F32)).astype(BF)
        sums = jnp.sum(g_mod.astype(F32), axis=0, keepdims=True)
        rows = [acc_bias[0:1, 128 * i : 128 * i + 128] for i in range(9)]
        rows += [sums[:, 128 * i : 128 * i + 128] for i in range(6)]
        rows += [jnp.zeros((33, 128), F32)]
        bias_block = jnp.concatenate(rows, axis=0).astype(BF)
        z_high, core, column = info[2], info[3], info[1]
        for owner in range(8):
            zh, xx = owner // 4, owner % 4
            spot = pl.multiple_of(lax.rem(xx - column + 4, 4) * 48, 16)
            is_mine = (z_high ^ core) == zh
            lo = 48 * owner

            def put(ref, spot=spot, lo=lo):
                ref[pl.ds(spot, 48), :QKV_W] = acc_qkv[lo : lo + 48, :].astype(BF)
                ref[pl.ds(spot, 48), QKV_W : QKV_W + MOD_ONE] = mod_grad[lo : lo + 48, :]
                ref[pl.ds(spot, 48), BIAS_ONE : BIAS_ONE + 128] = bias_block

            pl.when(is_mine)(functools.partial(put, keep))
            pl.when(jnp.logical_not(is_mine))(functools.partial(put, send))


def slot_spec(*shape):
    zeros = (0,) * len(shape)
    return pl.BlockSpec((1, *shape), lambda j, info: (jnp.minimum(j, jnp.maximum(info[0] - 1, 0)), *zeros))


def slot_out(*shape):
    zeros = (0,) * len(shape)
    return pl.BlockSpec((1, *shape), lambda j, info: (j, *zeros))


def held():
    return pl.BlockSpec(memory_space=pltpu.VMEM)


def whole(*shape):
    zeros = (0,) * len(shape)
    return pl.BlockSpec(shape, lambda j, info: zeros)


def params():
    return pltpu.CompilerParams(
        dimension_semantics=("arbitrary",), vmem_limit_bytes=VMEM_BYTES
    )


def run_forward(info, latents, conditions, pieces):
    return pl.pallas_call(
        forward_kernel,
        grid_spec=pltpu.PrefetchScalarGridSpec(
            num_scalar_prefetch=1,
            grid=(CAP,),
            in_specs=[slot_spec(TOK, D), whole(CAP, D)] + [held()] * 8,
            out_specs=[held()] * 8,
        ),
        out_shape=[
            jax.ShapeDtypeStruct((D, LANES_ONE), BF),
            jax.ShapeDtypeStruct((48, 128), F32),
            jax.ShapeDtypeStruct((CAP, MOD_ONE), F32),
            jax.ShapeDtypeStruct((CAP, TOK, QKV_W), BF),
            jax.ShapeDtypeStruct((CAP, HEADS, TOK, TOK), BF),
            jax.ShapeDtypeStruct((CAP, TOK, D), BF),
            jax.ShapeDtypeStruct((CAP, TOK, D), F32),
            jax.ShapeDtypeStruct((CAP, TOK, D), BF),
        ],
        compiler_params=params(),
        name="attention_forward",
        cost_estimate=pl.CostEstimate(
            flops=3_000_000_000, bytes_accessed=20_000_000, transcendentals=3_000_000
        ),
    )(info, latents, conditions, *pieces)


def run_middle(info, latents, conditions, mixed, grad_out, bias, pieces):
    return pl.pallas_call(
        middle_kernel,
        grid_spec=pltpu.PrefetchScalarGridSpec(
            num_scalar_prefetch=1,
            grid=(CAP,),
            in_specs=[
                slot_spec(TOK, D),
                whole(CAP, D),
                held(),
                slot_spec(TOK, D),
                held(),
            ]
            + [held()] * 8,
            out_specs=[held(), slot_out(TOK, D)] + [held()] * 5,
            scratch_shapes=[
                pltpu.VMEM((CAP, MOD_TWO), F32),
                pltpu.VMEM((D, FF), F32),
                pltpu.VMEM((FF, D), F32),
                pltpu.VMEM((D, D), F32),
                pltpu.VMEM((8, FF), F32),
            ],
        ),
        out_shape=[
            jax.ShapeDtypeStruct((D, LANES_TWO), BF),
            jax.ShapeDtypeStruct((CAP, TOK, D), BF),
            jax.ShapeDtypeStruct((CAP, TOK, D), F32),
            jax.ShapeDtypeStruct((CAP, TOK, D), BF),
            jax.ShapeDtypeStruct((CAP, MOD_TWO), F32),
            jax.ShapeDtypeStruct((192, LANES_TWO), BF),
            jax.ShapeDtypeStruct((192, LANES_TWO), BF),
        ],
        compiler_params=params(),
        name="feed_forward_both_ways",
        cost_estimate=pl.CostEstimate(
            flops=16_000_000_000, bytes_accessed=30_000_000, transcendentals=3_000_000
        ),
    )(info, latents, conditions, mixed, grad_out, bias, *pieces)


def run_backward(first, count, info, latents, shared, carried=None):
    last = carried is not None

    def slot_at(j, info):
        return (jnp.minimum(j + first, jnp.maximum(info[0] - 1, 0)), 0, 0)

    in_specs = [pl.BlockSpec((1, TOK, D), slot_at), whole(CAP, D)] + [held()] * 9
    out_specs = [pl.BlockSpec((1, TOK, D), lambda j, info: (j + first, 0, 0))]
    out_shape = [jax.ShapeDtypeStruct((CAP, TOK, D), BF)]
    state = [(D, QKV_W), (8, QKV_W), (CAP, MOD_ONE)]
    if last:
        in_specs += [held()] * 5 + [pl.BlockSpec(memory_space=pl.ANY)]
        out_specs += [whole(CAP, D), held(), held()]
        out_shape += [jax.ShapeDtypeStruct((CAP, D), BF)]
        out_shape += [jax.ShapeDtypeStruct((192, LANES_ONE), BF)] * 2
    else:
        out_specs += [held()] * 3
        out_shape += [jax.ShapeDtypeStruct(shape, F32) for shape in state]
    return pl.pallas_call(
        functools.partial(backward_kernel, first, last),
        grid_spec=pltpu.PrefetchScalarGridSpec(
            num_scalar_prefetch=1,
            grid=(count,),
            in_specs=in_specs,
            out_specs=out_specs,
            scratch_shapes=[pltpu.VMEM(shape, F32) for shape in state] if last else [],
        ),
        out_shape=out_shape,
        input_output_aliases={17: 0} if last else {},
        compiler_params=params(),
        name="attention_backward_rest" if last else "attention_backward_start",
        cost_estimate=pl.CostEstimate(
            flops=1_100_000_000 * count, bytes_accessed=4_000_000 * count, transcendentals=1_000
        ),
    )(info, latents, *shared, *(carried or ()))


def place(index):
    shard, rep = divmod(index, 16)
    return shard // 4, shard % 4, rep // 4, (rep // 2) % 2, rep % 2


def index_of(z_high, x, y, z_low, core):
    return (z_high * 4 + x) * 16 + y * 4 + z_low * 2 + core


def routes(target_of):
    return [(i, target_of(*place(i))) for i in range(TWIN)]


def fetch(k):
    def source(zh, x, y, zl, c):
        if c == 0:
            return index_of(zh, (x + k) % 4, y, zl, c)
        return index_of(1 - zh, (x + k) % 4, y, 1 - zl, c)

    return [(source(*place(i)), i) for i in range(TWIN)]


CORE_SWAP = routes(lambda zh, x, y, zl, c: index_of(zh, x, y, zl, 1 - c))
ZLOW_SWAP = routes(lambda zh, x, y, zl, c: index_of(zh, x, y, 1 - zl, c))
BOTH = ("shard", "rep")


def move(value, pairs):
    return lax.ppermute(value, BOTH, pairs)


def y_route(k):
    return routes(lambda zh, x, y, zl, c: index_of(zh, x, (y + k) % 4, zl, c))


def after(value, *earlier):
    return lax.optimization_barrier((value, *earlier))[0]


def fetch_all(block):
    return [move(block, fetch(k)) for k in range(4)]


def swap_all(pieces):
    return [move(piece, CORE_SWAP) for piece in pieces]


def add(values, dtype=BF):
    return sum(v.astype(F32) for v in values).astype(dtype)


def scatter(held_sum):
    arrived = []
    for k in range(4):
        back = [(target, source) for source, target in fetch(k)]
        arrived.append(move(held_sum[48 * k : 48 * k + 48], back))
    return arrived


def sum_replicas(arrived, core):
    lanes = arrived[0].shape[1] // 2
    total = add(arrived)
    mine = lax.dynamic_slice(total, (0, core * lanes), (48, lanes))
    other = lax.dynamic_slice(total, (0, (1 - core) * lanes), (48, lanes))
    total = add([mine, move(other, CORE_SWAP)])
    total = add([total, move(total, ZLOW_SWAP)])
    total = add([total] + [move(total, y_route(k)) for k in (1, 2, 3)])
    swapped = move(total, CORE_SWAP)
    halves = [jnp.where(core == 0, total, swapped), jnp.where(core == 0, swapped, total)]
    return jnp.concatenate(halves, axis=1).astype(F32)


def pack_bias(mod_bias, qv_bias, proj_bias, up_bias, down_bias):
    def whole_rows(value):
        return jnp.pad(value, (0, -value.shape[0] % 128))

    flat = jnp.concatenate(
        [whole_rows(v) for v in (qv_bias, mod_bias, proj_bias, up_bias, down_bias)]
    )
    return jnp.pad(flat.reshape(8, 128), ((0, 40), (0, 0)))


def on_device(
    latents, conditions, counts, mod_weight, mod_bias, qkv_weight, qv_bias, proj_weight,
    proj_bias, up_weight, up_bias, down_weight, down_bias, grad_out,
):
    shard = lax.axis_index("shard")
    rep = lax.axis_index("rep")
    info = jnp.stack([counts[0], shard % 4, shard // 4, rep % 2]).astype(jnp.int32)
    biases = pack_bias(mod_bias, qv_bias, proj_bias, up_bias, down_bias)
    block_one = jnp.concatenate([qkv_weight, mod_weight[:, :MOD_ONE], biases], axis=1)
    block_two = jnp.concatenate(
        [up_weight, mod_weight[:, MOD_ONE:], proj_weight]
        + [down_weight[48 * q : 48 * q + 48] for q in range(4)]
        + [jnp.zeros((48, 128), BF)],
        axis=1,
    )
    core = rep % 2
    mine_one = fetch_all(block_one)
    other_one = swap_all(mine_one)
    mine_two = fetch_all(after(block_two, *mine_one))
    weights, bias, mod, qkv, expo, mixed, rinv, hidden = run_forward(
        info, latents, conditions, mine_one + other_one
    )
    other_two = swap_all(mine_two)
    weights_two, out, grad_mid, grad_mixed, grad_mod_two, keep_two, send_two = run_middle(
        info, latents, conditions, mixed, grad_out, bias, mine_two + other_two
    )
    swapped_two = move(send_two, CORE_SWAP)
    shared = (
        conditions, qkv, expo, mixed, rinv, hidden, grad_mid, grad_mixed, mod, weights,
    )
    grad_latents, acc_qkv, acc_bias, grad_mod = run_backward(0, 2, info, latents, shared)
    held_two = add([keep_two, after(swapped_two, acc_bias)])
    arrived_two = scatter(held_two)
    grad_latents, grad_cond, keep_one, send_one = run_backward(
        2, 6, info, latents, shared,
        (weights_two, grad_mod_two, acc_qkv, acc_bias, after(grad_mod, held_two), grad_latents),
    )
    held_one = add([keep_one, move(send_one, CORE_SWAP)])
    arrived_one = scatter(held_one)
    two = sum_replicas(arrived_two, core)
    one = sum_replicas(arrived_one, core)
    grad_bias = (
        one[:, BIAS_ONE : BIAS_ONE + 128] + two[:, BIAS_TWO : BIAS_TWO + 128]
    ).reshape(-1)
    qv_at = shard * 96 + jnp.where(shard >= 4, D, 0)

    def part(first, size):
        return lax.dynamic_slice(grad_bias, (first,), (size,))

    return (
        out,
        grad_latents,
        grad_cond,
        jnp.concatenate([one[:, QKV_W : QKV_W + MOD_ONE], two[:, AT_MOD : AT_MOD + MOD_TWO]], 1),
        part(ROW_MOD * 128 + shard * 288, 288),
        one[:, :QKV_W],
        part(qv_at, 96),
        two[:, AT_PROJ : AT_PROJ + D],
        part(ROW_PROJ * 128 + shard * 48, 48),
        two[:, :FF],
        part(ROW_UP * 128 + shard * 192, 192),
        jnp.concatenate([two[:, AT_DOWN + D * q : AT_DOWN + D * q + D] for q in range(4)], 0),
        part(ROW_DOWN * 128 + shard * 48, 48),
    )


def solution(mesh):
    slots = P(("shard", "rep"), None, None)
    rows = P(("shard", "rep"), None)
    matrix, vector = P("shard", None), P("shard")
    in_specs = (slots, rows, P(("shard", "rep"))) + (matrix, vector) * 5 + (slots,)
    out_specs = (slots, slots, rows) + (matrix, vector) * 5
    return jax.shard_map(
        on_device, mesh=mesh, in_specs=in_specs, out_specs=out_specs, check_vma=False
    )
```

```python
import functools

import jax
import jax.numpy as jnp
from jax import lax
from jax.experimental import pallas as pl
from jax.experimental.pallas import tpu as pltpu
from jax.sharding import PartitionSpec as P

D = 384
HEADS = 6
HEAD_DIM = 64
FF = 1536
TOK = 256
CAP = 8
STEP = 1
TWIN = 128
BF = jnp.bfloat16
F32 = jnp.float32
MIB = 1024 * 1024

LANES_ONE = 2048
QKV_W = 3 * D
MOD_ONE = 2 * D
BIAS_ONE = QKV_W + MOD_ONE
LANES_TWO = 5120
MOD_TWO = 4 * D
AT_MOD = FF
AT_PROJ = AT_MOD + MOD_TWO
AT_DOWN = AT_PROJ + D
BIAS_TWO = AT_DOWN + FF
ROW_QKV, ROW_MOD, ROW_PROJ, ROW_UP, ROW_DOWN = 0, 9, 27, 30, 42


def dot(left, right):
    return jnp.dot(left, right, preferred_element_type=F32)


def dot_tn(left, right):
    return lax.dot_general(left, right, (((0,), (0,)), ((), ())), preferred_element_type=F32)


def dot_nt(left, right):
    return lax.dot_general(left, right, (((1,), (1,)), ((), ())), preferred_element_type=F32)


def normalize(value):
    center = jnp.mean(value, axis=-1, keepdims=True)
    centered = value - center
    spread = jnp.mean(centered * centered, axis=-1, keepdims=True)
    inverse = lax.rsqrt(spread + 1e-06)
    return centered * inverse, inverse


def norm_back(grad, normed, inverse):
    first = jnp.mean(grad, axis=-1, keepdims=True)
    second = jnp.mean(grad * normed, axis=-1, keepdims=True)
    return inverse * (grad - first - normed * second)


def spread(rows, size):
    width = 8 * size
    lane = lax.broadcasted_iota(jnp.int32, (8, width), 1)
    total = jnp.zeros((8, width), F32)
    for owner, row in enumerate(rows):
        padded = jnp.concatenate([row, jnp.zeros((1, width - row.shape[1]), F32)], axis=1)
        padded = jnp.where(lane < size, jnp.broadcast_to(padded, (8, width)), 0.0)
        total += pltpu.roll(padded, owner * size, 1) if owner else padded
    return total[0:1]


def all_biases(raw):
    def rows(first, count):
        return [
            jnp.concatenate([block[first + i : first + i + 1] for i in range(count)], axis=1)
            for block in raw
        ]

    qv = spread(rows(0, 1), 96)
    full = [qv[:, :D], jnp.zeros((1, D), F32), qv[:, D:]]
    full += [spread(rows(1, 3), 288), spread(rows(4, 1), 48)]
    full += [spread(rows(5, 2), 192), spread(rows(7, 1), 48)]
    full = jnp.concatenate(full, axis=1)
    cut = [full[:, 128 * i : 128 * i + 128] for i in range(45)]
    return jnp.concatenate(cut + [jnp.zeros((3, 128), F32)], axis=0)


def bias_row(bias, first, count):
    return jnp.concatenate([bias[first + i : first + i + 1, :] for i in range(count)], axis=1)


def silu(cond):
    return cond * (1.0 / (1.0 + jnp.exp(-cond)))


def assemble(info, pieces, full):
    column, z_high, core = info[1], info[2], info[3]
    for k in range(4):
        spot = lax.rem(column + k, 4) * 48
        mine = (z_high ^ core) * 192 + spot
        other = (1 - (z_high ^ core)) * 192 + spot
        full[pl.ds(pl.multiple_of(mine, 16), 48), :] = pieces[k][...]
        full[pl.ds(pl.multiple_of(other, 16), 48), :] = pieces[4 + k][...]


def forward_kernel(
    info, latents, conditions, p0, p1, p2, p3, p4, p5, p6, p7,
    weights, bias_out, mod_out, qkv_out, expo_out, mixed_out, rinv_out, hidden_out,
):
    step = pl.program_id(0)

    @pl.when(step == 0)
    def _():
        assemble(info, (p0, p1, p2, p3, p4, p5, p6, p7), weights)
        total = all_biases(
            [
                weights[48 * k : 48 * k + 16, BIAS_ONE : BIAS_ONE + 128].astype(F32)[:8]
                for k in range(8)
            ]
        )
        bias_out[...] = total
        cond_low = silu(conditions[...].astype(F32)).astype(BF)
        mod_out[...] = dot(cond_low, weights[:, QKV_W : QKV_W + MOD_ONE]) + bias_row(
            total, ROW_MOD, 6
        )

    @pl.when(step < info[0])
    def _():
        mod = mod_out[pl.ds(step, 1), :]
        normed, _ = normalize(latents[0].astype(F32))
        hidden = (normed * (1.0 + mod[:, D : 2 * D]) + mod[:, :D]).astype(BF)
        hidden_out[step] = hidden
        full_bias = bias_row(bias_out[0:16, :], ROW_QKV, 9)
        qkv = (dot(hidden, weights[:, :QKV_W]) + full_bias).astype(BF)
        qkv_out[step] = qkv
        low = lax.broadcasted_iota(jnp.int32, (TOK, 128), 1) < HEAD_DIM
        ones = jnp.ones((TOK, 128), BF)
        for pair in range(HEADS // 2):
            at = 128 * pair
            query = qkv[:, at : at + 128] * jnp.asarray(HEAD_DIM**-0.5, BF)
            key = qkv[:, D + at : D + at + 128]
            value = jnp.concatenate([qkv[:, 2 * D + at : 2 * D + at + 128], ones], axis=1)
            parts = []
            for half in range(2):
                chosen = jnp.where(low if half == 0 else ~low, query, jnp.zeros_like(query))
                scores = dot_nt(chosen, key)
                expo = jnp.exp(scores - jnp.max(scores, axis=-1, keepdims=True)).astype(BF)
                expo_out[step, 2 * pair + half] = expo
                parts.append(dot(expo, value))
            total = jnp.where(low, parts[0][:, 128:], parts[1][:, 128:])
            inverse = 1.0 / total
            rinv_out[step, :, at : at + 128] = inverse
            mixed_out[step, :, at : at + 128] = (
                jnp.where(low, parts[0][:, :128], parts[1][:, :128]) * inverse
            ).astype(BF)


def middle_kernel(
    info, latents, conditions, mixed_in, grad_out, bias_in, p0, p1, p2, p3, p4, p5, p6, p7,
    weights, out, grad_mid_out, grad_mixed_out, grad_mod, keep, send,
    mod, acc_up, acc_down, acc_proj, acc_bias,
):
    step = pl.program_id(0)

    @pl.when(step == 0)
    def _():
        assemble(info, (p0, p1, p2, p3, p4, p5, p6, p7), weights)
        cond_low = silu(conditions[...].astype(F32)).astype(BF)
        mod[...] = dot(cond_low, weights[:, AT_MOD : AT_MOD + MOD_TWO]) + bias_row(
            bias_in[...], ROW_MOD + 6, 12
        )
        acc_up[...] = jnp.zeros_like(acc_up)
        acc_down[...] = jnp.zeros_like(acc_down)
        acc_proj[...] = jnp.zeros_like(acc_proj)
        acc_bias[...] = jnp.zeros_like(acc_bias)
        grad_mod[...] = jnp.zeros_like(grad_mod)

    @pl.when(step >= info[0])
    def _():
        out[0] = jnp.zeros((TOK, D), BF)

    @pl.when(step < info[0])
    def _():
        row = mod[pl.ds(step, 1), :]
        gate_one, shift_two = row[:, :D], row[:, D : 2 * D]
        scale_two, gate_two = row[:, 2 * D : 3 * D], row[:, 3 * D :]
        bias = bias_in[...]
        mixed = mixed_in[step]
        w_proj = weights[:, AT_PROJ : AT_PROJ + D]
        branch_one = dot(mixed, w_proj) + bias_row(bias, ROW_PROJ, 3)
        middle = latents[0].astype(F32) + gate_one * branch_one
        normed, inverse = normalize(middle)
        hidden = (normed * (1.0 + scale_two) + shift_two).astype(BF)
        cot = grad_out[0].astype(F32)
        g_two = (cot * gate_two).astype(BF)
        up_bias = bias_row(bias, ROW_UP, 12)
        branch_two = bias_row(bias, ROW_DOWN, 3)
        d_hidden = jnp.zeros((TOK, D), F32)
        root = 0.7978845608028654
        cube = root * 0.044715
        for chunk in range(4):
            at = D * chunk
            w_up = weights[:, at : at + D]
            w_down = jnp.concatenate(
                [
                    weights[48 * s : 48 * s + 48, AT_DOWN + D * q : AT_DOWN + D * q + D]
                    for s in (2 * chunk, 2 * chunk + 1)
                    for q in range(4)
                ],
                axis=0,
            )
            upward = dot(hidden, w_up) + up_bias[:, at : at + D]
            square = upward * upward
            bend = jnp.tanh(upward * (root + cube * square))
            half = 0.5 + 0.5 * bend
            act = upward * half
            slope = half + act * (1.0 - bend) * (root + (3.0 * cube) * square)
            act_low = act.astype(BF)
            branch_two = branch_two + dot(act_low, w_down)
            acc_down[at : at + D, :] += dot_tn(act_low, g_two)
            g_up = (slope * dot_nt(g_two, w_down)).astype(BF)
            acc_up[:, at : at + D] += dot_tn(hidden, g_up)
            acc_bias[0:1, at : at + D] += jnp.sum(g_up.astype(F32), axis=0, keepdims=True)
            d_hidden = d_hidden + dot_nt(g_up, w_up)
        out[0] = (middle + gate_two * branch_two).astype(BF)
        acc_bias[1:2, :D] += jnp.sum(g_two.astype(F32), axis=0, keepdims=True)
        grad_mod[pl.ds(step, 1), 3 * D :] = jnp.sum(cot * branch_two, axis=0, keepdims=True)
        grad_mod[pl.ds(step, 1), D : 2 * D] = jnp.sum(d_hidden, axis=0, keepdims=True)
        grad_mod[pl.ds(step, 1), 2 * D : 3 * D] = jnp.sum(
            d_hidden * normed, axis=0, keepdims=True
        )
        grad_mid = cot + norm_back(d_hidden * (1.0 + scale_two), normed, inverse)
        grad_mid_out[step] = grad_mid
        grad_mod[pl.ds(step, 1), :D] = jnp.sum(grad_mid * branch_one, axis=0, keepdims=True)
        g_one = (grad_mid * gate_one).astype(BF)
        acc_bias[2:3, :D] += jnp.sum(g_one.astype(F32), axis=0, keepdims=True)
        acc_proj[...] += dot_tn(mixed, g_one)
        grad_mixed_out[step] = dot_nt(g_one, w_proj).astype(BF)

    @pl.when(step == CAP - 1)
    def _():
        cond_low = silu(conditions[...].astype(F32)).astype(BF)
        g_mod = grad_mod[...].astype(BF)
        mod_grad = dot_tn(cond_low.astype(F32), g_mod.astype(F32)).astype(BF)
        z_high, core, column = info[2], info[3], info[1]
        sums = jnp.sum(g_mod.astype(F32), axis=0, keepdims=True)
        rows = [jnp.zeros((ROW_MOD + 6, 128), F32)]
        rows += [sums[:, 128 * i : 128 * i + 128] for i in range(12)]
        rows += [acc_bias[2:3, 128 * i : 128 * i + 128] for i in range(3)]
        rows += [acc_bias[0:1, 128 * i : 128 * i + 128] for i in range(12)]
        rows += [acc_bias[1:2, 128 * i : 128 * i + 128] for i in range(3)]
        rows += [jnp.zeros((3, 128), F32)]
        bias_block = jnp.concatenate(rows, axis=0).astype(BF)
        for owner in range(8):
            zh, xx = owner // 4, owner % 4
            spot = lax.rem(xx - column + 4, 4) * 48
            spot = pl.multiple_of(spot, 16)
            is_mine = (z_high ^ core) == zh
            lo = 48 * owner

            def put(ref, spot=spot, lo=lo, owner=owner):
                ref[pl.ds(spot, 48), :FF] = acc_up[lo : lo + 48, :].astype(BF)
                ref[pl.ds(spot, 48), AT_MOD : AT_MOD + MOD_TWO] = mod_grad[lo : lo + 48, :]
                ref[pl.ds(spot, 48), AT_PROJ : AT_PROJ + D] = acc_proj[lo : lo + 48, :].astype(BF)
                for q in range(4):
                    at = 192 * owner + 48 * q
                    ref[pl.ds(spot, 48), AT_DOWN + D * q : AT_DOWN + D * q + D] = acc_down[
                        at : at + 48, :
                    ].astype(BF)
                ref[pl.ds(spot, 48), BIAS_TWO : BIAS_TWO + 128] = bias_block

            pl.when(is_mine)(functools.partial(put, keep))
            pl.when(jnp.logical_not(is_mine))(functools.partial(put, send))


def backward_kernel(
    first, last,
    info, latents, conditions, qkv_in, expo_in, mixed_in, rinv_in, hidden_in, grad_mid_in,
    grad_mixed_in, mod_in, weights, *refs,
):
    if last:
        weights_two, grad_mod_two, acc_in, bias_in, grad_mod_in, _, out, grad_cond, keep, send = refs[:10]
        acc_qkv, acc_bias, grad_mod = refs[10:]
    else:
        out, acc_qkv, acc_bias, grad_mod = refs
    step = pl.program_id(0)
    slot = step + first

    @pl.when(step == 0)
    def _():
        if last:
            acc_qkv[...] = acc_in[...]
            acc_bias[...] = bias_in[...]
            grad_mod[...] = grad_mod_in[...]
        else:
            acc_qkv[...] = jnp.zeros_like(acc_qkv)
            acc_bias[...] = jnp.zeros_like(acc_bias)
            grad_mod[...] = jnp.zeros_like(grad_mod)

    @pl.when(slot >= info[0])
    def _():
        out[0] = jnp.zeros((TOK, D), BF)

    @pl.when(slot < info[0])
    def _():
        row = mod_in[pl.ds(slot, 1), :]
        normed, inverse = normalize(latents[0].astype(F32))
        qkv = qkv_in[slot]
        hidden = hidden_in[slot]
        scaled = (grad_mixed_in[slot].astype(F32) * rinv_in[slot]).astype(BF)
        product = scaled.astype(F32) * mixed_in[slot].astype(F32)
        low = lax.broadcasted_iota(jnp.int32, (TOK, 128), 1) < HEAD_DIM
        low_wide = lax.broadcasted_iota(jnp.int32, (TOK, 128), 1) < HEAD_DIM
        factor = HEAD_DIM**-0.5
        g_query, g_key, g_value = [], [], []
        for pair in range(HEADS // 2):
            at = 128 * pair
            query = qkv[:, at : at + 128]
            key = qkv[:, D + at : D + at + 128]
            value = qkv[:, 2 * D + at : 2 * D + at + 128]
            grad = scaled[:, at : at + 128]
            weighed = product[:, at : at + 128]
            parts = []
            for half in range(2):
                mask = low if half == 0 else ~low
                chosen = jnp.where(mask, grad, jnp.zeros_like(grad))
                delta = jnp.sum(
                    jnp.where(low_wide if half == 0 else ~low_wide, weighed, 0.0),
                    axis=-1,
                    keepdims=True,
                )
                expo = expo_in[slot, 2 * pair + half]
                g_probs = dot_nt(chosen, value)
                g_scores = (expo.astype(F32) * (g_probs - delta)).astype(BF)
                parts.append(
                    (dot(g_scores, key), dot_tn(g_scores, query), dot_tn(expo, grad))
                )
            g_query.append((jnp.where(low_wide, parts[0][0], parts[1][0]) * factor).astype(BF))
            g_key.append((jnp.where(low_wide, parts[0][1], parts[1][1]) * factor).astype(BF))
            g_value.append(jnp.where(low_wide, parts[0][2], parts[1][2]).astype(BF))
        g_qkv = jnp.concatenate(g_query + g_key + g_value, axis=1)
        acc_qkv[...] += dot_tn(hidden, g_qkv)
        acc_bias[0:1, :] += jnp.sum(g_qkv.astype(F32), axis=0, keepdims=True)
        d_hidden = dot_nt(g_qkv, weights[:, :QKV_W])
        grad_mod[pl.ds(slot, 1), :D] = jnp.sum(d_hidden, axis=0, keepdims=True)
        grad_mod[pl.ds(slot, 1), D:] = jnp.sum(d_hidden * normed, axis=0, keepdims=True)
        out[0] = (
            grad_mid_in[slot] + norm_back(d_hidden * (1.0 + row[:, D : 2 * D]), normed, inverse)
        ).astype(BF)

    if not last:
        return

    @pl.when(step == CAP - 1 - first)
    def _():
        cond = conditions[...].astype(F32)
        sig = 1.0 / (1.0 + jnp.exp(-cond))
        cond_low = (cond * sig).astype(BF)
        g_mod = grad_mod[...].astype(BF)
        g_mod_two = grad_mod_two[...].astype(BF)
        g_cond = dot_nt(g_mod, weights[:, QKV_W : QKV_W + MOD_ONE])
        g_cond += dot_nt(g_mod_two, weights_two[:, AT_MOD : AT_MOD + MOD_TWO])
        grad_cond[...] = (g_cond * (sig * (1.0 + cond * (1.0 - sig)))).astype(BF)
        mod_grad = dot_tn(cond_low.astype(F32), g_mod.astype(F32)).astype(BF)
        sums = jnp.sum(g_mod.astype(F32), axis=0, keepdims=True)
        rows = [acc_bias[0:1, 128 * i : 128 * i + 128] for i in range(9)]
        rows += [sums[:, 128 * i : 128 * i + 128] for i in range(6)]
        rows += [jnp.zeros((33, 128), F32)]
        bias_block = jnp.concatenate(rows, axis=0).astype(BF)
        z_high, core, column = info[2], info[3], info[1]
        for owner in range(8):
            zh, xx = owner // 4, owner % 4
            spot = pl.multiple_of(lax.rem(xx - column + 4, 4) * 48, 16)
            is_mine = (z_high ^ core) == zh
            lo = 48 * owner

            def put(ref, spot=spot, lo=lo):
                ref[pl.ds(spot, 48), :QKV_W] = acc_qkv[lo : lo + 48, :].astype(BF)
                ref[pl.ds(spot, 48), QKV_W : QKV_W + MOD_ONE] = mod_grad[lo : lo + 48, :]
                ref[pl.ds(spot, 48), BIAS_ONE : BIAS_ONE + 128] = bias_block

            pl.when(is_mine)(functools.partial(put, keep))
            pl.when(jnp.logical_not(is_mine))(functools.partial(put, send))


def slot_spec(*shape):
    zeros = (0,) * len(shape)
    return pl.BlockSpec((1, *shape), lambda j, info: (jnp.minimum(j, jnp.maximum(info[0] - 1, 0)), *zeros))


def slot_out(*shape):
    zeros = (0,) * len(shape)
    return pl.BlockSpec((1, *shape), lambda j, info: (j, *zeros))


def held():
    return pl.BlockSpec(memory_space=pltpu.VMEM)


def whole(*shape):
    zeros = (0,) * len(shape)
    return pl.BlockSpec(shape, lambda j, info: zeros)


def params(mib):
    return pltpu.CompilerParams(
        dimension_semantics=("arbitrary",), vmem_limit_bytes=mib * MIB
    )


def stay(value):
    return pltpu.with_memory_space_constraint(value, pltpu.VMEM)


def run_forward(info, latents, conditions, pieces):
    return pl.pallas_call(
        forward_kernel,
        grid_spec=pltpu.PrefetchScalarGridSpec(
            num_scalar_prefetch=1,
            grid=(CAP,),
            in_specs=[slot_spec(TOK, D), whole(CAP, D)] + [held()] * 8,
            out_specs=[held()] * 8,
        ),
        out_shape=[
            pltpu.VMEM((D, LANES_ONE), BF),
            pltpu.VMEM((48, 128), F32),
            pltpu.VMEM((CAP, MOD_ONE), F32),
            pltpu.VMEM((CAP, TOK, QKV_W), BF),
            pltpu.VMEM((CAP, HEADS, TOK, TOK), BF),
            pltpu.VMEM((CAP, TOK, D), BF),
            pltpu.VMEM((CAP, TOK, D), F32),
            pltpu.VMEM((CAP, TOK, D), BF),
        ],
        compiler_params=params(10),
        name="attention_forward",
        cost_estimate=pl.CostEstimate(
            flops=3_000_000_000, bytes_accessed=20_000_000, transcendentals=3_000_000
        ),
    )(info, latents, conditions, *pieces)


def run_middle(info, latents, conditions, mixed, grad_out, bias, pieces):
    return pl.pallas_call(
        middle_kernel,
        grid_spec=pltpu.PrefetchScalarGridSpec(
            num_scalar_prefetch=1,
            grid=(CAP,),
            in_specs=[
                slot_spec(TOK, D),
                whole(CAP, D),
                held(),
                slot_spec(TOK, D),
                held(),
            ]
            + [held()] * 8,
            out_specs=[held(), slot_out(TOK, D)] + [held()] * 5,
            scratch_shapes=[
                pltpu.VMEM((CAP, MOD_TWO), F32),
                pltpu.VMEM((D, FF), F32),
                pltpu.VMEM((FF, D), F32),
                pltpu.VMEM((D, D), F32),
                pltpu.VMEM((8, FF), F32),
            ],
        ),
        out_shape=[
            pltpu.VMEM((D, LANES_TWO), BF),
            jax.ShapeDtypeStruct((CAP, TOK, D), BF),
            pltpu.VMEM((CAP, TOK, D), F32),
            pltpu.VMEM((CAP, TOK, D), BF),
            pltpu.VMEM((CAP, MOD_TWO), F32),
            pltpu.VMEM((192, LANES_TWO), BF),
            pltpu.VMEM((192, LANES_TWO), BF),
        ],
        compiler_params=params(16),
        name="feed_forward_both_ways",
        cost_estimate=pl.CostEstimate(
            flops=16_000_000_000, bytes_accessed=30_000_000, transcendentals=3_000_000
        ),
    )(info, latents, conditions, stay(mixed), grad_out, stay(bias), *pieces)


def run_backward(first, count, info, latents, shared, carried=None):
    last = carried is not None

    def slot_at(j, info):
        return (jnp.minimum(j + first, jnp.maximum(info[0] - 1, 0)), 0, 0)

    in_specs = [pl.BlockSpec((1, TOK, D), slot_at), whole(CAP, D)] + [held()] * 9
    out_specs = [pl.BlockSpec((1, TOK, D), lambda j, info: (j + first, 0, 0))]
    out_shape = [jax.ShapeDtypeStruct((CAP, TOK, D), BF)]
    state = [(D, QKV_W), (8, QKV_W), (CAP, MOD_ONE)]
    if last:
        in_specs += [held()] * 5 + [pl.BlockSpec(memory_space=pl.ANY)]
        out_specs += [whole(CAP, D), held(), held()]
        out_shape += [jax.ShapeDtypeStruct((CAP, D), BF)]
        out_shape += [pltpu.VMEM((192, LANES_ONE), BF)] * 2
    else:
        out_specs += [held()] * 3
        out_shape += [pltpu.VMEM(shape, F32) for shape in state]
    return pl.pallas_call(
        functools.partial(backward_kernel, first, last),
        grid_spec=pltpu.PrefetchScalarGridSpec(
            num_scalar_prefetch=1,
            grid=(count,),
            in_specs=in_specs,
            out_specs=out_specs,
            scratch_shapes=[pltpu.VMEM(shape, F32) for shape in state] if last else [],
        ),
        out_shape=out_shape,
        input_output_aliases={17: 0} if last else {},
        compiler_params=params(12),
        name="attention_backward_rest" if last else "attention_backward_start",
        cost_estimate=pl.CostEstimate(
            flops=1_100_000_000 * count, bytes_accessed=4_000_000 * count, transcendentals=1_000
        ),
    )(info, latents, shared[0], *map(stay, shared[1:]), *map(stay, (carried or ())[:-1]), *(carried or ())[-1:])


def place(index):
    shard, rep = divmod(index, 16)
    return shard // 4, shard % 4, rep // 4, (rep // 2) % 2, rep % 2


def index_of(z_high, x, y, z_low, core):
    return (z_high * 4 + x) * 16 + y * 4 + z_low * 2 + core


def routes(target_of):
    return [(i, target_of(*place(i))) for i in range(TWIN)]


def fetch(k):
    def source(zh, x, y, zl, c):
        if c == 0:
            return index_of(zh, (x + k) % 4, y, zl, c)
        return index_of(1 - zh, (x + k) % 4, y, 1 - zl, c)

    return [(source(*place(i)), i) for i in range(TWIN)]


CORE_SWAP = routes(lambda zh, x, y, zl, c: index_of(zh, x, y, zl, 1 - c))
ZLOW_SWAP = routes(lambda zh, x, y, zl, c: index_of(zh, x, y, 1 - zl, c))
BOTH = ("shard", "rep")


def move(value, pairs):
    return lax.ppermute(value, BOTH, pairs)


def y_route(k):
    return routes(lambda zh, x, y, zl, c: index_of(zh, x, (y + k) % 4, zl, c))


def after(value, *earlier):
    return lax.optimization_barrier((value, *earlier))[0]


def fetch_all(block):
    return [move(block, fetch(k)) for k in range(4)]


def swap_all(pieces):
    return [move(piece, CORE_SWAP) for piece in pieces]


def add(values, dtype=BF):
    return sum(v.astype(F32) for v in values).astype(dtype)


def scatter(held_sum):
    arrived = []
    for k in range(4):
        back = [(target, source) for source, target in fetch(k)]
        arrived.append(move(held_sum[48 * k : 48 * k + 48], back))
    return arrived


def sum_replicas(arrived, core):
    lanes = arrived[0].shape[1] // 2
    total = add(arrived)
    mine = lax.dynamic_slice(total, (0, core * lanes), (48, lanes))
    other = lax.dynamic_slice(total, (0, (1 - core) * lanes), (48, lanes))
    total = add([mine, move(other, CORE_SWAP)])
    total = add([total, move(total, ZLOW_SWAP)])
    total = add([total] + [move(total, y_route(k)) for k in (1, 2, 3)])
    swapped = move(total, CORE_SWAP)
    return [total, swapped]


def row_of(ref):
    size = ref.shape[0]
    row = ref[...].astype(F32).reshape(1, size)
    if size % 128:
        row = jnp.concatenate([row, jnp.zeros((1, -size % 128), F32)], axis=1)
    return row


def pack_one_kernel(qkv, mod, qv_bias, mod_bias, proj_bias, up_bias, down_bias, out):
    out[:, :QKV_W] = qkv[...]
    out[:, QKV_W:BIAS_ONE] = mod[:, :MOD_ONE]
    flat = [row_of(ref) for ref in (qv_bias, mod_bias, proj_bias, up_bias, down_bias)]
    flat = jnp.concatenate(flat, axis=1)
    rows = [flat[:, 128 * i : 128 * i + 128] for i in range(8)] + [jnp.zeros((40, 128), F32)]
    out[:, BIAS_ONE:] = jnp.concatenate(rows, axis=0).astype(BF)


def pack_two_kernel(up, mod, proj, down, out):
    out[:, :FF] = up[...]
    out[:, AT_MOD:AT_PROJ] = mod[:, MOD_ONE:]
    out[:, AT_PROJ:AT_DOWN] = proj[...]
    for q in range(4):
        out[:, AT_DOWN + D * q : AT_DOWN + D * q + D] = down[48 * q : 48 * q + 48, :]
    out[:, BIAS_TWO:] = jnp.zeros((48, 128), BF)


def pack(kernel, name, lanes, *values):
    return pl.pallas_call(
        kernel,
        out_shape=jax.ShapeDtypeStruct((48, lanes), BF),
        compiler_params=pltpu.CompilerParams(vmem_limit_bytes=8 * MIB),
        name=name,
    )(*values)


def finish_kernel(
    info, one_a, one_b, two_a, two_b, g_mod, g_mod_bias, g_qkv, g_qv_bias, g_proj, g_proj_bias,
    g_up, g_up_bias, g_down, g_down_bias,
):
    shard, first = info[1] + 4 * info[2], info[3] == 0

    def joined(mine, other):
        mine, other = mine[...].astype(F32), other[...].astype(F32)
        return jnp.concatenate(
            [jnp.where(first, mine, other), jnp.where(first, other, mine)], axis=1
        )

    one, two = joined(one_a, one_b), joined(two_a, two_b)
    g_mod[:, :MOD_ONE] = one[:, QKV_W:BIAS_ONE]
    g_mod[:, MOD_ONE:] = two[:, AT_MOD:AT_PROJ]
    g_qkv[...] = one[:, :QKV_W]
    g_proj[...] = two[:, AT_PROJ:AT_DOWN]
    g_up[...] = two[:, :FF]
    for q in range(4):
        g_down[48 * q : 48 * q + 48, :] = two[:, AT_DOWN + D * q : AT_DOWN + D * q + D]
    bias = one[:, BIAS_ONE:] + two[:, BIAS_TWO:]

    def own(first_row, count, size, out):
        row = bias_row(bias, first_row, count)
        row = jnp.broadcast_to(row, (8, 128 * count))
        turn = lax.rem(8 * size - shard * size, 8 * size)
        out[...] = pltpu.roll(row, turn, 1)[0:1, :size].reshape(size)

    own(ROW_MOD, 18, 288, g_mod_bias)
    query, value = bias_row(bias, 0, 3), bias_row(bias, 6, 3)
    row = jnp.broadcast_to(jnp.concatenate([query, value], axis=1), (8, 2 * D))
    turn = lax.rem(2 * D - shard * 96, 2 * D)
    g_qv_bias[...] = pltpu.roll(row, turn, 1)[0:1, :96].reshape(96)
    own(ROW_PROJ, 3, 48, g_proj_bias)
    own(ROW_UP, 12, 192, g_up_bias)
    own(ROW_DOWN, 3, 48, g_down_bias)


def finish(info, parts):
    shapes = [
        (48, 6 * D), (288,), (48, QKV_W), (96,), (48, D), (48,), (48, FF), (192,), (192, D), (48,),
    ]
    return pl.pallas_call(
        finish_kernel,
        in_specs=[pl.BlockSpec(memory_space=pltpu.SMEM)] + [held()] * 4,
        out_shape=[jax.ShapeDtypeStruct(shape, F32) for shape in shapes],
        compiler_params=pltpu.CompilerParams(vmem_limit_bytes=12 * MIB),
        name="unpack_gradients",
    )(info, *parts)


def on_device(
    latents, conditions, counts, mod_weight, mod_bias, qkv_weight, qv_bias, proj_weight,
    proj_bias, up_weight, up_bias, down_weight, down_bias, grad_out,
):
    shard = lax.axis_index("shard")
    rep = lax.axis_index("rep")
    info = jnp.stack([counts[0], shard % 4, shard // 4, rep % 2]).astype(jnp.int32)
    block_one = pack(
        pack_one_kernel, "pack_attention_weights", LANES_ONE,
        qkv_weight, mod_weight, qv_bias, mod_bias, proj_bias, up_bias, down_bias,
    )
    block_two = pack(
        pack_two_kernel, "pack_feed_forward_weights", LANES_TWO,
        up_weight, mod_weight, proj_weight, down_weight,
    )
    core = rep % 2
    mine_one = fetch_all(block_one)
    other_one = swap_all(mine_one)
    mine_two = fetch_all(after(block_two, *mine_one))
    weights, bias, mod, qkv, expo, mixed, rinv, hidden = run_forward(
        info, latents, conditions, mine_one + other_one
    )
    mine_two = [after(piece, mod) for piece in mine_two]
    other_two = swap_all(mine_two)
    weights_two, out, grad_mid, grad_mixed, grad_mod_two, keep_two, send_two = run_middle(
        info, latents, conditions, mixed, grad_out, bias, mine_two + other_two
    )
    swapped_two = move(send_two, CORE_SWAP)
    shared = (
        conditions, qkv, expo, mixed, rinv, hidden, grad_mid, grad_mixed, mod, weights,
    )
    grad_latents, acc_qkv, acc_bias, grad_mod = run_backward(0, 2, info, latents, shared)
    held_two = add([keep_two, after(swapped_two, acc_bias)])
    arrived_two = scatter(held_two)
    grad_latents, grad_cond, keep_one, send_one = run_backward(
        2, 6, info, latents, shared,
        (weights_two, grad_mod_two, acc_qkv, acc_bias, after(grad_mod, held_two), grad_latents),
    )
    held_one = add([keep_one, move(after(send_one, *arrived_two), CORE_SWAP)])
    arrived_one = scatter(held_one)
    two = sum_replicas(arrived_two, core)
    one = sum_replicas(arrived_one, core)
    return (out, grad_latents, grad_cond, *finish(info, one + two))


def solution(mesh):
    slots = P(("shard", "rep"), None, None)
    rows = P(("shard", "rep"), None)
    matrix, vector = P("shard", None), P("shard")
    in_specs = (slots, rows, P(("shard", "rep"))) + (matrix, vector) * 5 + (slots,)
    out_specs = (slots, slots, rows) + (matrix, vector) * 5
    return jax.shard_map(
        on_device, mesh=mesh, in_specs=in_specs, out_specs=out_specs, check_vma=False
    )
```

```python
import functools

import jax
import jax.numpy as jnp
from jax import lax
from jax.experimental import pallas as pl
from jax.experimental.pallas import tpu as pltpu
from jax.sharding import PartitionSpec as P

D = 384
HEADS = 6
HEAD_DIM = 64
FF = 1536
TOK = 256
CAP = 8
PAIR = 2
STEPS = CAP // PAIR
TWIN = 128
BF = jnp.bfloat16
F32 = jnp.float32
MIB = 1024 * 1024

LANES_ONE = 2048
QKV_W = 3 * D
MOD_ONE = 2 * D
BIAS_ONE = QKV_W + MOD_ONE
LANES_TWO = 5120
MOD_TWO = 4 * D
AT_MOD = FF
AT_PROJ = AT_MOD + MOD_TWO
AT_DOWN = AT_PROJ + D
BIAS_TWO = AT_DOWN + FF
ROW_QKV, ROW_MOD, ROW_PROJ, ROW_UP, ROW_DOWN = 0, 9, 27, 30, 42


def dot(left, right):
    return jnp.dot(left, right, preferred_element_type=F32)


def dot_tn(left, right):
    return lax.dot_general(left, right, (((0,), (0,)), ((), ())), preferred_element_type=F32)


def dot_nt(left, right):
    return lax.dot_general(left, right, (((1,), (1,)), ((), ())), preferred_element_type=F32)


def normalize(value):
    center = jnp.mean(value, axis=-1, keepdims=True)
    centered = value - center
    spread = jnp.mean(centered * centered, axis=-1, keepdims=True)
    inverse = lax.rsqrt(spread + 1e-06)
    return centered * inverse, inverse


def norm_back(grad, normed, inverse):
    first = jnp.mean(grad, axis=-1, keepdims=True)
    second = jnp.mean(grad * normed, axis=-1, keepdims=True)
    return inverse * (grad - first - normed * second)


def spread(rows, size):
    width = 8 * size
    lane = lax.broadcasted_iota(jnp.int32, (8, width), 1)
    total = jnp.zeros((8, width), F32)
    for owner, row in enumerate(rows):
        padded = jnp.concatenate([row, jnp.zeros((1, width - row.shape[1]), F32)], axis=1)
        padded = jnp.where(lane < size, jnp.broadcast_to(padded, (8, width)), 0.0)
        total += pltpu.roll(padded, owner * size, 1) if owner else padded
    return total[0:1]


def all_biases(raw):
    def rows(first, count):
        return [
            jnp.concatenate([block[first + i : first + i + 1] for i in range(count)], axis=1)
            for block in raw
        ]

    qv = spread(rows(0, 1), 96)
    full = [qv[:, :D], jnp.zeros((1, D), F32), qv[:, D:]]
    full += [spread(rows(1, 3), 288), spread(rows(4, 1), 48)]
    full += [spread(rows(5, 2), 192), spread(rows(7, 1), 48)]
    full = jnp.concatenate(full, axis=1)
    cut = [full[:, 128 * i : 128 * i + 128] for i in range(45)]
    return jnp.concatenate(cut + [jnp.zeros((3, 128), F32)], axis=0)


def bias_row(bias, first, count):
    return jnp.concatenate([bias[first + i : first + i + 1, :] for i in range(count)], axis=1)


def silu(cond):
    return cond * (1.0 / (1.0 + jnp.exp(-cond)))


def assemble(info, pieces, full):
    column, z_high, core = info[1], info[2], info[3]
    for k in range(4):
        spot = lax.rem(column + k, 4) * 48
        mine = (z_high ^ core) * 192 + spot
        other = (1 - (z_high ^ core)) * 192 + spot
        full[pl.ds(pl.multiple_of(mine, 16), 48), :] = pieces[k][...]
        full[pl.ds(pl.multiple_of(other, 16), 48), :] = pieces[4 + k][...]


def forward_kernel(
    info, latents, conditions, p0, p1, p2, p3, p4, p5, p6, p7,
    weights, bias_out, mod_out, qkv_out, expo_out, mixed_out, rinv_out, hidden_out,
):
    step = pl.program_id(0)

    @pl.when(step == 0)
    def _():
        assemble(info, (p0, p1, p2, p3, p4, p5, p6, p7), weights)
        total = all_biases(
            [
                weights[48 * k : 48 * k + 16, BIAS_ONE : BIAS_ONE + 128].astype(F32)[:8]
                for k in range(8)
            ]
        )
        bias_out[...] = total
        cond_low = silu(conditions[...].astype(F32)).astype(BF)
        mod_out[...] = dot(cond_low, weights[:, QKV_W : QKV_W + MOD_ONE]) + bias_row(
            total, ROW_MOD, 6
        )

    @pl.when(PAIR * step < info[0])
    def _():
        hidden = []
        for i in range(PAIR):
            mod = mod_out[pl.ds(PAIR * step + i, 1), :]
            normed, _ = normalize(latents[i].astype(F32))
            hidden.append((normed * (1.0 + mod[:, D : 2 * D]) + mod[:, :D]).astype(BF))
            hidden_out[PAIR * step + i] = hidden[i]
        full_bias = bias_row(bias_out[0:16, :], ROW_QKV, 9)
        qkv_all = dot(jnp.concatenate(hidden, axis=0), weights[:, :QKV_W])
        qkv_all = (qkv_all + full_bias).astype(BF)
        low = lax.broadcasted_iota(jnp.int32, (TOK, 128), 1) < HEAD_DIM
        ones = jnp.ones((TOK, 128), BF)
        for i in range(PAIR):
            slot = PAIR * step + i
            qkv = qkv_all[TOK * i : TOK * i + TOK]
            qkv_out[slot] = qkv
            for pair in range(HEADS // 2):
                at = 128 * pair
                query = qkv[:, at : at + 128] * jnp.asarray(HEAD_DIM**-0.5, BF)
                key = qkv[:, D + at : D + at + 128]
                value = jnp.concatenate([qkv[:, 2 * D + at : 2 * D + at + 128], ones], axis=1)
                parts = []
                for half in range(2):
                    chosen = jnp.where(low if half == 0 else ~low, query, jnp.zeros_like(query))
                    scores = dot_nt(chosen, key)
                    expo = jnp.exp(scores - jnp.max(scores, axis=-1, keepdims=True)).astype(BF)
                    expo_out[slot, 2 * pair + half] = expo
                    parts.append(dot(expo, value))
                total = jnp.where(low, parts[0][:, 128:], parts[1][:, 128:])
                inverse = 1.0 / total
                rinv_out[slot, :, at : at + 128] = inverse
                mixed_out[slot, :, at : at + 128] = (
                    jnp.where(low, parts[0][:, :128], parts[1][:, :128]) * inverse
                ).astype(BF)


def middle_kernel(
    info, latents, conditions, mixed_in, grad_out, bias_in, p0, p1, p2, p3, p4, p5, p6, p7,
    weights, out, grad_mid_out, grad_mixed_out, grad_mod, keep, send,
    mod, acc_up, acc_down, acc_proj, acc_bias,
):
    step = pl.program_id(0)

    @pl.when(step == 0)
    def _():
        assemble(info, (p0, p1, p2, p3, p4, p5, p6, p7), weights)
        cond_low = silu(conditions[...].astype(F32)).astype(BF)
        mod[...] = dot(cond_low, weights[:, AT_MOD : AT_MOD + MOD_TWO]) + bias_row(
            bias_in[...], ROW_MOD + 6, 12
        )
        acc_up[...] = jnp.zeros_like(acc_up)
        acc_down[...] = jnp.zeros_like(acc_down)
        acc_proj[...] = jnp.zeros_like(acc_proj)
        acc_bias[...] = jnp.zeros_like(acc_bias)
        grad_mod[...] = jnp.zeros_like(grad_mod)

    @pl.when(PAIR * step >= info[0])
    def _():
        out[...] = jnp.zeros((PAIR, TOK, D), BF)

    @pl.when(PAIR * step < info[0])
    def _():
        bias = bias_in[...]
        w_proj = weights[:, AT_PROJ : AT_PROJ + D]
        up_bias = bias_row(bias, ROW_UP, 12)
        mixed = mixed_in[pl.ds(PAIR * step, PAIR)].reshape(PAIR * TOK, D)
        branch_all = dot(mixed, w_proj) + bias_row(bias, ROW_PROJ, 3)
        rows = [mod[pl.ds(PAIR * step + i, 1), :] for i in range(PAIR)]
        span = [slice(TOK * i, TOK * i + TOK) for i in range(PAIR)]
        middle, normed, inverse, hidden, cot, g_two = [], [], [], [], [], []
        for i in range(PAIR):
            row = rows[i]
            middle.append(latents[i].astype(F32) + row[:, :D] * branch_all[span[i]])
            value, scale = normalize(middle[i])
            normed.append(value)
            inverse.append(scale)
            hidden.append((value * (1.0 + row[:, 2 * D : 3 * D]) + row[:, D : 2 * D]).astype(BF))
            held = (PAIR * step + i < info[0]).astype(F32)
            cot.append(grad_out[i].astype(F32) * held)
            g_two.append((cot[i] * row[:, 3 * D :]).astype(BF))
        hidden = jnp.concatenate(hidden, axis=0)
        g_two = jnp.concatenate(g_two, axis=0)
        branch_two = bias_row(bias, ROW_DOWN, 3)
        d_hidden = jnp.zeros((PAIR * TOK, D), F32)
        root = 0.7978845608028654
        cube = root * 0.044715
        for chunk in range(4):
            at = D * chunk
            w_up = weights[:, at : at + D]
            w_down = jnp.concatenate(
                [
                    weights[48 * s : 48 * s + 48, AT_DOWN + D * q : AT_DOWN + D * q + D]
                    for s in (2 * chunk, 2 * chunk + 1)
                    for q in range(4)
                ],
                axis=0,
            )
            upward = dot(hidden, w_up) + up_bias[:, at : at + D]
            square = upward * upward
            bend = jnp.tanh(upward * (root + cube * square))
            half = 0.5 + 0.5 * bend
            act = upward * half
            slope = half + act * (1.0 - bend) * (root + (3.0 * cube) * square)
            act_low = act.astype(BF)
            branch_two = branch_two + dot(act_low, w_down)
            acc_down[at : at + D, :] += dot_tn(act_low, g_two)
            g_up = (slope * dot_nt(g_two, w_down)).astype(BF)
            acc_up[:, at : at + D] += dot_tn(hidden, g_up)
            acc_bias[0:1, at : at + D] += jnp.sum(g_up.astype(F32), axis=0, keepdims=True)
            d_hidden = d_hidden + dot_nt(g_up, w_up)
        acc_bias[1:2, :D] += jnp.sum(g_two.astype(F32), axis=0, keepdims=True)
        g_one = []
        for i in range(PAIR):
            row, slot = rows[i], PAIR * step + i
            d_hid, br_two = d_hidden[span[i]], branch_two[span[i]]
            held = (slot < info[0]).astype(F32)
            out[i] = ((middle[i] + row[:, 3 * D :] * br_two) * held).astype(BF)
            grad_mod[pl.ds(slot, 1), 3 * D :] = jnp.sum(cot[i] * br_two, axis=0, keepdims=True)
            grad_mod[pl.ds(slot, 1), D : 2 * D] = jnp.sum(d_hid, axis=0, keepdims=True)
            grad_mod[pl.ds(slot, 1), 2 * D : 3 * D] = jnp.sum(
                d_hid * normed[i], axis=0, keepdims=True
            )
            grad_mid = cot[i] + norm_back(
                d_hid * (1.0 + row[:, 2 * D : 3 * D]), normed[i], inverse[i]
            )
            grad_mid_out[slot] = grad_mid
            grad_mod[pl.ds(slot, 1), :D] = jnp.sum(
                grad_mid * branch_all[span[i]], axis=0, keepdims=True
            )
            g_one.append((grad_mid * row[:, :D]).astype(BF))
        g_one = jnp.concatenate(g_one, axis=0)
        acc_bias[2:3, :D] += jnp.sum(g_one.astype(F32), axis=0, keepdims=True)
        acc_proj[...] += dot_tn(mixed, g_one)
        grad_mixed_out[pl.ds(PAIR * step, PAIR)] = (
            dot_nt(g_one, w_proj).astype(BF).reshape(PAIR, TOK, D)
        )

    @pl.when(step == STEPS - 1)
    def _():
        cond_low = silu(conditions[...].astype(F32)).astype(BF)
        g_mod = grad_mod[...].astype(BF)
        mod_grad = dot_tn(cond_low.astype(F32), g_mod.astype(F32)).astype(BF)
        z_high, core, column = info[2], info[3], info[1]
        sums = jnp.sum(g_mod.astype(F32), axis=0, keepdims=True)
        rows = [jnp.zeros((ROW_MOD + 6, 128), F32)]
        rows += [sums[:, 128 * i : 128 * i + 128] for i in range(12)]
        rows += [acc_bias[2:3, 128 * i : 128 * i + 128] for i in range(3)]
        rows += [acc_bias[0:1, 128 * i : 128 * i + 128] for i in range(12)]
        rows += [acc_bias[1:2, 128 * i : 128 * i + 128] for i in range(3)]
        rows += [jnp.zeros((3, 128), F32)]
        bias_block = jnp.concatenate(rows, axis=0).astype(BF)
        for owner in range(8):
            zh, xx = owner // 4, owner % 4
            spot = lax.rem(xx - column + 4, 4) * 48
            spot = pl.multiple_of(spot, 16)
            is_mine = (z_high ^ core) == zh
            lo = 48 * owner

            def put(ref, spot=spot, lo=lo, owner=owner):
                ref[pl.ds(spot, 48), :FF] = acc_up[lo : lo + 48, :].astype(BF)
                ref[pl.ds(spot, 48), AT_MOD : AT_MOD + MOD_TWO] = mod_grad[lo : lo + 48, :]
                ref[pl.ds(spot, 48), AT_PROJ : AT_PROJ + D] = acc_proj[lo : lo + 48, :].astype(BF)
                for q in range(4):
                    at = 192 * owner + 48 * q
                    ref[pl.ds(spot, 48), AT_DOWN + D * q : AT_DOWN + D * q + D] = acc_down[
                        at : at + 48, :
                    ].astype(BF)
                ref[pl.ds(spot, 48), BIAS_TWO : BIAS_TWO + 128] = bias_block

            pl.when(is_mine)(functools.partial(put, keep))
            pl.when(jnp.logical_not(is_mine))(functools.partial(put, send))


def backward_kernel(
    first, last,
    info, latents, conditions, qkv_in, expo_in, mixed_in, rinv_in, hidden_in, grad_mid_in,
    grad_mixed_in, mod_in, weights, *refs,
):
    if last:
        weights_two, grad_mod_two, acc_in, bias_in, grad_mod_in, _, out, grad_cond, keep, send = refs[:10]
        acc_qkv, acc_bias, grad_mod = refs[10:]
    else:
        out, acc_qkv, acc_bias, grad_mod = refs
    step = pl.program_id(0)
    slot = PAIR * (step + first)

    @pl.when(step == 0)
    def _():
        if last:
            acc_qkv[...] = acc_in[...]
            acc_bias[...] = bias_in[...]
            grad_mod[...] = grad_mod_in[...]
        else:
            acc_qkv[...] = jnp.zeros_like(acc_qkv)
            acc_bias[...] = jnp.zeros_like(acc_bias)
            grad_mod[...] = jnp.zeros_like(grad_mod)

    @pl.when(slot >= info[0])
    def _():
        out[...] = jnp.zeros((PAIR, TOK, D), BF)

    @pl.when(slot < info[0])
    def _():
        low = lax.broadcasted_iota(jnp.int32, (TOK, 128), 1) < HEAD_DIM
        factor = HEAD_DIM**-0.5
        g_all = []
        for i in range(PAIR):
            qkv = qkv_in[slot + i]
            scaled = (grad_mixed_in[slot + i].astype(F32) * rinv_in[slot + i]).astype(BF)
            product = scaled.astype(F32) * mixed_in[slot + i].astype(F32)
            g_query, g_key, g_value = [], [], []
            for pair in range(HEADS // 2):
                at = 128 * pair
                query = qkv[:, at : at + 128]
                key = qkv[:, D + at : D + at + 128]
                value = qkv[:, 2 * D + at : 2 * D + at + 128]
                grad = scaled[:, at : at + 128]
                weighed = product[:, at : at + 128]
                parts = []
                for half in range(2):
                    mask = low if half == 0 else ~low
                    chosen = jnp.where(mask, grad, jnp.zeros_like(grad))
                    delta = jnp.sum(jnp.where(mask, weighed, 0.0), axis=-1, keepdims=True)
                    expo = expo_in[slot + i, 2 * pair + half]
                    g_probs = dot_nt(chosen, value)
                    g_scores = (expo.astype(F32) * (g_probs - delta)).astype(BF)
                    parts.append(
                        (dot(g_scores, key), dot_tn(g_scores, query), dot_tn(expo, grad))
                    )
                g_query.append((jnp.where(low, parts[0][0], parts[1][0]) * factor).astype(BF))
                g_key.append((jnp.where(low, parts[0][1], parts[1][1]) * factor).astype(BF))
                g_value.append(jnp.where(low, parts[0][2], parts[1][2]).astype(BF))
            g_all.append(jnp.concatenate(g_query + g_key + g_value, axis=1))
        g_qkv = jnp.concatenate(g_all, axis=0)
        hidden = hidden_in[pl.ds(slot, PAIR)].reshape(PAIR * TOK, D)
        acc_qkv[...] += dot_tn(hidden, g_qkv)
        acc_bias[0:1, :] += jnp.sum(g_qkv.astype(F32), axis=0, keepdims=True)
        d_all = dot_nt(g_qkv, weights[:, :QKV_W])
        for i in range(PAIR):
            row = mod_in[pl.ds(slot + i, 1), :]
            normed, inverse = normalize(latents[i].astype(F32))
            d_hidden = d_all[TOK * i : TOK * i + TOK]
            grad_mod[pl.ds(slot + i, 1), :D] = jnp.sum(d_hidden, axis=0, keepdims=True)
            grad_mod[pl.ds(slot + i, 1), D:] = jnp.sum(d_hidden * normed, axis=0, keepdims=True)
            back = norm_back(d_hidden * (1.0 + row[:, D : 2 * D]), normed, inverse)
            out[i] = (grad_mid_in[slot + i] + back).astype(BF)

    if not last:
        return

    @pl.when(step == STEPS - 1 - first)
    def _():
        cond = conditions[...].astype(F32)
        sig = 1.0 / (1.0 + jnp.exp(-cond))
        cond_low = (cond * sig).astype(BF)
        g_mod = grad_mod[...].astype(BF)
        g_mod_two = grad_mod_two[...].astype(BF)
        g_cond = dot_nt(g_mod, weights[:, QKV_W : QKV_W + MOD_ONE])
        g_cond += dot_nt(g_mod_two, weights_two[:, AT_MOD : AT_MOD + MOD_TWO])
        grad_cond[...] = (g_cond * (sig * (1.0 + cond * (1.0 - sig)))).astype(BF)
        mod_grad = dot_tn(cond_low.astype(F32), g_mod.astype(F32)).astype(BF)
        sums = jnp.sum(g_mod.astype(F32), axis=0, keepdims=True)
        rows = [acc_bias[0:1, 128 * i : 128 * i + 128] for i in range(9)]
        rows += [sums[:, 128 * i : 128 * i + 128] for i in range(6)]
        rows += [jnp.zeros((33, 128), F32)]
        bias_block = jnp.concatenate(rows, axis=0).astype(BF)
        z_high, core, column = info[2], info[3], info[1]
        for owner in range(8):
            zh, xx = owner // 4, owner % 4
            spot = pl.multiple_of(lax.rem(xx - column + 4, 4) * 48, 16)
            is_mine = (z_high ^ core) == zh
            lo = 48 * owner

            def put(ref, spot=spot, lo=lo):
                ref[pl.ds(spot, 48), :QKV_W] = acc_qkv[lo : lo + 48, :].astype(BF)
                ref[pl.ds(spot, 48), QKV_W : QKV_W + MOD_ONE] = mod_grad[lo : lo + 48, :]
                ref[pl.ds(spot, 48), BIAS_ONE : BIAS_ONE + 128] = bias_block

            pl.when(is_mine)(functools.partial(put, keep))
            pl.when(jnp.logical_not(is_mine))(functools.partial(put, send))


def slot_spec(first=0):
    def index(j, info):
        return (jnp.minimum(j + first, jnp.maximum((info[0] + 1) // 2 - 1, 0)), 0, 0)

    return pl.BlockSpec((PAIR, TOK, D), index)


def slot_out(first=0):
    return pl.BlockSpec((PAIR, TOK, D), lambda j, info: (j + first, 0, 0))


def held():
    return pl.BlockSpec(memory_space=pltpu.VMEM)


def whole(*shape):
    zeros = (0,) * len(shape)
    return pl.BlockSpec(shape, lambda j, info: zeros)


def params(mib):
    return pltpu.CompilerParams(
        dimension_semantics=("arbitrary",), vmem_limit_bytes=mib * MIB
    )


def stay(value):
    return pltpu.with_memory_space_constraint(value, pltpu.VMEM)


def run_forward(info, latents, conditions, pieces):
    return pl.pallas_call(
        forward_kernel,
        grid_spec=pltpu.PrefetchScalarGridSpec(
            num_scalar_prefetch=1,
            grid=(STEPS,),
            in_specs=[slot_spec(), whole(CAP, D)] + [held()] * 8,
            out_specs=[held()] * 8,
        ),
        out_shape=[
            pltpu.VMEM((D, LANES_ONE), BF),
            pltpu.VMEM((48, 128), F32),
            pltpu.VMEM((CAP, MOD_ONE), F32),
            pltpu.VMEM((CAP, TOK, QKV_W), BF),
            pltpu.VMEM((CAP, HEADS, TOK, TOK), BF),
            pltpu.VMEM((CAP, TOK, D), BF),
            pltpu.VMEM((CAP, TOK, D), F32),
            pltpu.VMEM((CAP, TOK, D), BF),
        ],
        compiler_params=params(10),
        name="attention_forward",
        cost_estimate=pl.CostEstimate(
            flops=3_000_000_000, bytes_accessed=20_000_000, transcendentals=3_000_000
        ),
    )(info, latents, conditions, *pieces)


def run_middle(info, latents, conditions, mixed, grad_out, bias, pieces):
    return pl.pallas_call(
        middle_kernel,
        grid_spec=pltpu.PrefetchScalarGridSpec(
            num_scalar_prefetch=1,
            grid=(STEPS,),
            in_specs=[
                slot_spec(),
                whole(CAP, D),
                held(),
                slot_spec(),
                held(),
            ]
            + [held()] * 8,
            out_specs=[held(), slot_out()] + [held()] * 5,
            scratch_shapes=[
                pltpu.VMEM((CAP, MOD_TWO), F32),
                pltpu.VMEM((D, FF), F32),
                pltpu.VMEM((FF, D), F32),
                pltpu.VMEM((D, D), F32),
                pltpu.VMEM((8, FF), F32),
            ],
        ),
        out_shape=[
            pltpu.VMEM((D, LANES_TWO), BF),
            jax.ShapeDtypeStruct((CAP, TOK, D), BF),
            pltpu.VMEM((CAP, TOK, D), F32),
            pltpu.VMEM((CAP, TOK, D), BF),
            pltpu.VMEM((CAP, MOD_TWO), F32),
            pltpu.VMEM((192, LANES_TWO), BF),
            pltpu.VMEM((192, LANES_TWO), BF),
        ],
        compiler_params=params(16),
        name="feed_forward_both_ways",
        cost_estimate=pl.CostEstimate(
            flops=16_000_000_000, bytes_accessed=30_000_000, transcendentals=3_000_000
        ),
    )(info, latents, conditions, stay(mixed), grad_out, stay(bias), *pieces)


def run_backward(first, count, info, latents, shared, carried=None):
    last = carried is not None

    in_specs = [slot_spec(first), whole(CAP, D)] + [held()] * 9
    out_specs = [slot_out(first)]
    out_shape = [jax.ShapeDtypeStruct((CAP, TOK, D), BF)]
    state = [(D, QKV_W), (8, QKV_W), (CAP, MOD_ONE)]
    if last:
        in_specs += [held()] * 5 + [pl.BlockSpec(memory_space=pl.ANY)]
        out_specs += [whole(CAP, D), held(), held()]
        out_shape += [jax.ShapeDtypeStruct((CAP, D), BF)]
        out_shape += [pltpu.VMEM((192, LANES_ONE), BF)] * 2
    else:
        out_specs += [held()] * 3
        out_shape += [pltpu.VMEM(shape, F32) for shape in state]
    return pl.pallas_call(
        functools.partial(backward_kernel, first, last),
        grid_spec=pltpu.PrefetchScalarGridSpec(
            num_scalar_prefetch=1,
            grid=(count,),
            in_specs=in_specs,
            out_specs=out_specs,
            scratch_shapes=[pltpu.VMEM(shape, F32) for shape in state] if last else [],
        ),
        out_shape=out_shape,
        input_output_aliases={17: 0} if last else {},
        compiler_params=params(12),
        name="attention_backward_rest" if last else "attention_backward_start",
        cost_estimate=pl.CostEstimate(
            flops=2_200_000_000 * count, bytes_accessed=8_000_000 * count, transcendentals=1_000
        ),
    )(info, latents, shared[0], *map(stay, shared[1:]), *map(stay, (carried or ())[:-1]), *(carried or ())[-1:])


def place(index):
    shard, rep = divmod(index, 16)
    return shard // 4, shard % 4, rep // 4, (rep // 2) % 2, rep % 2


def index_of(z_high, x, y, z_low, core):
    return (z_high * 4 + x) * 16 + y * 4 + z_low * 2 + core


def routes(target_of):
    return [(i, target_of(*place(i))) for i in range(TWIN)]


def fetch(k):
    def source(zh, x, y, zl, c):
        if c == 0:
            return index_of(zh, (x + k) % 4, y, zl, c)
        return index_of(1 - zh, (x + k) % 4, y, 1 - zl, c)

    return [(source(*place(i)), i) for i in range(TWIN)]


CORE_SWAP = routes(lambda zh, x, y, zl, c: index_of(zh, x, y, zl, 1 - c))
ZLOW_SWAP = routes(lambda zh, x, y, zl, c: index_of(zh, x, y, 1 - zl, c))
BOTH = ("shard", "rep")


def move(value, pairs):
    return lax.ppermute(value, BOTH, pairs)


def y_route(k):
    return routes(lambda zh, x, y, zl, c: index_of(zh, x, (y + k) % 4, zl, c))


def after(value, *earlier):
    return lax.optimization_barrier((value, *earlier))[0]


def fetch_all(block):
    return [move(block, fetch(k)) for k in range(4)]


def swap_all(pieces):
    return [move(piece, CORE_SWAP) for piece in pieces]


def small_call(kernel, name, shapes, *values, scalars=False):
    return pl.pallas_call(
        kernel,
        in_specs=[pl.BlockSpec(memory_space=pltpu.SMEM)] * scalars
        + [held()] * (len(values) - scalars),
        out_shape=[jax.ShapeDtypeStruct(shape, BF) for shape in shapes],
        compiler_params=pltpu.CompilerParams(vmem_limit_bytes=14 * MIB),
        name=name,
    )(*values)


def add_kernel(*refs):
    refs[-1][...] = sum(ref[...].astype(F32) for ref in refs[:-1]).astype(BF)


def add(*values):
    return small_call(add_kernel, "add", [values[0].shape], *values)[0]


def add_blocks_kernel(left, right, *outs):
    for k, out in enumerate(outs):
        rows = slice(48 * k, 48 * k + 48)
        out[...] = (left[rows, :].astype(F32) + right[rows, :].astype(F32)).astype(BF)


def add_blocks(left, right):
    shape = (48, left.shape[1])
    return small_call(add_blocks_kernel, "add_blocks", [shape] * 4, left, right)


def add_halves_kernel(info, *refs):
    lanes = refs[-1].shape[1]
    for out, core in ((refs[-2], info[3]), (refs[-1], 1 - info[3])):
        at = pl.ds(pl.multiple_of(core * lanes, 128), lanes)
        out[...] = sum(ref[:, at].astype(F32) for ref in refs[:-2]).astype(BF)


def add_halves(info, pieces):
    shape = (48, pieces[0].shape[1] // 2)
    return small_call(
        add_halves_kernel, "add_halves", [shape] * 2, info, *pieces, scalars=True
    )


def scatter(blocks):
    back = [[(target, source) for source, target in fetch(k)] for k in range(4)]
    return [move(block, pairs) for block, pairs in zip(blocks, back)]


def sum_replicas(arrived, info):
    mine, other = add_halves(info, arrived)
    total = add(mine, move(other, CORE_SWAP))
    total = add(total, move(total, ZLOW_SWAP))
    total = add(total, *(move(total, y_route(k)) for k in (1, 2, 3)))
    return [total, move(total, CORE_SWAP)]


def row_of(ref):
    size = ref.shape[0]
    row = ref[...].astype(F32).reshape(1, size)
    if size % 128:
        row = jnp.concatenate([row, jnp.zeros((1, -size % 128), F32)], axis=1)
    return row


def pack_one_kernel(qkv, mod, qv_bias, mod_bias, proj_bias, up_bias, down_bias, out):
    out[:, :QKV_W] = qkv[...]
    out[:, QKV_W:BIAS_ONE] = mod[:, :MOD_ONE]
    flat = [row_of(ref) for ref in (qv_bias, mod_bias, proj_bias, up_bias, down_bias)]
    flat = jnp.concatenate(flat, axis=1)
    rows = [flat[:, 128 * i : 128 * i + 128] for i in range(8)] + [jnp.zeros((40, 128), F32)]
    out[:, BIAS_ONE:] = jnp.concatenate(rows, axis=0).astype(BF)


def pack_two_kernel(up, mod, proj, down, out):
    out[:, :FF] = up[...]
    out[:, AT_MOD:AT_PROJ] = mod[:, MOD_ONE:]
    out[:, AT_PROJ:AT_DOWN] = proj[...]
    for q in range(4):
        out[:, AT_DOWN + D * q : AT_DOWN + D * q + D] = down[48 * q : 48 * q + 48, :]
    out[:, BIAS_TWO:] = jnp.zeros((48, 128), BF)


def pack(kernel, name, lanes, *values):
    return pl.pallas_call(
        kernel,
        out_shape=jax.ShapeDtypeStruct((48, lanes), BF),
        compiler_params=pltpu.CompilerParams(vmem_limit_bytes=8 * MIB),
        name=name,
    )(*values)


def finish_kernel(
    info, one_a, one_b, two_a, two_b, g_mod, g_mod_bias, g_qkv, g_qv_bias, g_proj, g_proj_bias,
    g_up, g_up_bias, g_down, g_down_bias,
):
    shard, first = info[1] + 4 * info[2], info[3] == 0

    def joined(mine, other):
        mine, other = mine[...].astype(F32), other[...].astype(F32)
        return jnp.concatenate(
            [jnp.where(first, mine, other), jnp.where(first, other, mine)], axis=1
        )

    one, two = joined(one_a, one_b), joined(two_a, two_b)
    g_mod[:, :MOD_ONE] = one[:, QKV_W:BIAS_ONE]
    g_mod[:, MOD_ONE:] = two[:, AT_MOD:AT_PROJ]
    g_qkv[...] = one[:, :QKV_W]
    g_proj[...] = two[:, AT_PROJ:AT_DOWN]
    g_up[...] = two[:, :FF]
    for q in range(4):
        g_down[48 * q : 48 * q + 48, :] = two[:, AT_DOWN + D * q : AT_DOWN + D * q + D]
    bias = one[:, BIAS_ONE:] + two[:, BIAS_TWO:]

    def own(first_row, count, size, out):
        row = bias_row(bias, first_row, count)
        row = jnp.broadcast_to(row, (8, 128 * count))
        turn = lax.rem(8 * size - shard * size, 8 * size)
        out[...] = pltpu.roll(row, turn, 1)[0:1, :size].reshape(size)

    own(ROW_MOD, 18, 288, g_mod_bias)
    query, value = bias_row(bias, 0, 3), bias_row(bias, 6, 3)
    row = jnp.broadcast_to(jnp.concatenate([query, value], axis=1), (8, 2 * D))
    turn = lax.rem(2 * D - shard * 96, 2 * D)
    g_qv_bias[...] = pltpu.roll(row, turn, 1)[0:1, :96].reshape(96)
    own(ROW_PROJ, 3, 48, g_proj_bias)
    own(ROW_UP, 12, 192, g_up_bias)
    own(ROW_DOWN, 3, 48, g_down_bias)


def finish(info, parts):
    shapes = [
        (48, 6 * D), (288,), (48, QKV_W), (96,), (48, D), (48,), (48, FF), (192,), (192, D), (48,),
    ]
    return pl.pallas_call(
        finish_kernel,
        in_specs=[pl.BlockSpec(memory_space=pltpu.SMEM)] + [held()] * 4,
        out_shape=[jax.ShapeDtypeStruct(shape, F32) for shape in shapes],
        compiler_params=pltpu.CompilerParams(vmem_limit_bytes=12 * MIB),
        name="unpack_gradients",
    )(info, *parts)


def on_device(
    latents, conditions, counts, mod_weight, mod_bias, qkv_weight, qv_bias, proj_weight,
    proj_bias, up_weight, up_bias, down_weight, down_bias, grad_out,
):
    shard = lax.axis_index("shard")
    rep = lax.axis_index("rep")
    info = jnp.stack([counts[0], shard % 4, shard // 4, rep % 2]).astype(jnp.int32)
    block_one = pack(
        pack_one_kernel, "pack_attention_weights", LANES_ONE,
        after(qkv_weight, info), mod_weight, qv_bias, mod_bias, proj_bias, up_bias, down_bias,
    )
    block_two = pack(
        pack_two_kernel, "pack_feed_forward_weights", LANES_TWO,
        up_weight, mod_weight, proj_weight, down_weight,
    )
    mine_one = fetch_all(block_one)
    other_one = swap_all(mine_one)
    mine_two = fetch_all(after(block_two, *mine_one))
    weights, bias, mod, qkv, expo, mixed, rinv, hidden = run_forward(
        info, latents, conditions, mine_one + other_one
    )
    mine_two = [after(piece, mod) for piece in mine_two]
    other_two = swap_all(mine_two)
    weights_two, out, grad_mid, grad_mixed, grad_mod_two, keep_two, send_two = run_middle(
        info, latents, conditions, mixed, grad_out, bias, mine_two + other_two
    )
    swapped_two = move(send_two, CORE_SWAP)
    shared = (
        conditions, qkv, expo, mixed, rinv, hidden, grad_mid, grad_mixed, mod, weights,
    )
    grad_latents, acc_qkv, acc_bias, grad_mod = run_backward(0, 1, info, latents, shared)
    held_two = add_blocks(keep_two, after(swapped_two, acc_bias))
    arrived_two = scatter(held_two)
    grad_latents, grad_cond, keep_one, send_one = run_backward(
        1, 3, info, latents, shared,
        (weights_two, grad_mod_two, acc_qkv, acc_bias, after(grad_mod, held_two[0]), grad_latents),
    )
    held_one = add_blocks(keep_one, move(after(send_one, *arrived_two), CORE_SWAP))
    arrived_one = scatter(held_one)
    two = sum_replicas(arrived_two, info)
    one = sum_replicas(arrived_one, info)
    return (out, grad_latents, grad_cond, *finish(info, one + two))


def solution(mesh):
    slots = P(("shard", "rep"), None, None)
    rows = P(("shard", "rep"), None)
    matrix, vector = P("shard", None), P("shard")
    in_specs = (slots, rows, P(("shard", "rep"))) + (matrix, vector) * 5 + (slots,)
    out_specs = (slots, slots, rows) + (matrix, vector) * 5
    return jax.shard_map(
        on_device, mesh=mesh, in_specs=in_specs, out_specs=out_specs, check_vma=False
    )
```

```python
import functools

import jax
import jax.numpy as jnp
from jax import lax
from jax.experimental import pallas as pl
from jax.experimental.pallas import tpu as pltpu
from jax.sharding import PartitionSpec as P

D = 384
HEADS = 6
HEAD_DIM = 64
FF = 1536
TOK = 256
CAP = 8
PAIR = 2
STEPS = CAP // PAIR
TWIN = 128
BF = jnp.bfloat16
F32 = jnp.float32
MIB = 1024 * 1024

LANES_ONE = 2048
QKV_W = 3 * D
MOD_ONE = 2 * D
BIAS_ONE = QKV_W + MOD_ONE
LANES_TWO = 5120
MOD_TWO = 4 * D
AT_MOD = FF
AT_PROJ = AT_MOD + MOD_TWO
AT_DOWN = AT_PROJ + D
BIAS_TWO = AT_DOWN + FF
ROW_QKV, ROW_MOD, ROW_PROJ, ROW_UP, ROW_DOWN = 0, 9, 27, 30, 42


def dot(left, right):
    return jnp.dot(left, right, preferred_element_type=F32)


def dot_tn(left, right):
    return lax.dot_general(left, right, (((0,), (0,)), ((), ())), preferred_element_type=F32)


def dot_nt(left, right):
    return lax.dot_general(left, right, (((1,), (1,)), ((), ())), preferred_element_type=F32)


def normalize(value):
    center = jnp.mean(value, axis=-1, keepdims=True)
    centered = value - center
    spread = jnp.mean(centered * centered, axis=-1, keepdims=True)
    inverse = lax.rsqrt(spread + 1e-06)
    return centered * inverse, inverse


def norm_back(grad, normed, inverse):
    first = jnp.mean(grad, axis=-1, keepdims=True)
    second = jnp.mean(grad * normed, axis=-1, keepdims=True)
    return inverse * (grad - first - normed * second)


def spread(rows, size):
    width = 8 * size
    lane = lax.broadcasted_iota(jnp.int32, (8, width), 1)
    total = jnp.zeros((8, width), F32)
    for owner, row in enumerate(rows):
        padded = jnp.concatenate([row, jnp.zeros((1, width - row.shape[1]), F32)], axis=1)
        padded = jnp.where(lane < size, jnp.broadcast_to(padded, (8, width)), 0.0)
        total += pltpu.roll(padded, owner * size, 1) if owner else padded
    return total[0:1]


def all_biases(raw):
    def rows(first, count):
        return [
            jnp.concatenate([block[first + i : first + i + 1] for i in range(count)], axis=1)
            for block in raw
        ]

    qv = spread(rows(0, 1), 96)
    full = [qv[:, :D], jnp.zeros((1, D), F32), qv[:, D:]]
    full += [spread(rows(1, 3), 288), spread(rows(4, 1), 48)]
    full += [spread(rows(5, 2), 192), spread(rows(7, 1), 48)]
    full = jnp.concatenate(full, axis=1)
    cut = [full[:, 128 * i : 128 * i + 128] for i in range(45)]
    return jnp.concatenate(cut + [jnp.zeros((3, 128), F32)], axis=0)


def bias_row(bias, first, count):
    return jnp.concatenate([bias[first + i : first + i + 1, :] for i in range(count)], axis=1)


def silu(cond):
    return cond * (1.0 / (1.0 + jnp.exp(-cond)))


def assemble(info, pieces, full):
    column, z_high, core = info[1], info[2], info[3]
    for k in range(4):
        spot = lax.rem(column + k, 4) * 48
        mine = (z_high ^ core) * 192 + spot
        other = (1 - (z_high ^ core)) * 192 + spot
        full[pl.ds(pl.multiple_of(mine, 16), 48), :] = pieces[k][...]
        full[pl.ds(pl.multiple_of(other, 16), 48), :] = pieces[4 + k][...]


def forward_kernel(
    info, latents, conditions, p0, p1, p2, p3, p4, p5, p6, p7,
    weights, bias_out, mod_out, qkv_out, expo_out, mixed_out, rinv_out, hidden_out,
):
    step = pl.program_id(0)

    @pl.when(step == 0)
    def _():
        assemble(info, (p0, p1, p2, p3, p4, p5, p6, p7), weights)
        total = all_biases(
            [
                weights[48 * k : 48 * k + 16, BIAS_ONE : BIAS_ONE + 128].astype(F32)[:8]
                for k in range(8)
            ]
        )
        bias_out[...] = total
        cond_low = silu(conditions[...].astype(F32)).astype(BF)
        mod_out[...] = dot(cond_low, weights[:, QKV_W : QKV_W + MOD_ONE]) + bias_row(
            total, ROW_MOD, 6
        )

    @pl.when(PAIR * step < info[0])
    def _():
        hidden = []
        for i in range(PAIR):
            mod = mod_out[pl.ds(PAIR * step + i, 1), :]
            normed, _ = normalize(latents[i].astype(F32))
            hidden.append((normed * (1.0 + mod[:, D : 2 * D]) + mod[:, :D]).astype(BF))
            hidden_out[PAIR * step + i] = hidden[i]
        full_bias = bias_row(bias_out[0:16, :], ROW_QKV, 9)
        qkv_all = dot(jnp.concatenate(hidden, axis=0), weights[:, :QKV_W])
        qkv_all = (qkv_all + full_bias).astype(BF)
        low = lax.broadcasted_iota(jnp.int32, (TOK, 128), 1) < HEAD_DIM
        ones = jnp.ones((TOK, 128), BF)
        for i in range(PAIR):
            slot = PAIR * step + i
            qkv = qkv_all[TOK * i : TOK * i + TOK]
            qkv_out[slot] = qkv
            for pair in range(HEADS // 2):
                at = 128 * pair
                query = qkv[:, at : at + 128] * jnp.asarray(HEAD_DIM**-0.5, BF)
                key = qkv[:, D + at : D + at + 128]
                value = jnp.concatenate([qkv[:, 2 * D + at : 2 * D + at + 128], ones], axis=1)
                parts = []
                for half in range(2):
                    chosen = jnp.where(low if half == 0 else ~low, query, jnp.zeros_like(query))
                    scores = dot_nt(chosen, key)
                    expo = jnp.exp(scores - jnp.max(scores, axis=-1, keepdims=True)).astype(BF)
                    expo_out[slot, 2 * pair + half] = expo
                    parts.append(dot(expo, value))
                total = jnp.where(low, parts[0][:, 128:], parts[1][:, 128:])
                inverse = 1.0 / total
                rinv_out[slot, :, at : at + 128] = inverse
                mixed_out[slot, :, at : at + 128] = (
                    jnp.where(low, parts[0][:, :128], parts[1][:, :128]) * inverse
                ).astype(BF)


def middle_kernel(
    info, latents, conditions, mixed_in, grad_out, bias_in, p0, p1, p2, p3, p4, p5, p6, p7,
    weights, out, grad_mid_out, grad_mixed_out, grad_mod, keep, send,
    mod, acc_up, acc_down, acc_proj, acc_bias,
):
    step = pl.program_id(0)

    @pl.when(step == 0)
    def _():
        assemble(info, (p0, p1, p2, p3, p4, p5, p6, p7), weights)
        cond_low = silu(conditions[...].astype(F32)).astype(BF)
        mod[...] = dot(cond_low, weights[:, AT_MOD : AT_MOD + MOD_TWO]) + bias_row(
            bias_in[...], ROW_MOD + 6, 12
        )
        acc_up[...] = jnp.zeros_like(acc_up)
        acc_down[...] = jnp.zeros_like(acc_down)
        acc_proj[...] = jnp.zeros_like(acc_proj)
        acc_bias[...] = jnp.zeros_like(acc_bias)
        grad_mod[...] = jnp.zeros_like(grad_mod)

    @pl.when(PAIR * step >= info[0])
    def _():
        out[...] = jnp.zeros((PAIR, TOK, D), BF)

    @pl.when(PAIR * step < info[0])
    def _():
        bias = bias_in[...]
        w_proj = weights[:, AT_PROJ : AT_PROJ + D]
        up_bias = bias_row(bias, ROW_UP, 12)
        mixed = mixed_in[pl.ds(PAIR * step, PAIR)].reshape(PAIR * TOK, D)
        branch_all = dot(mixed, w_proj) + bias_row(bias, ROW_PROJ, 3)
        rows = [mod[pl.ds(PAIR * step + i, 1), :] for i in range(PAIR)]
        span = [slice(TOK * i, TOK * i + TOK) for i in range(PAIR)]
        middle, normed, inverse, hidden, cot, g_two = [], [], [], [], [], []
        for i in range(PAIR):
            row = rows[i]
            middle.append(latents[i].astype(F32) + row[:, :D] * branch_all[span[i]])
            value, scale = normalize(middle[i])
            normed.append(value)
            inverse.append(scale)
            hidden.append((value * (1.0 + row[:, 2 * D : 3 * D]) + row[:, D : 2 * D]).astype(BF))
            held = (PAIR * step + i < info[0]).astype(F32)
            cot.append(grad_out[i].astype(F32) * held)
            g_two.append((cot[i] * row[:, 3 * D :]).astype(BF))
        hidden = jnp.concatenate(hidden, axis=0)
        g_two = jnp.concatenate(g_two, axis=0)
        branch_two = bias_row(bias, ROW_DOWN, 3)
        d_hidden = jnp.zeros((PAIR * TOK, D), F32)
        root = 0.7978845608028654
        cube = root * 0.044715
        for chunk in range(4):
            at = D * chunk
            w_up = weights[:, at : at + D]
            w_down = jnp.concatenate(
                [
                    weights[48 * s : 48 * s + 48, AT_DOWN + D * q : AT_DOWN + D * q + D]
                    for s in (2 * chunk, 2 * chunk + 1)
                    for q in range(4)
                ],
                axis=0,
            )
            upward = dot(hidden, w_up) + up_bias[:, at : at + D]
            square = upward * upward
            bend = jnp.tanh(upward * (root + cube * square))
            half = 0.5 + 0.5 * bend
            act = upward * half
            slope = half + act * (1.0 - bend) * (root + (3.0 * cube) * square)
            act_low = act.astype(BF)
            branch_two = branch_two + dot(act_low, w_down)
            acc_down[at : at + D, :] += dot_tn(act_low, g_two)
            g_up = (slope * dot_nt(g_two, w_down)).astype(BF)
            acc_up[:, at : at + D] += dot_tn(hidden, g_up)
            acc_bias[0:1, at : at + D] += jnp.sum(g_up.astype(F32), axis=0, keepdims=True)
            d_hidden = d_hidden + dot_nt(g_up, w_up)
        acc_bias[1:2, :D] += jnp.sum(g_two.astype(F32), axis=0, keepdims=True)
        g_one = []
        for i in range(PAIR):
            row, slot = rows[i], PAIR * step + i
            d_hid, br_two = d_hidden[span[i]], branch_two[span[i]]
            held = (slot < info[0]).astype(F32)
            out[i] = ((middle[i] + row[:, 3 * D :] * br_two) * held).astype(BF)
            grad_mod[pl.ds(slot, 1), 3 * D :] = jnp.sum(cot[i] * br_two, axis=0, keepdims=True)
            grad_mod[pl.ds(slot, 1), D : 2 * D] = jnp.sum(d_hid, axis=0, keepdims=True)
            grad_mod[pl.ds(slot, 1), 2 * D : 3 * D] = jnp.sum(
                d_hid * normed[i], axis=0, keepdims=True
            )
            grad_mid = cot[i] + norm_back(
                d_hid * (1.0 + row[:, 2 * D : 3 * D]), normed[i], inverse[i]
            )
            grad_mid_out[slot] = grad_mid
            grad_mod[pl.ds(slot, 1), :D] = jnp.sum(
                grad_mid * branch_all[span[i]], axis=0, keepdims=True
            )
            g_one.append((grad_mid * row[:, :D]).astype(BF))
        g_one = jnp.concatenate(g_one, axis=0)
        acc_bias[2:3, :D] += jnp.sum(g_one.astype(F32), axis=0, keepdims=True)
        acc_proj[...] += dot_tn(mixed, g_one)
        grad_mixed_out[pl.ds(PAIR * step, PAIR)] = (
            dot_nt(g_one, w_proj).astype(BF).reshape(PAIR, TOK, D)
        )

    @pl.when(step == STEPS - 1)
    def _():
        cond_low = silu(conditions[...].astype(F32)).astype(BF)
        g_mod = grad_mod[...].astype(BF)
        mod_grad = dot_tn(cond_low.astype(F32), g_mod.astype(F32)).astype(BF)
        z_high, core, column = info[2], info[3], info[1]
        sums = jnp.sum(g_mod.astype(F32), axis=0, keepdims=True)
        rows = [jnp.zeros((ROW_MOD + 6, 128), F32)]
        rows += [sums[:, 128 * i : 128 * i + 128] for i in range(12)]
        rows += [acc_bias[2:3, 128 * i : 128 * i + 128] for i in range(3)]
        rows += [acc_bias[0:1, 128 * i : 128 * i + 128] for i in range(12)]
        rows += [acc_bias[1:2, 128 * i : 128 * i + 128] for i in range(3)]
        rows += [jnp.zeros((3, 128), F32)]
        bias_block = jnp.concatenate(rows, axis=0).astype(BF)
        for owner in range(8):
            zh, xx = owner // 4, owner % 4
            spot = lax.rem(xx - column + 4, 4) * 48
            spot = pl.multiple_of(spot, 16)
            is_mine = (z_high ^ core) == zh
            lo = 48 * owner

            def put(ref, spot=spot, lo=lo, owner=owner):
                ref[pl.ds(spot, 48), :FF] = acc_up[lo : lo + 48, :].astype(BF)
                ref[pl.ds(spot, 48), AT_MOD : AT_MOD + MOD_TWO] = mod_grad[lo : lo + 48, :]
                ref[pl.ds(spot, 48), AT_PROJ : AT_PROJ + D] = acc_proj[lo : lo + 48, :].astype(BF)
                for q in range(4):
                    at = 192 * owner + 48 * q
                    ref[pl.ds(spot, 48), AT_DOWN + D * q : AT_DOWN + D * q + D] = acc_down[
                        at : at + 48, :
                    ].astype(BF)
                ref[pl.ds(spot, 48), BIAS_TWO : BIAS_TWO + 128] = bias_block

            pl.when(is_mine)(functools.partial(put, keep))
            pl.when(jnp.logical_not(is_mine))(functools.partial(put, send))


def backward_kernel(
    first, last,
    info, latents, conditions, qkv_in, expo_in, mixed_in, rinv_in, hidden_in, grad_mid_in,
    grad_mixed_in, mod_in, weights, *refs,
):
    if last:
        weights_two, grad_mod_two, acc_in, bias_in, grad_mod_in, _, out, grad_cond, keep, send = refs[:10]
        acc_qkv, acc_bias, grad_mod = refs[10:]
    else:
        out, acc_qkv, acc_bias, grad_mod = refs
    step = pl.program_id(0)
    slot = PAIR * (step + first)

    @pl.when(step == 0)
    def _():
        if last:
            acc_qkv[...] = acc_in[...]
            acc_bias[...] = bias_in[...]
            grad_mod[...] = grad_mod_in[...]
        else:
            acc_qkv[...] = jnp.zeros_like(acc_qkv)
            acc_bias[...] = jnp.zeros_like(acc_bias)
            grad_mod[...] = jnp.zeros_like(grad_mod)

    @pl.when(slot >= info[0])
    def _():
        out[...] = jnp.zeros((PAIR, TOK, D), BF)

    @pl.when(slot < info[0])
    def _():
        low = lax.broadcasted_iota(jnp.int32, (TOK, 128), 1) < HEAD_DIM
        factor = HEAD_DIM**-0.5
        g_all = []
        for i in range(PAIR):
            qkv = qkv_in[slot + i]
            scaled = (grad_mixed_in[slot + i].astype(F32) * rinv_in[slot + i]).astype(BF)
            product = scaled.astype(F32) * mixed_in[slot + i].astype(F32)
            g_query, g_key, g_value = [], [], []
            for pair in range(HEADS // 2):
                at = 128 * pair
                query = qkv[:, at : at + 128]
                key = qkv[:, D + at : D + at + 128]
                value = qkv[:, 2 * D + at : 2 * D + at + 128]
                grad = scaled[:, at : at + 128]
                weighed = product[:, at : at + 128]
                parts = []
                for half in range(2):
                    mask = low if half == 0 else ~low
                    chosen = jnp.where(mask, grad, jnp.zeros_like(grad))
                    delta = jnp.sum(jnp.where(mask, weighed, 0.0), axis=-1, keepdims=True)
                    expo = expo_in[slot + i, 2 * pair + half]
                    g_probs = dot_nt(chosen, value)
                    g_scores = (expo.astype(F32) * (g_probs - delta)).astype(BF)
                    parts.append(
                        (dot(g_scores, key), dot_tn(g_scores, query), dot_tn(expo, grad))
                    )
                g_query.append((jnp.where(low, parts[0][0], parts[1][0]) * factor).astype(BF))
                g_key.append((jnp.where(low, parts[0][1], parts[1][1]) * factor).astype(BF))
                g_value.append(jnp.where(low, parts[0][2], parts[1][2]).astype(BF))
            g_all.append(jnp.concatenate(g_query + g_key + g_value, axis=1))
        g_qkv = jnp.concatenate(g_all, axis=0)
        hidden = hidden_in[pl.ds(slot, PAIR)].reshape(PAIR * TOK, D)
        acc_qkv[...] += dot_tn(hidden, g_qkv)
        acc_bias[0:1, :] += jnp.sum(g_qkv.astype(F32), axis=0, keepdims=True)
        d_all = dot_nt(g_qkv, weights[:, :QKV_W])
        for i in range(PAIR):
            row = mod_in[pl.ds(slot + i, 1), :]
            normed, inverse = normalize(latents[i].astype(F32))
            d_hidden = d_all[TOK * i : TOK * i + TOK]
            grad_mod[pl.ds(slot + i, 1), :D] = jnp.sum(d_hidden, axis=0, keepdims=True)
            grad_mod[pl.ds(slot + i, 1), D:] = jnp.sum(d_hidden * normed, axis=0, keepdims=True)
            back = norm_back(d_hidden * (1.0 + row[:, D : 2 * D]), normed, inverse)
            out[i] = (grad_mid_in[slot + i] + back).astype(BF)

    if not last:
        return

    @pl.when(step == STEPS - 1 - first)
    def _():
        cond = conditions[...].astype(F32)
        sig = 1.0 / (1.0 + jnp.exp(-cond))
        cond_low = (cond * sig).astype(BF)
        g_mod = grad_mod[...].astype(BF)
        g_mod_two = grad_mod_two[...].astype(BF)
        g_cond = dot_nt(g_mod, weights[:, QKV_W : QKV_W + MOD_ONE])
        g_cond += dot_nt(g_mod_two, weights_two[:, AT_MOD : AT_MOD + MOD_TWO])
        grad_cond[...] = (g_cond * (sig * (1.0 + cond * (1.0 - sig)))).astype(BF)
        mod_grad = dot_tn(cond_low.astype(F32), g_mod.astype(F32)).astype(BF)
        sums = jnp.sum(g_mod.astype(F32), axis=0, keepdims=True)
        rows = [acc_bias[0:1, 128 * i : 128 * i + 128] for i in range(9)]
        rows += [sums[:, 128 * i : 128 * i + 128] for i in range(6)]
        rows += [jnp.zeros((33, 128), F32)]
        bias_block = jnp.concatenate(rows, axis=0).astype(BF)
        z_high, core, column = info[2], info[3], info[1]
        for owner in range(8):
            zh, xx = owner // 4, owner % 4
            spot = pl.multiple_of(lax.rem(xx - column + 4, 4) * 48, 16)
            is_mine = (z_high ^ core) == zh
            lo = 48 * owner

            def put(ref, spot=spot, lo=lo):
                ref[pl.ds(spot, 48), :QKV_W] = acc_qkv[lo : lo + 48, :].astype(BF)
                ref[pl.ds(spot, 48), QKV_W : QKV_W + MOD_ONE] = mod_grad[lo : lo + 48, :]
                ref[pl.ds(spot, 48), BIAS_ONE : BIAS_ONE + 128] = bias_block

            pl.when(is_mine)(functools.partial(put, keep))
            pl.when(jnp.logical_not(is_mine))(functools.partial(put, send))


def slot_spec(first=0):
    def index(j, info):
        return (jnp.minimum(j + first, jnp.maximum((info[0] + 1) // 2 - 1, 0)), 0, 0)

    return pl.BlockSpec((PAIR, TOK, D), index)


def slot_out(first=0):
    return pl.BlockSpec((PAIR, TOK, D), lambda j, info: (j + first, 0, 0))


def held():
    return pl.BlockSpec(memory_space=pltpu.VMEM)


def whole(*shape):
    zeros = (0,) * len(shape)
    return pl.BlockSpec(shape, lambda j, info: zeros)


def params(mib):
    return pltpu.CompilerParams(
        dimension_semantics=("arbitrary",), vmem_limit_bytes=mib * MIB
    )


def far(value):
    return pltpu.with_memory_space_constraint(value, pltpu.HBM)


def stay(value):
    return pltpu.with_memory_space_constraint(value, pltpu.VMEM)


def run_forward(info, latents, conditions, pieces):
    return pl.pallas_call(
        forward_kernel,
        grid_spec=pltpu.PrefetchScalarGridSpec(
            num_scalar_prefetch=1,
            grid=(STEPS,),
            in_specs=[slot_spec(), whole(CAP, D)] + [held()] * 8,
            out_specs=[held()] * 8,
        ),
        out_shape=[
            pltpu.VMEM((D, LANES_ONE), BF),
            pltpu.VMEM((48, 128), F32),
            pltpu.VMEM((CAP, MOD_ONE), F32),
            pltpu.VMEM((CAP, TOK, QKV_W), BF),
            pltpu.VMEM((CAP, HEADS, TOK, TOK), BF),
            pltpu.VMEM((CAP, TOK, D), BF),
            pltpu.VMEM((CAP, TOK, D), F32),
            pltpu.VMEM((CAP, TOK, D), BF),
        ],
        compiler_params=params(13),
        name="attention_forward",
        cost_estimate=pl.CostEstimate(
            flops=3_000_000_000, bytes_accessed=20_000_000, transcendentals=3_000_000
        ),
    )(info, far(latents), far(conditions), *pieces)


def run_middle(info, latents, conditions, mixed, grad_out, bias, pieces):
    return pl.pallas_call(
        middle_kernel,
        grid_spec=pltpu.PrefetchScalarGridSpec(
            num_scalar_prefetch=1,
            grid=(STEPS,),
            in_specs=[
                slot_spec(),
                whole(CAP, D),
                held(),
                slot_spec(),
                held(),
            ]
            + [held()] * 8,
            out_specs=[held(), slot_out()] + [held()] * 5,
            scratch_shapes=[
                pltpu.VMEM((CAP, MOD_TWO), F32),
                pltpu.VMEM((D, FF), F32),
                pltpu.VMEM((FF, D), F32),
                pltpu.VMEM((D, D), F32),
                pltpu.VMEM((8, FF), F32),
            ],
        ),
        out_shape=[
            pltpu.VMEM((D, LANES_TWO), BF),
            jax.ShapeDtypeStruct((CAP, TOK, D), BF),
            pltpu.VMEM((CAP, TOK, D), F32),
            pltpu.VMEM((CAP, TOK, D), BF),
            pltpu.VMEM((CAP, MOD_TWO), F32),
            pltpu.VMEM((192, LANES_TWO), BF),
            pltpu.VMEM((192, LANES_TWO), BF),
        ],
        compiler_params=params(22),
        name="feed_forward_both_ways",
        cost_estimate=pl.CostEstimate(
            flops=16_000_000_000, bytes_accessed=30_000_000, transcendentals=3_000_000
        ),
    )(info, far(latents), far(conditions), stay(mixed), far(grad_out), stay(bias), *pieces)


def run_backward(first, count, info, latents, shared, carried=None):
    last = carried is not None

    in_specs = [slot_spec(first), whole(CAP, D)] + [held()] * 9
    out_specs = [slot_out(first)]
    out_shape = [jax.ShapeDtypeStruct((CAP, TOK, D), BF)]
    state = [(D, QKV_W), (8, QKV_W), (CAP, MOD_ONE)]
    if last:
        in_specs += [held()] * 5 + [pl.BlockSpec(memory_space=pl.ANY)]
        out_specs += [whole(CAP, D), held(), held()]
        out_shape += [jax.ShapeDtypeStruct((CAP, D), BF)]
        out_shape += [pltpu.VMEM((192, LANES_ONE), BF)] * 2
    else:
        out_specs += [held()] * 3
        out_shape += [pltpu.VMEM(shape, F32) for shape in state]
    return pl.pallas_call(
        functools.partial(backward_kernel, first, last),
        grid_spec=pltpu.PrefetchScalarGridSpec(
            num_scalar_prefetch=1,
            grid=(count,),
            in_specs=in_specs,
            out_specs=out_specs,
            scratch_shapes=[pltpu.VMEM(shape, F32) for shape in state] if last else [],
        ),
        out_shape=out_shape,
        input_output_aliases={17: 0} if last else {},
        compiler_params=params(15),
        name="attention_backward_rest" if last else "attention_backward_start",
        cost_estimate=pl.CostEstimate(
            flops=2_200_000_000 * count, bytes_accessed=8_000_000 * count, transcendentals=1_000
        ),
    )(info, far(latents), far(shared[0]), *map(stay, shared[1:]), *map(stay, (carried or ())[:-1]), *(carried or ())[-1:])


def place(index):
    shard, rep = divmod(index, 16)
    return shard // 4, shard % 4, rep // 4, (rep // 2) % 2, rep % 2


def index_of(z_high, x, y, z_low, core):
    return (z_high * 4 + x) * 16 + y * 4 + z_low * 2 + core


def routes(target_of):
    return [(i, target_of(*place(i))) for i in range(TWIN)]


def fetch(k):
    def source(zh, x, y, zl, c):
        if c == 0:
            return index_of(zh, (x + k) % 4, y, zl, c)
        return index_of(1 - zh, (x + k) % 4, y, 1 - zl, c)

    return [(source(*place(i)), i) for i in range(TWIN)]


CORE_SWAP = routes(lambda zh, x, y, zl, c: index_of(zh, x, y, zl, 1 - c))
ZLOW_SWAP = routes(lambda zh, x, y, zl, c: index_of(zh, x, y, 1 - zl, c))
BOTH = ("shard", "rep")


def move(value, pairs):
    return lax.ppermute(value, BOTH, pairs)


def y_route(k):
    return routes(lambda zh, x, y, zl, c: index_of(zh, x, (y + k) % 4, zl, c))


def after(value, *earlier):
    return lax.optimization_barrier((value, *earlier))[0]


def fetch_all(block):
    return [move(block, fetch(k)) for k in range(4)]


def swap_all(pieces):
    return [move(piece, CORE_SWAP) for piece in pieces]


def small_call(kernel, name, shapes, *values, scalars=False):
    return pl.pallas_call(
        kernel,
        in_specs=[pl.BlockSpec(memory_space=pltpu.SMEM)] * scalars
        + [held()] * (len(values) - scalars),
        out_shape=[jax.ShapeDtypeStruct(shape, BF) for shape in shapes],
        compiler_params=pltpu.CompilerParams(vmem_limit_bytes=14 * MIB),
        name=name,
    )(*values)


def add_kernel(*refs):
    refs[-1][...] = sum(ref[...].astype(F32) for ref in refs[:-1]).astype(BF)


def add(*values):
    return small_call(add_kernel, "add", [values[0].shape], *values)[0]


def add_blocks_kernel(left, right, *outs):
    for k, out in enumerate(outs):
        rows = slice(48 * k, 48 * k + 48)
        out[...] = (left[rows, :].astype(F32) + right[rows, :].astype(F32)).astype(BF)


def add_blocks(left, right):
    shape = (48, left.shape[1])
    return small_call(add_blocks_kernel, "add_blocks", [shape] * 4, left, right)


def add_halves_kernel(info, *refs):
    lanes = refs[-1].shape[1]
    for out, core in ((refs[-2], info[3]), (refs[-1], 1 - info[3])):
        at = pl.ds(pl.multiple_of(core * lanes, 128), lanes)
        out[...] = sum(ref[:, at].astype(F32) for ref in refs[:-2]).astype(BF)


def add_halves(info, pieces):
    shape = (48, pieces[0].shape[1] // 2)
    return small_call(
        add_halves_kernel, "add_halves", [shape] * 2, info, *pieces, scalars=True
    )


def scatter(blocks):
    back = [[(target, source) for source, target in fetch(k)] for k in range(4)]
    return [move(block, pairs) for block, pairs in zip(blocks, back)]


def sum_replicas(arrived, info):
    mine, other = add_halves(info, arrived)
    total = add(mine, move(other, CORE_SWAP))
    total = add(total, move(total, ZLOW_SWAP))
    total = add(total, *(move(total, y_route(k)) for k in (1, 2, 3)))
    return [total, move(total, CORE_SWAP)]


def row_of(ref):
    size = ref.shape[0]
    row = ref[...].astype(F32).reshape(1, size)
    if size % 128:
        row = jnp.concatenate([row, jnp.zeros((1, -size % 128), F32)], axis=1)
    return row


def pack_one_kernel(qkv, mod, qv_bias, mod_bias, proj_bias, up_bias, down_bias, out):
    out[:, :QKV_W] = qkv[...]
    out[:, QKV_W:BIAS_ONE] = mod[:, :MOD_ONE]
    flat = [row_of(ref) for ref in (qv_bias, mod_bias, proj_bias, up_bias, down_bias)]
    flat = jnp.concatenate(flat, axis=1)
    rows = [flat[:, 128 * i : 128 * i + 128] for i in range(8)] + [jnp.zeros((40, 128), F32)]
    out[:, BIAS_ONE:] = jnp.concatenate(rows, axis=0).astype(BF)


def pack_two_kernel(up, mod, proj, down, out):
    out[:, :FF] = up[...]
    out[:, AT_MOD:AT_PROJ] = mod[:, MOD_ONE:]
    out[:, AT_PROJ:AT_DOWN] = proj[...]
    for q in range(4):
        out[:, AT_DOWN + D * q : AT_DOWN + D * q + D] = down[48 * q : 48 * q + 48, :]
    out[:, BIAS_TWO:] = jnp.zeros((48, 128), BF)


def pack(kernel, name, lanes, *values):
    def once(shape):
        return pl.BlockSpec(shape, lambda j: (0,) * len(shape))

    return pl.pallas_call(
        kernel,
        grid=(1,),
        in_specs=[once(value.shape) for value in values],
        out_specs=once((48, lanes)),
        out_shape=pltpu.VMEM((48, lanes), BF),
        compiler_params=pltpu.CompilerParams(vmem_limit_bytes=8 * MIB),
        name=name,
    )(*map(far, values))


def finish_kernel(
    info, one_a, one_b, two_a, two_b, g_mod, g_mod_bias, g_qkv, g_qv_bias, g_proj, g_proj_bias,
    g_up, g_up_bias, g_down, g_down_bias,
):
    shard, first = info[1] + 4 * info[2], info[3] == 0

    def joined(mine, other):
        mine, other = mine[...].astype(F32), other[...].astype(F32)
        return jnp.concatenate(
            [jnp.where(first, mine, other), jnp.where(first, other, mine)], axis=1
        )

    one, two = joined(one_a, one_b), joined(two_a, two_b)
    g_mod[:, :MOD_ONE] = one[:, QKV_W:BIAS_ONE]
    g_mod[:, MOD_ONE:] = two[:, AT_MOD:AT_PROJ]
    g_qkv[...] = one[:, :QKV_W]
    g_proj[...] = two[:, AT_PROJ:AT_DOWN]
    g_up[...] = two[:, :FF]
    for q in range(4):
        g_down[48 * q : 48 * q + 48, :] = two[:, AT_DOWN + D * q : AT_DOWN + D * q + D]
    bias = one[:, BIAS_ONE:] + two[:, BIAS_TWO:]

    def own(first_row, count, size, out):
        row = bias_row(bias, first_row, count)
        row = jnp.broadcast_to(row, (8, 128 * count))
        turn = lax.rem(8 * size - shard * size, 8 * size)
        out[...] = pltpu.roll(row, turn, 1)[0:1, :size].reshape(size)

    own(ROW_MOD, 18, 288, g_mod_bias)
    query, value = bias_row(bias, 0, 3), bias_row(bias, 6, 3)
    row = jnp.broadcast_to(jnp.concatenate([query, value], axis=1), (8, 2 * D))
    turn = lax.rem(2 * D - shard * 96, 2 * D)
    g_qv_bias[...] = pltpu.roll(row, turn, 1)[0:1, :96].reshape(96)
    own(ROW_PROJ, 3, 48, g_proj_bias)
    own(ROW_UP, 12, 192, g_up_bias)
    own(ROW_DOWN, 3, 48, g_down_bias)


def finish(info, parts):
    shapes = [
        (48, 6 * D), (288,), (48, QKV_W), (96,), (48, D), (48,), (48, FF), (192,), (192, D), (48,),
    ]
    return pl.pallas_call(
        finish_kernel,
        in_specs=[pl.BlockSpec(memory_space=pltpu.SMEM)] + [held()] * 4,
        out_shape=[jax.ShapeDtypeStruct(shape, F32) for shape in shapes],
        compiler_params=pltpu.CompilerParams(vmem_limit_bytes=12 * MIB),
        name="unpack_gradients",
    )(info, *parts)


def on_device(
    latents, conditions, counts, mod_weight, mod_bias, qkv_weight, qv_bias, proj_weight,
    proj_bias, up_weight, up_bias, down_weight, down_bias, grad_out,
):
    shard = lax.axis_index("shard")
    rep = lax.axis_index("rep")
    info = jnp.stack([counts[0], shard % 4, shard // 4, rep % 2]).astype(jnp.int32)
    block_one = pack(
        pack_one_kernel, "pack_attention_weights", LANES_ONE,
        after(qkv_weight, info), mod_weight, qv_bias, mod_bias, proj_bias, up_bias, down_bias,
    )
    block_two = pack(
        pack_two_kernel, "pack_feed_forward_weights", LANES_TWO,
        up_weight, mod_weight, proj_weight, down_weight,
    )
    mine_one = fetch_all(block_one)
    other_one = swap_all(mine_one)
    mine_two = [move(block_two, fetch(0))]
    block_two = after(block_two, *other_one)
    mine_two += [move(block_two, fetch(k)) for k in (1, 2, 3)]
    weights, bias, mod, qkv, expo, mixed, rinv, hidden = run_forward(
        info, latents, conditions, mine_one + other_one
    )
    mine_two = [after(piece, mod) for piece in mine_two]
    other_two = swap_all(mine_two)
    weights_two, out, grad_mid, grad_mixed, grad_mod_two, keep_two, send_two = run_middle(
        info, latents, conditions, mixed, grad_out, bias, mine_two + other_two
    )
    swapped_two = move(send_two, CORE_SWAP)
    shared = (
        conditions, qkv, expo, mixed, rinv, hidden, grad_mid, grad_mixed, mod, weights,
    )
    grad_latents, acc_qkv, acc_bias, grad_mod = run_backward(0, 1, info, latents, shared)
    held_two = add_blocks(keep_two, after(swapped_two, acc_bias))
    arrived_two = scatter(held_two)
    grad_latents, grad_cond, keep_one, send_one = run_backward(
        1, 3, info, latents, shared,
        (weights_two, grad_mod_two, acc_qkv, acc_bias, after(grad_mod, held_two[0]), grad_latents),
    )
    held_one = add_blocks(keep_one, move(after(send_one, *arrived_two), CORE_SWAP))
    arrived_one = scatter(held_one)
    two = sum_replicas(arrived_two, info)
    one = sum_replicas(arrived_one, info)
    return (out, grad_latents, grad_cond, *finish(info, one + two))


def solution(mesh):
    slots = P(("shard", "rep"), None, None)
    rows = P(("shard", "rep"), None)
    matrix, vector = P("shard", None), P("shard")
    in_specs = (slots, rows, P(("shard", "rep"))) + (matrix, vector) * 5 + (slots,)
    out_specs = (slots, slots, rows) + (matrix, vector) * 5
    return jax.shard_map(
        on_device, mesh=mesh, in_specs=in_specs, out_specs=out_specs, check_vma=False
    )
```

```python
import functools

import jax
import jax.numpy as jnp
from jax import lax
from jax.experimental import pallas as pl
from jax.experimental.pallas import tpu as pltpu
from jax.sharding import PartitionSpec as P

D = 384
HEADS = 6
HEAD_DIM = 64
FF = 1536
TOK = 256
CAP = 8
PAIR = 2
CHUNK = 768
STEPS = CAP // PAIR
TWIN = 128
BF = jnp.bfloat16
F32 = jnp.float32
MIB = 1024 * 1024

LANES_ONE = 2048
QKV_W = 3 * D
MOD_ONE = 2 * D
BIAS_ONE = QKV_W + MOD_ONE
LANES_TWO = 5120
MOD_TWO = 4 * D
AT_MOD = FF
AT_PROJ = AT_MOD + MOD_TWO
AT_DOWN = AT_PROJ + D
BIAS_TWO = AT_DOWN + FF
ROW_QKV, ROW_MOD, ROW_PROJ, ROW_UP, ROW_DOWN = 0, 9, 27, 30, 42


def dot(left, right):
    return jnp.dot(left, right, preferred_element_type=F32)


def dot_tn(left, right):
    return lax.dot_general(left, right, (((0,), (0,)), ((), ())), preferred_element_type=F32)


def dot_nt(left, right):
    return lax.dot_general(left, right, (((1,), (1,)), ((), ())), preferred_element_type=F32)


def normalize(value):
    center = jnp.mean(value, axis=-1, keepdims=True)
    centered = value - center
    spread = jnp.mean(centered * centered, axis=-1, keepdims=True)
    inverse = lax.rsqrt(spread + 1e-06)
    return centered * inverse, inverse


def norm_back(grad, normed, inverse):
    first = jnp.mean(grad, axis=-1, keepdims=True)
    second = jnp.mean(grad * normed, axis=-1, keepdims=True)
    return inverse * (grad - first - normed * second)


def spread(rows, size):
    width = 8 * size
    lane = lax.broadcasted_iota(jnp.int32, (8, width), 1)
    total = jnp.zeros((8, width), F32)
    for owner, row in enumerate(rows):
        padded = jnp.concatenate([row, jnp.zeros((1, width - row.shape[1]), F32)], axis=1)
        padded = jnp.where(lane < size, jnp.broadcast_to(padded, (8, width)), 0.0)
        total += pltpu.roll(padded, owner * size, 1) if owner else padded
    return total[0:1]


def all_biases(raw):
    def rows(first, count):
        return [
            jnp.concatenate([block[first + i : first + i + 1] for i in range(count)], axis=1)
            for block in raw
        ]

    qv = spread(rows(0, 1), 96)
    full = [qv[:, :D], jnp.zeros((1, D), F32), qv[:, D:]]
    full += [spread(rows(1, 3), 288), spread(rows(4, 1), 48)]
    full += [spread(rows(5, 2), 192), spread(rows(7, 1), 48)]
    full = jnp.concatenate(full, axis=1)
    cut = [full[:, 128 * i : 128 * i + 128] for i in range(45)]
    return jnp.concatenate(cut + [jnp.zeros((3, 128), F32)], axis=0)


def by_head(value, low):
    zero = jnp.zeros_like(value)
    return jnp.concatenate([jnp.where(low, value, zero), jnp.where(low, zero, value)], axis=0)


def bias_row(bias, first, count):
    return jnp.concatenate([bias[first + i : first + i + 1, :] for i in range(count)], axis=1)


def silu(cond):
    return cond * (1.0 / (1.0 + jnp.exp(-cond)))


def assemble(info, pieces, full):
    column, z_high, core = info[1], info[2], info[3]
    for k in range(4):
        spot = lax.rem(column + k, 4) * 48
        mine = (z_high ^ core) * 192 + spot
        other = (1 - (z_high ^ core)) * 192 + spot
        full[pl.ds(pl.multiple_of(mine, 16), 48), :] = pieces[k][...]
        full[pl.ds(pl.multiple_of(other, 16), 48), :] = pieces[4 + k][...]


def forward_kernel(
    info, latents, conditions, p0, p1, p2, p3, p4, p5, p6, p7,
    weights, bias_out, mod_out, qkv_out, expo_out, mixed_out, rinv_out, hidden_out,
):
    step = pl.program_id(0)

    @pl.when(step == 0)
    def _():
        assemble(info, (p0, p1, p2, p3, p4, p5, p6, p7), weights)
        total = all_biases(
            [
                weights[48 * k : 48 * k + 16, BIAS_ONE : BIAS_ONE + 128].astype(F32)[:8]
                for k in range(8)
            ]
        )
        bias_out[...] = total
        cond_low = silu(conditions[...].astype(F32)).astype(BF)
        mod_out[...] = dot(cond_low, weights[:, QKV_W : QKV_W + MOD_ONE]) + bias_row(
            total, ROW_MOD, 6
        )

    @pl.when(PAIR * step < info[0])
    def _():
        hidden = []
        for i in range(PAIR):
            mod = mod_out[pl.ds(PAIR * step + i, 1), :]
            normed, _ = normalize(latents[i].astype(F32))
            hidden.append((normed * (1.0 + mod[:, D : 2 * D]) + mod[:, :D]).astype(BF))
            hidden_out[PAIR * step + i] = hidden[i]
        full_bias = bias_row(bias_out[0:16, :], ROW_QKV, 9)
        qkv_all = dot(jnp.concatenate(hidden, axis=0), weights[:, :QKV_W])
        qkv_all = (qkv_all + full_bias).astype(BF)
        low = lax.broadcasted_iota(jnp.int32, (TOK, 128), 1) < HEAD_DIM
        for i in range(PAIR):
            slot = PAIR * step + i
            qkv = qkv_all[TOK * i : TOK * i + TOK]
            qkv_out[slot] = qkv
            for pair in range(HEADS // 2):
                at = 128 * pair
                query = qkv[:, at : at + 128] * jnp.asarray(HEAD_DIM**-0.5, BF)
                value = qkv[:, 2 * D + at : 2 * D + at + 128]
                scores = dot_nt(query, by_head(qkv[:, D + at : D + at + 128], low))
                expo = jnp.concatenate(
                    [
                        jnp.exp(part - jnp.max(part, axis=-1, keepdims=True)).astype(BF)
                        for part in (scores[:, :TOK], scores[:, TOK:])
                    ],
                    axis=1,
                )
                expo_out[slot, pair] = expo
                sums = by_head(jnp.ones((TOK, 128), BF), low)
                both = dot(expo, jnp.concatenate([by_head(value, low), sums], axis=1))
                inverse = 1.0 / both[:, 128:]
                rinv_out[slot, :, at : at + 128] = inverse
                mixed_out[slot, :, at : at + 128] = (both[:, :128] * inverse).astype(BF)


def middle_kernel(
    info, latents, conditions, mixed_in, grad_out, bias_in, p0, p1, p2, p3, p4, p5, p6, p7,
    weights, out, grad_mid_out, grad_mixed_out, grad_mod, keep, send,
    mod, acc_up, acc_down, acc_proj, acc_bias, down,
):
    step = pl.program_id(0)

    @pl.when(step == 0)
    def _():
        assemble(info, (p0, p1, p2, p3, p4, p5, p6, p7), weights)
        cond_low = silu(conditions[...].astype(F32)).astype(BF)
        mod[...] = dot(cond_low, weights[:, AT_MOD : AT_MOD + MOD_TWO]) + bias_row(
            bias_in[...], ROW_MOD + 6, 12
        )
        for owner in range(8):
            for q in range(4):
                at = 192 * owner + 48 * q
                down[at : at + 48, :] = weights[
                    48 * owner : 48 * owner + 48, AT_DOWN + D * q : AT_DOWN + D * q + D
                ]
        acc_up[...] = jnp.zeros_like(acc_up)
        acc_down[...] = jnp.zeros_like(acc_down)
        acc_proj[...] = jnp.zeros_like(acc_proj)
        acc_bias[...] = jnp.zeros_like(acc_bias)
        grad_mod[...] = jnp.zeros_like(grad_mod)

    @pl.when(PAIR * step >= info[0])
    def _():
        out[...] = jnp.zeros((PAIR, TOK, D), BF)

    @pl.when(PAIR * step < info[0])
    def _():
        bias = bias_in[...]
        w_proj = weights[:, AT_PROJ : AT_PROJ + D]
        up_bias = bias_row(bias, ROW_UP, 12)
        mixed = mixed_in[pl.ds(PAIR * step, PAIR)].reshape(PAIR * TOK, D)
        branch_all = dot(mixed, w_proj) + bias_row(bias, ROW_PROJ, 3)
        rows = [mod[pl.ds(PAIR * step + i, 1), :] for i in range(PAIR)]
        span = [slice(TOK * i, TOK * i + TOK) for i in range(PAIR)]
        middle, normed, inverse, hidden, cot, g_two = [], [], [], [], [], []
        for i in range(PAIR):
            row = rows[i]
            middle.append(latents[i].astype(F32) + row[:, :D] * branch_all[span[i]])
            value, scale = normalize(middle[i])
            normed.append(value)
            inverse.append(scale)
            hidden.append((value * (1.0 + row[:, 2 * D : 3 * D]) + row[:, D : 2 * D]).astype(BF))
            held = (PAIR * step + i < info[0]).astype(F32)
            cot.append(grad_out[i].astype(F32) * held)
            g_two.append((cot[i] * row[:, 3 * D :]).astype(BF))
        hidden = jnp.concatenate(hidden, axis=0)
        g_two = jnp.concatenate(g_two, axis=0)
        branch_two = bias_row(bias, ROW_DOWN, 3)
        d_hidden = jnp.zeros((PAIR * TOK, D), F32)
        root = 0.7978845608028654
        cube = root * 0.044715
        for chunk in range(FF // CHUNK):
            at = CHUNK * chunk
            w_up = weights[:, at : at + CHUNK]
            w_down = down[at : at + CHUNK, :]
            upward = dot(hidden, w_up) + up_bias[:, at : at + CHUNK]
            square = upward * upward
            bend = jnp.tanh(upward * (root + cube * square))
            half = 0.5 + 0.5 * bend
            act = upward * half
            slope = half + act * (1.0 - bend) * (root + (3.0 * cube) * square)
            act_low = act.astype(BF)
            branch_two = branch_two + dot(act_low, w_down)
            acc_down[at : at + CHUNK, :] += dot_tn(act_low, g_two)
            g_up = (slope * dot_nt(g_two, w_down)).astype(BF)
            acc_up[:, at : at + CHUNK] += dot_tn(hidden, g_up)
            acc_bias[0:1, at : at + CHUNK] += jnp.sum(g_up.astype(F32), axis=0, keepdims=True)
            d_hidden = d_hidden + dot_nt(g_up, w_up)
        acc_bias[1:2, :D] += jnp.sum(g_two.astype(F32), axis=0, keepdims=True)
        g_one = []
        for i in range(PAIR):
            row, slot = rows[i], PAIR * step + i
            d_hid, br_two = d_hidden[span[i]], branch_two[span[i]]
            held = (slot < info[0]).astype(F32)
            out[i] = ((middle[i] + row[:, 3 * D :] * br_two) * held).astype(BF)
            grad_mod[pl.ds(slot, 1), 3 * D :] = jnp.sum(cot[i] * br_two, axis=0, keepdims=True)
            grad_mod[pl.ds(slot, 1), D : 2 * D] = jnp.sum(d_hid, axis=0, keepdims=True)
            grad_mod[pl.ds(slot, 1), 2 * D : 3 * D] = jnp.sum(
                d_hid * normed[i], axis=0, keepdims=True
            )
            grad_mid = cot[i] + norm_back(
                d_hid * (1.0 + row[:, 2 * D : 3 * D]), normed[i], inverse[i]
            )
            grad_mid_out[slot] = grad_mid
            grad_mod[pl.ds(slot, 1), :D] = jnp.sum(
                grad_mid * branch_all[span[i]], axis=0, keepdims=True
            )
            g_one.append((grad_mid * row[:, :D]).astype(BF))
        g_one = jnp.concatenate(g_one, axis=0)
        acc_bias[2:3, :D] += jnp.sum(g_one.astype(F32), axis=0, keepdims=True)
        acc_proj[...] += dot_tn(mixed, g_one)
        grad_mixed_out[pl.ds(PAIR * step, PAIR)] = (
            dot_nt(g_one, w_proj).astype(BF).reshape(PAIR, TOK, D)
        )

    @pl.when(step == STEPS - 1)
    def _():
        cond_low = silu(conditions[...].astype(F32)).astype(BF)
        g_mod = grad_mod[...].astype(BF)
        mod_grad = dot_tn(cond_low.astype(F32), g_mod.astype(F32)).astype(BF)
        z_high, core, column = info[2], info[3], info[1]
        sums = jnp.sum(g_mod.astype(F32), axis=0, keepdims=True)
        rows = [jnp.zeros((ROW_MOD + 6, 128), F32)]
        rows += [sums[:, 128 * i : 128 * i + 128] for i in range(12)]
        rows += [acc_bias[2:3, 128 * i : 128 * i + 128] for i in range(3)]
        rows += [acc_bias[0:1, 128 * i : 128 * i + 128] for i in range(12)]
        rows += [acc_bias[1:2, 128 * i : 128 * i + 128] for i in range(3)]
        rows += [jnp.zeros((3, 128), F32)]
        bias_block = jnp.concatenate(rows, axis=0).astype(BF)
        for owner in range(8):
            zh, xx = owner // 4, owner % 4
            spot = lax.rem(xx - column + 4, 4) * 48
            spot = pl.multiple_of(spot, 16)
            is_mine = (z_high ^ core) == zh
            lo = 48 * owner

            def put(ref, spot=spot, lo=lo, owner=owner):
                ref[pl.ds(spot, 48), :FF] = acc_up[lo : lo + 48, :].astype(BF)
                ref[pl.ds(spot, 48), AT_MOD : AT_MOD + MOD_TWO] = mod_grad[lo : lo + 48, :]
                ref[pl.ds(spot, 48), AT_PROJ : AT_PROJ + D] = acc_proj[lo : lo + 48, :].astype(BF)
                for q in range(4):
                    at = 192 * owner + 48 * q
                    ref[pl.ds(spot, 48), AT_DOWN + D * q : AT_DOWN + D * q + D] = acc_down[
                        at : at + 48, :
                    ].astype(BF)
                ref[pl.ds(spot, 48), BIAS_TWO : BIAS_TWO + 128] = bias_block

            pl.when(is_mine)(functools.partial(put, keep))
            pl.when(jnp.logical_not(is_mine))(functools.partial(put, send))


def backward_kernel(
    first, last,
    info, latents, conditions, qkv_in, expo_in, mixed_in, rinv_in, hidden_in, grad_mid_in,
    grad_mixed_in, mod_in, weights, *refs,
):
    if last:
        weights_two, grad_mod_two, acc_in, bias_in, grad_mod_in, _, out, grad_cond, keep, send = refs[:10]
        acc_qkv, acc_bias, grad_mod = refs[10:]
    else:
        out, acc_qkv, acc_bias, grad_mod = refs
    step = pl.program_id(0)
    slot = PAIR * (step + first)

    @pl.when(step == 0)
    def _():
        if last:
            acc_qkv[...] = acc_in[...]
            acc_bias[...] = bias_in[...]
            grad_mod[...] = grad_mod_in[...]
        else:
            acc_qkv[...] = jnp.zeros_like(acc_qkv)
            acc_bias[...] = jnp.zeros_like(acc_bias)
            grad_mod[...] = jnp.zeros_like(grad_mod)

    @pl.when(slot >= info[0])
    def _():
        out[...] = jnp.zeros((PAIR, TOK, D), BF)

    @pl.when(slot < info[0])
    def _():
        low = lax.broadcasted_iota(jnp.int32, (TOK, 128), 1) < HEAD_DIM
        factor = HEAD_DIM**-0.5
        g_all = []
        for i in range(PAIR):
            qkv = qkv_in[slot + i]
            scaled = (grad_mixed_in[slot + i].astype(F32) * rinv_in[slot + i]).astype(BF)
            product = scaled.astype(F32) * mixed_in[slot + i].astype(F32)
            g_query, g_key, g_value = [], [], []
            for pair in range(HEADS // 2):
                at = 128 * pair
                query = qkv[:, at : at + 128]
                key = by_head(qkv[:, D + at : D + at + 128], low)
                value = by_head(qkv[:, 2 * D + at : 2 * D + at + 128], low)
                grad = scaled[:, at : at + 128]
                weighed = product[:, at : at + 128]
                expo = expo_in[slot + i, pair]
                g_probs = dot_nt(grad, value)
                g_scores = []
                for half in range(2):
                    mask = low if half == 0 else ~low
                    delta = jnp.sum(jnp.where(mask, weighed, 0.0), axis=-1, keepdims=True)
                    lanes = slice(TOK * half, TOK * half + TOK)
                    g_scores.append(
                        (expo[:, lanes].astype(F32) * (g_probs[:, lanes] - delta)).astype(BF)
                    )
                g_scores = jnp.concatenate(g_scores, axis=1)
                d_key, d_value = dot_tn(g_scores, query), dot_tn(expo, grad)
                g_query.append((dot(g_scores, key) * factor).astype(BF))
                g_key.append((jnp.where(low, d_key[:TOK], d_key[TOK:]) * factor).astype(BF))
                g_value.append(jnp.where(low, d_value[:TOK], d_value[TOK:]).astype(BF))
            g_all.append(jnp.concatenate(g_query + g_key + g_value, axis=1))
        g_qkv = jnp.concatenate(g_all, axis=0)
        hidden = hidden_in[pl.ds(slot, PAIR)].reshape(PAIR * TOK, D)
        acc_qkv[...] += dot_tn(hidden, g_qkv)
        acc_bias[0:1, :] += jnp.sum(g_qkv.astype(F32), axis=0, keepdims=True)
        d_all = dot_nt(g_qkv, weights[:, :QKV_W])
        for i in range(PAIR):
            row = mod_in[pl.ds(slot + i, 1), :]
            normed, inverse = normalize(latents[i].astype(F32))
            d_hidden = d_all[TOK * i : TOK * i + TOK]
            grad_mod[pl.ds(slot + i, 1), :D] = jnp.sum(d_hidden, axis=0, keepdims=True)
            grad_mod[pl.ds(slot + i, 1), D:] = jnp.sum(d_hidden * normed, axis=0, keepdims=True)
            back = norm_back(d_hidden * (1.0 + row[:, D : 2 * D]), normed, inverse)
            out[i] = (grad_mid_in[slot + i] + back).astype(BF)

    if not last:
        return

    @pl.when(step == STEPS - 1 - first)
    def _():
        cond = conditions[...].astype(F32)
        sig = 1.0 / (1.0 + jnp.exp(-cond))
        cond_low = (cond * sig).astype(BF)
        g_mod = grad_mod[...].astype(BF)
        g_mod_two = grad_mod_two[...].astype(BF)
        g_cond = dot_nt(g_mod, weights[:, QKV_W : QKV_W + MOD_ONE])
        g_cond += dot_nt(g_mod_two, weights_two[:, AT_MOD : AT_MOD + MOD_TWO])
        grad_cond[...] = (g_cond * (sig * (1.0 + cond * (1.0 - sig)))).astype(BF)
        mod_grad = dot_tn(cond_low.astype(F32), g_mod.astype(F32)).astype(BF)
        sums = jnp.sum(g_mod.astype(F32), axis=0, keepdims=True)
        rows = [acc_bias[0:1, 128 * i : 128 * i + 128] for i in range(9)]
        rows += [sums[:, 128 * i : 128 * i + 128] for i in range(6)]
        rows += [jnp.zeros((33, 128), F32)]
        bias_block = jnp.concatenate(rows, axis=0).astype(BF)
        z_high, core, column = info[2], info[3], info[1]
        for owner in range(8):
            zh, xx = owner // 4, owner % 4
            spot = pl.multiple_of(lax.rem(xx - column + 4, 4) * 48, 16)
            is_mine = (z_high ^ core) == zh
            lo = 48 * owner

            def put(ref, spot=spot, lo=lo):
                ref[pl.ds(spot, 48), :QKV_W] = acc_qkv[lo : lo + 48, :].astype(BF)
                ref[pl.ds(spot, 48), QKV_W : QKV_W + MOD_ONE] = mod_grad[lo : lo + 48, :]
                ref[pl.ds(spot, 48), BIAS_ONE : BIAS_ONE + 128] = bias_block

            pl.when(is_mine)(functools.partial(put, keep))
            pl.when(jnp.logical_not(is_mine))(functools.partial(put, send))


def slot_spec(first=0):
    def index(j, info):
        return (jnp.minimum(j + first, jnp.maximum((info[0] + 1) // 2 - 1, 0)), 0, 0)

    return pl.BlockSpec((PAIR, TOK, D), index)


def slot_out(first=0):
    return pl.BlockSpec((PAIR, TOK, D), lambda j, info: (j + first, 0, 0))


def held():
    return pl.BlockSpec(memory_space=pltpu.VMEM)


def whole(*shape):
    zeros = (0,) * len(shape)
    return pl.BlockSpec(shape, lambda j, info: zeros)


def params(mib):
    return pltpu.CompilerParams(
        dimension_semantics=("arbitrary",), vmem_limit_bytes=mib * MIB
    )


def far(value):
    return pltpu.with_memory_space_constraint(value, pltpu.HBM)


def stay(value):
    return pltpu.with_memory_space_constraint(value, pltpu.VMEM)


def run_forward(info, latents, conditions, pieces):
    return pl.pallas_call(
        forward_kernel,
        grid_spec=pltpu.PrefetchScalarGridSpec(
            num_scalar_prefetch=1,
            grid=(STEPS,),
            in_specs=[slot_spec(), whole(CAP, D)] + [held()] * 8,
            out_specs=[held()] * 8,
        ),
        out_shape=[
            pltpu.VMEM((D, LANES_ONE), BF),
            pltpu.VMEM((48, 128), F32),
            pltpu.VMEM((CAP, MOD_ONE), F32),
            pltpu.VMEM((CAP, TOK, QKV_W), BF),
            pltpu.VMEM((CAP, HEADS // 2, TOK, 2 * TOK), BF),
            pltpu.VMEM((CAP, TOK, D), BF),
            pltpu.VMEM((CAP, TOK, D), F32),
            pltpu.VMEM((CAP, TOK, D), BF),
        ],
        compiler_params=params(10),
        name="attention_forward",
        cost_estimate=pl.CostEstimate(
            flops=3_000_000_000, bytes_accessed=20_000_000, transcendentals=3_000_000
        ),
    )(info, far(latents), far(conditions), *pieces)


def run_middle(info, latents, conditions, mixed, grad_out, bias, pieces):
    return pl.pallas_call(
        middle_kernel,
        grid_spec=pltpu.PrefetchScalarGridSpec(
            num_scalar_prefetch=1,
            grid=(STEPS,),
            in_specs=[
                slot_spec(),
                whole(CAP, D),
                held(),
                slot_spec(),
                held(),
            ]
            + [held()] * 8,
            out_specs=[held(), slot_out()] + [held()] * 5,
            scratch_shapes=[
                pltpu.VMEM((CAP, MOD_TWO), F32),
                pltpu.VMEM((D, FF), F32),
                pltpu.VMEM((FF, D), F32),
                pltpu.VMEM((D, D), F32),
                pltpu.VMEM((8, FF), F32),
                pltpu.VMEM((FF, D), BF),
            ],
        ),
        out_shape=[
            pltpu.VMEM((D, LANES_TWO), BF),
            jax.ShapeDtypeStruct((CAP, TOK, D), BF),
            pltpu.VMEM((CAP, TOK, D), F32),
            pltpu.VMEM((CAP, TOK, D), BF),
            pltpu.VMEM((CAP, MOD_TWO), F32),
            pltpu.VMEM((192, LANES_TWO), BF),
            pltpu.VMEM((192, LANES_TWO), BF),
        ],
        compiler_params=params(23),
        name="feed_forward_both_ways",
        cost_estimate=pl.CostEstimate(
            flops=16_000_000_000, bytes_accessed=30_000_000, transcendentals=3_000_000
        ),
    )(info, far(latents), far(conditions), stay(mixed), far(grad_out), stay(bias), *pieces)


def run_backward(first, count, info, latents, shared, carried=None):
    last = carried is not None

    in_specs = [slot_spec(first), whole(CAP, D)] + [held()] * 9
    out_specs = [slot_out(first)]
    out_shape = [jax.ShapeDtypeStruct((CAP, TOK, D), BF)]
    state = [(D, QKV_W), (8, QKV_W), (CAP, MOD_ONE)]
    if last:
        in_specs += [held()] * 5 + [pl.BlockSpec(memory_space=pl.ANY)]
        out_specs += [whole(CAP, D), held(), held()]
        out_shape += [jax.ShapeDtypeStruct((CAP, D), BF)]
        out_shape += [pltpu.VMEM((192, LANES_ONE), BF)] * 2
    else:
        out_specs += [held()] * 3
        out_shape += [pltpu.VMEM(shape, F32) for shape in state]
    return pl.pallas_call(
        functools.partial(backward_kernel, first, last),
        grid_spec=pltpu.PrefetchScalarGridSpec(
            num_scalar_prefetch=1,
            grid=(count,),
            in_specs=in_specs,
            out_specs=out_specs,
            scratch_shapes=[pltpu.VMEM(shape, F32) for shape in state] if last else [],
        ),
        out_shape=out_shape,
        input_output_aliases={17: 0} if last else {},
        compiler_params=params(10),
        name="attention_backward_rest" if last else "attention_backward_start",
        cost_estimate=pl.CostEstimate(
            flops=2_200_000_000 * count, bytes_accessed=8_000_000 * count, transcendentals=1_000
        ),
    )(info, far(latents), far(shared[0]), *map(stay, shared[1:]), *map(stay, (carried or ())[:-1]), *(carried or ())[-1:])


def place(index):
    shard, rep = divmod(index, 16)
    return shard // 4, shard % 4, rep // 4, (rep // 2) % 2, rep % 2


def index_of(z_high, x, y, z_low, core):
    return (z_high * 4 + x) * 16 + y * 4 + z_low * 2 + core


def routes(target_of):
    return [(i, target_of(*place(i))) for i in range(TWIN)]


def fetch(k):
    def source(zh, x, y, zl, c):
        if c == 0:
            return index_of(zh, (x + k) % 4, y, zl, c)
        return index_of(1 - zh, (x + k) % 4, y, 1 - zl, c)

    return [(source(*place(i)), i) for i in range(TWIN)]


CORE_SWAP = routes(lambda zh, x, y, zl, c: index_of(zh, x, y, zl, 1 - c))
ZLOW_SWAP = routes(lambda zh, x, y, zl, c: index_of(zh, x, y, 1 - zl, c))
BOTH = ("shard", "rep")


def move(value, pairs):
    return lax.ppermute(value, BOTH, pairs)


def y_route(k):
    return routes(lambda zh, x, y, zl, c: index_of(zh, x, (y + k) % 4, zl, c))


def after(value, *earlier):
    return lax.optimization_barrier((value, *earlier))[0]


def fetch_all(block):
    return [move(block, fetch(k)) for k in range(4)]


def swap_all(pieces):
    return [move(piece, CORE_SWAP) for piece in pieces]


def small_call(kernel, name, shapes, *values, scalars=False):
    return pl.pallas_call(
        kernel,
        in_specs=[pl.BlockSpec(memory_space=pltpu.SMEM)] * scalars
        + [held()] * (len(values) - scalars),
        out_shape=[jax.ShapeDtypeStruct(shape, BF) for shape in shapes],
        compiler_params=pltpu.CompilerParams(vmem_limit_bytes=14 * MIB),
        name=name,
    )(*values)


def add_kernel(*refs):
    refs[-1][...] = sum(ref[...].astype(F32) for ref in refs[:-1]).astype(BF)


def add(*values):
    return small_call(add_kernel, "add", [values[0].shape], *values)[0]


def add_blocks_kernel(left, right, *outs):
    for k, out in enumerate(outs):
        rows = slice(48 * k, 48 * k + 48)
        out[...] = (left[rows, :].astype(F32) + right[rows, :].astype(F32)).astype(BF)


def add_blocks(left, right):
    shape = (48, left.shape[1])
    return small_call(add_blocks_kernel, "add_blocks", [shape] * 4, left, right)


def add_halves_kernel(info, *refs):
    lanes = refs[-1].shape[1]
    for out, core in ((refs[-2], info[3]), (refs[-1], 1 - info[3])):
        at = pl.ds(pl.multiple_of(core * lanes, 128), lanes)
        out[...] = sum(ref[:, at].astype(F32) for ref in refs[:-2]).astype(BF)


def add_halves(info, pieces):
    shape = (48, pieces[0].shape[1] // 2)
    return small_call(
        add_halves_kernel, "add_halves", [shape] * 2, info, *pieces, scalars=True
    )


def scatter(blocks):
    back = [[(target, source) for source, target in fetch(k)] for k in range(4)]
    return [move(block, pairs) for block, pairs in zip(blocks, back)]


def sum_replicas(arrived, info):
    mine, other = add_halves(info, arrived)
    total = add(mine, move(other, CORE_SWAP))
    total = add(total, move(total, ZLOW_SWAP))
    total = add(total, *(move(total, y_route(k)) for k in (1, 2, 3)))
    return [total, move(total, CORE_SWAP)]


def row_of(ref):
    size = ref.shape[0]
    row = ref[...].astype(F32).reshape(1, size)
    if size % 128:
        row = jnp.concatenate([row, jnp.zeros((1, -size % 128), F32)], axis=1)
    return row


def pack_one_kernel(qkv, mod, qv_bias, mod_bias, proj_bias, up_bias, down_bias, out):
    out[:, :QKV_W] = qkv[...]
    out[:, QKV_W:BIAS_ONE] = mod[:, :MOD_ONE]
    flat = [row_of(ref) for ref in (qv_bias, mod_bias, proj_bias, up_bias, down_bias)]
    flat = jnp.concatenate(flat, axis=1)
    rows = [flat[:, 128 * i : 128 * i + 128] for i in range(8)] + [jnp.zeros((40, 128), F32)]
    out[:, BIAS_ONE:] = jnp.concatenate(rows, axis=0).astype(BF)


def pack_two_kernel(up, mod, proj, down, out):
    out[:, :FF] = up[...]
    out[:, AT_MOD:AT_PROJ] = mod[:, MOD_ONE:]
    out[:, AT_PROJ:AT_DOWN] = proj[...]
    for q in range(4):
        out[:, AT_DOWN + D * q : AT_DOWN + D * q + D] = down[48 * q : 48 * q + 48, :]
    out[:, BIAS_TWO:] = jnp.zeros((48, 128), BF)


def pack(kernel, name, lanes, *values):
    def once(shape):
        return pl.BlockSpec(shape, lambda j: (0,) * len(shape))

    return pl.pallas_call(
        kernel,
        grid=(1,),
        in_specs=[once(value.shape) for value in values],
        out_specs=once((48, lanes)),
        out_shape=pltpu.VMEM((48, lanes), BF),
        compiler_params=pltpu.CompilerParams(vmem_limit_bytes=8 * MIB),
        name=name,
    )(*map(far, values))


def finish_kernel(
    info, one_a, one_b, two_a, two_b, g_mod, g_mod_bias, g_qkv, g_qv_bias, g_proj, g_proj_bias,
    g_up, g_up_bias, g_down, g_down_bias,
):
    shard, first = info[1] + 4 * info[2], info[3] == 0

    def joined(mine, other):
        mine, other = mine[...].astype(F32), other[...].astype(F32)
        return jnp.concatenate(
            [jnp.where(first, mine, other), jnp.where(first, other, mine)], axis=1
        )

    one, two = joined(one_a, one_b), joined(two_a, two_b)
    g_mod[:, :MOD_ONE] = one[:, QKV_W:BIAS_ONE]
    g_mod[:, MOD_ONE:] = two[:, AT_MOD:AT_PROJ]
    g_qkv[...] = one[:, :QKV_W]
    g_proj[...] = two[:, AT_PROJ:AT_DOWN]
    g_up[...] = two[:, :FF]
    for q in range(4):
        g_down[48 * q : 48 * q + 48, :] = two[:, AT_DOWN + D * q : AT_DOWN + D * q + D]
    bias = one[:, BIAS_ONE:] + two[:, BIAS_TWO:]

    def own(first_row, count, size, out):
        row = bias_row(bias, first_row, count)
        row = jnp.broadcast_to(row, (8, 128 * count))
        turn = lax.rem(8 * size - shard * size, 8 * size)
        out[...] = pltpu.roll(row, turn, 1)[0:1, :size].reshape(size)

    own(ROW_MOD, 18, 288, g_mod_bias)
    query, value = bias_row(bias, 0, 3), bias_row(bias, 6, 3)
    row = jnp.broadcast_to(jnp.concatenate([query, value], axis=1), (8, 2 * D))
    turn = lax.rem(2 * D - shard * 96, 2 * D)
    g_qv_bias[...] = pltpu.roll(row, turn, 1)[0:1, :96].reshape(96)
    own(ROW_PROJ, 3, 48, g_proj_bias)
    own(ROW_UP, 12, 192, g_up_bias)
    own(ROW_DOWN, 3, 48, g_down_bias)


def finish(info, parts):
    shapes = [
        (48, 6 * D), (288,), (48, QKV_W), (96,), (48, D), (48,), (48, FF), (192,), (192, D), (48,),
    ]
    return pl.pallas_call(
        finish_kernel,
        in_specs=[pl.BlockSpec(memory_space=pltpu.SMEM)] + [held()] * 4,
        out_shape=[jax.ShapeDtypeStruct(shape, F32) for shape in shapes],
        compiler_params=pltpu.CompilerParams(vmem_limit_bytes=12 * MIB),
        name="unpack_gradients",
    )(info, *parts)


def on_device(
    latents, conditions, counts, mod_weight, mod_bias, qkv_weight, qv_bias, proj_weight,
    proj_bias, up_weight, up_bias, down_weight, down_bias, grad_out,
):
    shard = lax.axis_index("shard")
    rep = lax.axis_index("rep")
    info = jnp.stack([counts[0], shard % 4, shard // 4, rep % 2]).astype(jnp.int32)
    block_one = pack(
        pack_one_kernel, "pack_attention_weights", LANES_ONE,
        after(qkv_weight, info), mod_weight, qv_bias, mod_bias, proj_bias, up_bias, down_bias,
    )
    block_two = pack(
        pack_two_kernel, "pack_feed_forward_weights", LANES_TWO,
        up_weight, mod_weight, proj_weight, down_weight,
    )
    mine_one = fetch_all(block_one)
    mine_two = [move(block_two, fetch(0))]
    other_one = swap_all([mine_one[0]] + [after(piece, block_two) for piece in mine_one[1:]])
    block_two = after(block_two, *mine_one)
    mine_two += [move(block_two, fetch(k)) for k in (1, 2, 3)]
    weights, bias, mod, qkv, expo, mixed, rinv, hidden = run_forward(
        info, latents, conditions, mine_one + other_one
    )
    mine_two = [after(piece, mod) for piece in mine_two]
    other_two = swap_all(mine_two)
    weights_two, out, grad_mid, grad_mixed, grad_mod_two, keep_two, send_two = run_middle(
        info, latents, conditions, mixed, grad_out, bias, mine_two + other_two
    )
    swapped_two = move(send_two, CORE_SWAP)
    shared = (
        conditions, qkv, expo, mixed, rinv, hidden, grad_mid, grad_mixed, mod, weights,
    )
    grad_latents, acc_qkv, acc_bias, grad_mod = run_backward(0, 1, info, latents, shared)
    held_two = add_blocks(keep_two, after(swapped_two, acc_bias))
    arrived_two = scatter(held_two)
    grad_latents, grad_cond, keep_one, send_one = run_backward(
        1, 3, info, latents, shared,
        (weights_two, grad_mod_two, acc_qkv, acc_bias, after(grad_mod, held_two[0]), grad_latents),
    )
    held_one = add_blocks(keep_one, move(after(send_one, *arrived_two), CORE_SWAP))
    arrived_one = scatter(held_one)
    two = sum_replicas(arrived_two, info)
    one = sum_replicas(arrived_one, info)
    return (out, grad_latents, grad_cond, *finish(info, one + two))


def solution(mesh):
    slots = P(("shard", "rep"), None, None)
    rows = P(("shard", "rep"), None)
    matrix, vector = P("shard", None), P("shard")
    in_specs = (slots, rows, P(("shard", "rep"))) + (matrix, vector) * 5 + (slots,)
    out_specs = (slots, slots, rows) + (matrix, vector) * 5
    return jax.shard_map(
        on_device, mesh=mesh, in_specs=in_specs, out_specs=out_specs, check_vma=False
    )
```

```python
import functools

import jax
import jax.numpy as jnp
from jax import lax
from jax.experimental import pallas as pl
from jax.experimental.pallas import tpu as pltpu
from jax.sharding import PartitionSpec as P

D = 384
HEADS = 6
HEAD_DIM = 64
FF = 1536
TOK = 256
CAP = 8
PAIR = 2
CHUNK = 768
STEPS = CAP // PAIR
TWIN = 128
BF = jnp.bfloat16
F32 = jnp.float32
MIB = 1024 * 1024

LANES_ONE = 2048
QKV_W = 3 * D
MOD_ONE = 2 * D
BIAS_ONE = QKV_W + MOD_ONE
LANES_TWO = 5120
MOD_TWO = 4 * D
AT_MOD = FF
AT_PROJ = AT_MOD + MOD_TWO
AT_DOWN = AT_PROJ + D
BIAS_TWO = AT_DOWN + FF
ROW_QKV, ROW_MOD, ROW_PROJ, ROW_UP, ROW_DOWN = 0, 9, 27, 30, 42


def dot(left, right):
    return jnp.dot(left, right, preferred_element_type=F32)


def dot_tn(left, right):
    return lax.dot_general(left, right, (((0,), (0,)), ((), ())), preferred_element_type=F32)


def dot_nt(left, right):
    return lax.dot_general(left, right, (((1,), (1,)), ((), ())), preferred_element_type=F32)


def normalize(value):
    center = jnp.mean(value, axis=-1, keepdims=True)
    centered = value - center
    spread = jnp.mean(centered * centered, axis=-1, keepdims=True)
    inverse = lax.rsqrt(spread + 1e-06)
    return centered * inverse, inverse


def norm_back(grad, normed, inverse):
    first = jnp.mean(grad, axis=-1, keepdims=True)
    second = jnp.mean(grad * normed, axis=-1, keepdims=True)
    return inverse * (grad - first - normed * second)


def spread(rows, size):
    width = 8 * size
    lane = lax.broadcasted_iota(jnp.int32, (8, width), 1)
    total = jnp.zeros((8, width), F32)
    for owner, row in enumerate(rows):
        padded = jnp.concatenate([row, jnp.zeros((1, width - row.shape[1]), F32)], axis=1)
        padded = jnp.where(lane < size, jnp.broadcast_to(padded, (8, width)), 0.0)
        total += pltpu.roll(padded, owner * size, 1) if owner else padded
    return total[0:1]


def all_biases(raw):
    def rows(first, count):
        return [
            jnp.concatenate([block[first + i : first + i + 1] for i in range(count)], axis=1)
            for block in raw
        ]

    qv = spread(rows(0, 1), 96)
    full = [qv[:, :D], jnp.zeros((1, D), F32), qv[:, D:]]
    full += [spread(rows(1, 3), 288), spread(rows(4, 1), 48)]
    full += [spread(rows(5, 2), 192), spread(rows(7, 1), 48)]
    full = jnp.concatenate(full, axis=1)
    cut = [full[:, 128 * i : 128 * i + 128] for i in range(45)]
    return jnp.concatenate(cut + [jnp.zeros((3, 128), F32)], axis=0)


def by_head(value, low):
    zero = jnp.zeros_like(value)
    return jnp.concatenate([jnp.where(low, value, zero), jnp.where(low, zero, value)], axis=0)


def bias_row(bias, first, count):
    return jnp.concatenate([bias[first + i : first + i + 1, :] for i in range(count)], axis=1)


def silu(cond):
    return cond * (1.0 / (1.0 + jnp.exp(-cond)))


def assemble(info, pieces, full):
    column, z_high, core = info[1], info[2], info[3]
    for k in range(4):
        spot = lax.rem(column + k, 4) * 48
        mine = (z_high ^ core) * 192 + spot
        other = (1 - (z_high ^ core)) * 192 + spot
        full[pl.ds(pl.multiple_of(mine, 16), 48), :] = pieces[k][...]
        full[pl.ds(pl.multiple_of(other, 16), 48), :] = pieces[4 + k][...]


def forward_kernel(
    info, latents, conditions, p0, p1, p2, p3, p4, p5, p6, p7,
    weights, bias_out, mod_out, qkv_out, expo_out, mixed_out, rinv_out, hidden_out,
):
    step = pl.program_id(0)

    @pl.when(step == 0)
    def _():
        assemble(info, (p0, p1, p2, p3, p4, p5, p6, p7), weights)
        total = all_biases(
            [
                weights[48 * k : 48 * k + 16, BIAS_ONE : BIAS_ONE + 128].astype(F32)[:8]
                for k in range(8)
            ]
        )
        bias_out[...] = total
        cond_low = silu(conditions[...].astype(F32)).astype(BF)
        mod_out[...] = dot(cond_low, weights[:, QKV_W : QKV_W + MOD_ONE]) + bias_row(
            total, ROW_MOD, 6
        )

    @pl.when(PAIR * step < info[0])
    def _():
        hidden = []
        for i in range(PAIR):
            mod = mod_out[pl.ds(PAIR * step + i, 1), :]
            normed, _ = normalize(latents[i].astype(F32))
            hidden.append((normed * (1.0 + mod[:, D : 2 * D]) + mod[:, :D]).astype(BF))
            hidden_out[PAIR * step + i] = hidden[i]
        full_bias = bias_row(bias_out[0:16, :], ROW_QKV, 9)
        qkv_all = dot(jnp.concatenate(hidden, axis=0), weights[:, :QKV_W])
        qkv_all = (qkv_all + full_bias).astype(BF)
        low = lax.broadcasted_iota(jnp.int32, (TOK, 128), 1) < HEAD_DIM
        for i in range(PAIR):
            slot = PAIR * step + i
            qkv = qkv_all[TOK * i : TOK * i + TOK]
            qkv_out[slot] = qkv
            for pair in range(HEADS // 2):
                at = 128 * pair
                query = qkv[:, at : at + 128] * jnp.asarray(HEAD_DIM**-0.5, BF)
                value = qkv[:, 2 * D + at : 2 * D + at + 128]
                scores = dot_nt(query, by_head(qkv[:, D + at : D + at + 128], low))
                expo = jnp.concatenate(
                    [
                        jnp.exp(part - jnp.max(part, axis=-1, keepdims=True)).astype(BF)
                        for part in (scores[:, :TOK], scores[:, TOK:])
                    ],
                    axis=1,
                )
                expo_out[slot, pair] = expo
                sums = by_head(jnp.ones((TOK, 128), BF), low)
                both = dot(expo, jnp.concatenate([by_head(value, low), sums], axis=1))
                inverse = 1.0 / both[:, 128:]
                rinv_out[slot, :, at : at + 128] = inverse
                mixed_out[slot, :, at : at + 128] = (both[:, :128] * inverse).astype(BF)


def middle_kernel(
    info, latents, conditions, mixed_in, grad_out, bias_in, p0, p1, p2, p3, p4, p5, p6, p7,
    weights, out, grad_mid_out, grad_mixed_out, grad_mod, keep, send,
    mod, acc_up, acc_down, acc_proj, acc_bias, down,
):
    step = pl.program_id(0)

    @pl.when(step == 0)
    def _():
        assemble(info, (p0, p1, p2, p3, p4, p5, p6, p7), weights)
        cond_low = silu(conditions[...].astype(F32)).astype(BF)
        mod[...] = dot(cond_low, weights[:, AT_MOD : AT_MOD + MOD_TWO]) + bias_row(
            bias_in[...], ROW_MOD + 6, 12
        )
        for owner in range(8):
            for q in range(4):
                at = 192 * owner + 48 * q
                down[at : at + 48, :] = weights[
                    48 * owner : 48 * owner + 48, AT_DOWN + D * q : AT_DOWN + D * q + D
                ]
        acc_up[...] = jnp.zeros_like(acc_up)
        acc_down[...] = jnp.zeros_like(acc_down)
        acc_proj[...] = jnp.zeros_like(acc_proj)
        acc_bias[...] = jnp.zeros_like(acc_bias)
        grad_mod[...] = jnp.zeros_like(grad_mod)

    @pl.when(PAIR * step >= info[0])
    def _():
        out[...] = jnp.zeros((PAIR, TOK, D), BF)

    @pl.when(PAIR * step < info[0])
    def _():
        bias = bias_in[...]
        w_proj = weights[:, AT_PROJ : AT_PROJ + D]
        up_bias = bias_row(bias, ROW_UP, 12)
        mixed = mixed_in[pl.ds(PAIR * step, PAIR)].reshape(PAIR * TOK, D)
        branch_all = dot(mixed, w_proj) + bias_row(bias, ROW_PROJ, 3)
        rows = [mod[pl.ds(PAIR * step + i, 1), :] for i in range(PAIR)]
        span = [slice(TOK * i, TOK * i + TOK) for i in range(PAIR)]
        middle, normed, inverse, hidden, cot, g_two = [], [], [], [], [], []
        for i in range(PAIR):
            row = rows[i]
            middle.append(latents[i].astype(F32) + row[:, :D] * branch_all[span[i]])
            value, scale = normalize(middle[i])
            normed.append(value)
            inverse.append(scale)
            hidden.append((value * (1.0 + row[:, 2 * D : 3 * D]) + row[:, D : 2 * D]).astype(BF))
            held = (PAIR * step + i < info[0]).astype(F32)
            cot.append(grad_out[i].astype(F32) * held)
            g_two.append((cot[i] * row[:, 3 * D :]).astype(BF))
        hidden = jnp.concatenate(hidden, axis=0)
        g_two = jnp.concatenate(g_two, axis=0)
        branch_two = bias_row(bias, ROW_DOWN, 3)
        d_hidden = jnp.zeros((PAIR * TOK, D), F32)
        root = 0.7978845608028654
        cube = root * 0.044715
        for chunk in range(FF // CHUNK):
            at = CHUNK * chunk
            w_up = weights[:, at : at + CHUNK]
            w_down = down[at : at + CHUNK, :]
            upward = dot(hidden, w_up) + up_bias[:, at : at + CHUNK]
            square = upward * upward
            bend = jnp.tanh(upward * (root + cube * square))
            half = 0.5 + 0.5 * bend
            act = upward * half
            slope = half + act * (1.0 - bend) * (root + (3.0 * cube) * square)
            act_low = act.astype(BF)
            branch_two = branch_two + dot(act_low, w_down)
            acc_down[at : at + CHUNK, :] += dot_tn(act_low, g_two)
            g_up = (slope * dot_nt(g_two, w_down)).astype(BF)
            acc_up[:, at : at + CHUNK] += dot_tn(hidden, g_up)
            acc_bias[0:1, at : at + CHUNK] += jnp.sum(g_up.astype(F32), axis=0, keepdims=True)
            d_hidden = d_hidden + dot_nt(g_up, w_up)
        acc_bias[1:2, :D] += jnp.sum(g_two.astype(F32), axis=0, keepdims=True)
        g_one = []
        for i in range(PAIR):
            row, slot = rows[i], PAIR * step + i
            d_hid, br_two = d_hidden[span[i]], branch_two[span[i]]
            held = (slot < info[0]).astype(F32)
            out[i] = ((middle[i] + row[:, 3 * D :] * br_two) * held).astype(BF)
            grad_mod[pl.ds(slot, 1), 3 * D :] = jnp.sum(cot[i] * br_two, axis=0, keepdims=True)
            grad_mod[pl.ds(slot, 1), D : 2 * D] = jnp.sum(d_hid, axis=0, keepdims=True)
            grad_mod[pl.ds(slot, 1), 2 * D : 3 * D] = jnp.sum(
                d_hid * normed[i], axis=0, keepdims=True
            )
            grad_mid = cot[i] + norm_back(
                d_hid * (1.0 + row[:, 2 * D : 3 * D]), normed[i], inverse[i]
            )
            grad_mid_out[slot] = grad_mid
            grad_mod[pl.ds(slot, 1), :D] = jnp.sum(
                grad_mid * branch_all[span[i]], axis=0, keepdims=True
            )
            g_one.append((grad_mid * row[:, :D]).astype(BF))
        g_one = jnp.concatenate(g_one, axis=0)
        acc_bias[2:3, :D] += jnp.sum(g_one.astype(F32), axis=0, keepdims=True)
        acc_proj[...] += dot_tn(mixed, g_one)
        grad_mixed_out[pl.ds(PAIR * step, PAIR)] = (
            dot_nt(g_one, w_proj).astype(BF).reshape(PAIR, TOK, D)
        )

    @pl.when(step == STEPS - 1)
    def _():
        cond_low = silu(conditions[...].astype(F32)).astype(BF)
        g_mod = grad_mod[...].astype(BF)
        mod_grad = dot_tn(cond_low.astype(F32), g_mod.astype(F32)).astype(BF)
        z_high, core, column = info[2], info[3], info[1]
        sums = jnp.sum(g_mod.astype(F32), axis=0, keepdims=True)
        rows = [jnp.zeros((ROW_MOD + 6, 128), F32)]
        rows += [sums[:, 128 * i : 128 * i + 128] for i in range(12)]
        rows += [acc_bias[2:3, 128 * i : 128 * i + 128] for i in range(3)]
        rows += [acc_bias[0:1, 128 * i : 128 * i + 128] for i in range(12)]
        rows += [acc_bias[1:2, 128 * i : 128 * i + 128] for i in range(3)]
        rows += [jnp.zeros((3, 128), F32)]
        bias_block = jnp.concatenate(rows, axis=0).astype(BF)
        for owner in range(8):
            zh, xx = owner // 4, owner % 4
            spot = lax.rem(xx - column + 4, 4) * 48
            spot = pl.multiple_of(spot, 16)
            is_mine = (z_high ^ core) == zh
            lo = 48 * owner

            def put(ref, spot=spot, lo=lo, owner=owner):
                ref[pl.ds(spot, 48), :FF] = acc_up[lo : lo + 48, :].astype(BF)
                ref[pl.ds(spot, 48), AT_MOD : AT_MOD + MOD_TWO] = mod_grad[lo : lo + 48, :]
                ref[pl.ds(spot, 48), AT_PROJ : AT_PROJ + D] = acc_proj[lo : lo + 48, :].astype(BF)
                for q in range(4):
                    at = 192 * owner + 48 * q
                    ref[pl.ds(spot, 48), AT_DOWN + D * q : AT_DOWN + D * q + D] = acc_down[
                        at : at + 48, :
                    ].astype(BF)
                ref[pl.ds(spot, 48), BIAS_TWO : BIAS_TWO + 128] = bias_block

            pl.when(is_mine)(functools.partial(put, keep))
            pl.when(jnp.logical_not(is_mine))(functools.partial(put, send))


def backward_kernel(
    info, latents, conditions, qkv_in, expo_in, mixed_in, rinv_in, hidden_in, grad_mid_in,
    grad_mixed_in, mod_in, weights, weights_two, grad_mod_two,
    out, grad_cond, keep, send,
    acc_qkv, acc_bias, grad_mod,
):
    step = pl.program_id(0)
    slot = PAIR * step

    @pl.when(step == 0)
    def _():
        acc_qkv[...] = jnp.zeros_like(acc_qkv)
        acc_bias[...] = jnp.zeros_like(acc_bias)
        grad_mod[...] = jnp.zeros_like(grad_mod)

    @pl.when(slot >= info[0])
    def _():
        out[...] = jnp.zeros((PAIR, TOK, D), BF)

    @pl.when(slot < info[0])
    def _():
        low = lax.broadcasted_iota(jnp.int32, (TOK, 128), 1) < HEAD_DIM
        factor = HEAD_DIM**-0.5
        g_all = []
        for i in range(PAIR):
            qkv = qkv_in[slot + i]
            scaled = (grad_mixed_in[slot + i].astype(F32) * rinv_in[slot + i]).astype(BF)
            product = scaled.astype(F32) * mixed_in[slot + i].astype(F32)
            g_query, g_key, g_value = [], [], []
            for pair in range(HEADS // 2):
                at = 128 * pair
                query = qkv[:, at : at + 128]
                key = by_head(qkv[:, D + at : D + at + 128], low)
                value = by_head(qkv[:, 2 * D + at : 2 * D + at + 128], low)
                grad = scaled[:, at : at + 128]
                weighed = product[:, at : at + 128]
                expo = expo_in[slot + i, pair]
                g_probs = dot_nt(grad, value)
                g_scores = []
                for half in range(2):
                    mask = low if half == 0 else ~low
                    delta = jnp.sum(jnp.where(mask, weighed, 0.0), axis=-1, keepdims=True)
                    lanes = slice(TOK * half, TOK * half + TOK)
                    g_scores.append(
                        (expo[:, lanes].astype(F32) * (g_probs[:, lanes] - delta)).astype(BF)
                    )
                g_scores = jnp.concatenate(g_scores, axis=1)
                d_key, d_value = dot_tn(g_scores, query), dot_tn(expo, grad)
                g_query.append((dot(g_scores, key) * factor).astype(BF))
                g_key.append((jnp.where(low, d_key[:TOK], d_key[TOK:]) * factor).astype(BF))
                g_value.append(jnp.where(low, d_value[:TOK], d_value[TOK:]).astype(BF))
            g_all.append(jnp.concatenate(g_query + g_key + g_value, axis=1))
        g_qkv = jnp.concatenate(g_all, axis=0)
        hidden = hidden_in[pl.ds(slot, PAIR)].reshape(PAIR * TOK, D)
        acc_qkv[...] += dot_tn(hidden, g_qkv)
        acc_bias[0:1, :] += jnp.sum(g_qkv.astype(F32), axis=0, keepdims=True)
        d_all = dot_nt(g_qkv, weights[:, :QKV_W])
        for i in range(PAIR):
            row = mod_in[pl.ds(slot + i, 1), :]
            normed, inverse = normalize(latents[i].astype(F32))
            d_hidden = d_all[TOK * i : TOK * i + TOK]
            grad_mod[pl.ds(slot + i, 1), :D] = jnp.sum(d_hidden, axis=0, keepdims=True)
            grad_mod[pl.ds(slot + i, 1), D:] = jnp.sum(d_hidden * normed, axis=0, keepdims=True)
            back = norm_back(d_hidden * (1.0 + row[:, D : 2 * D]), normed, inverse)
            out[i] = (grad_mid_in[slot + i] + back).astype(BF)

    @pl.when(step == STEPS - 1)
    def _():
        cond = conditions[...].astype(F32)
        sig = 1.0 / (1.0 + jnp.exp(-cond))
        cond_low = (cond * sig).astype(BF)
        g_mod = grad_mod[...].astype(BF)
        g_mod_two = grad_mod_two[...].astype(BF)
        g_cond = dot_nt(g_mod, weights[:, QKV_W : QKV_W + MOD_ONE])
        g_cond += dot_nt(g_mod_two, weights_two[:, AT_MOD : AT_MOD + MOD_TWO])
        grad_cond[...] = (g_cond * (sig * (1.0 + cond * (1.0 - sig)))).astype(BF)
        mod_grad = dot_tn(cond_low.astype(F32), g_mod.astype(F32)).astype(BF)
        sums = jnp.sum(g_mod.astype(F32), axis=0, keepdims=True)
        rows = [acc_bias[0:1, 128 * i : 128 * i + 128] for i in range(9)]
        rows += [sums[:, 128 * i : 128 * i + 128] for i in range(6)]
        rows += [jnp.zeros((33, 128), F32)]
        bias_block = jnp.concatenate(rows, axis=0).astype(BF)
        z_high, core, column = info[2], info[3], info[1]
        for owner in range(8):
            zh, xx = owner // 4, owner % 4
            spot = pl.multiple_of(lax.rem(xx - column + 4, 4) * 48, 16)
            is_mine = (z_high ^ core) == zh
            lo = 48 * owner

            def put(ref, spot=spot, lo=lo):
                ref[pl.ds(spot, 48), :QKV_W] = acc_qkv[lo : lo + 48, :].astype(BF)
                ref[pl.ds(spot, 48), QKV_W : QKV_W + MOD_ONE] = mod_grad[lo : lo + 48, :]
                ref[pl.ds(spot, 48), BIAS_ONE : BIAS_ONE + 128] = bias_block

            pl.when(is_mine)(functools.partial(put, keep))
            pl.when(jnp.logical_not(is_mine))(functools.partial(put, send))


def slot_spec():
    def index(j, info):
        return (jnp.minimum(j, jnp.maximum((info[0] + 1) // 2 - 1, 0)), 0, 0)

    return pl.BlockSpec((PAIR, TOK, D), index)


def slot_out():
    return pl.BlockSpec((PAIR, TOK, D), lambda j, info: (j, 0, 0))


def held():
    return pl.BlockSpec(memory_space=pltpu.VMEM)


def whole(*shape):
    zeros = (0,) * len(shape)
    return pl.BlockSpec(shape, lambda j, info: zeros)


def params(mib):
    return pltpu.CompilerParams(
        dimension_semantics=("arbitrary",), vmem_limit_bytes=mib * MIB
    )


def far(value):
    return pltpu.with_memory_space_constraint(value, pltpu.HBM)


def stay(value):
    return pltpu.with_memory_space_constraint(value, pltpu.VMEM)


def run_forward(info, latents, conditions, pieces):
    return pl.pallas_call(
        forward_kernel,
        grid_spec=pltpu.PrefetchScalarGridSpec(
            num_scalar_prefetch=1,
            grid=(STEPS,),
            in_specs=[slot_spec(), whole(CAP, D)] + [held()] * 8,
            out_specs=[held()] * 8,
        ),
        out_shape=[
            pltpu.VMEM((D, LANES_ONE), BF),
            pltpu.VMEM((48, 128), F32),
            pltpu.VMEM((CAP, MOD_ONE), F32),
            pltpu.VMEM((CAP, TOK, QKV_W), BF),
            pltpu.VMEM((CAP, HEADS // 2, TOK, 2 * TOK), BF),
            pltpu.VMEM((CAP, TOK, D), BF),
            pltpu.VMEM((CAP, TOK, D), F32),
            pltpu.VMEM((CAP, TOK, D), BF),
        ],
        compiler_params=params(10),
        name="attention_forward",
        cost_estimate=pl.CostEstimate(
            flops=3_000_000_000, bytes_accessed=20_000_000, transcendentals=3_000_000
        ),
    )(info, far(latents), far(conditions), *pieces)


def run_middle(info, latents, conditions, mixed, grad_out, bias, pieces):
    return pl.pallas_call(
        middle_kernel,
        grid_spec=pltpu.PrefetchScalarGridSpec(
            num_scalar_prefetch=1,
            grid=(STEPS,),
            in_specs=[
                slot_spec(),
                whole(CAP, D),
                held(),
                slot_spec(),
                held(),
            ]
            + [held()] * 8,
            out_specs=[held(), slot_out()] + [held()] * 5,
            scratch_shapes=[
                pltpu.VMEM((CAP, MOD_TWO), F32),
                pltpu.VMEM((D, FF), F32),
                pltpu.VMEM((FF, D), F32),
                pltpu.VMEM((D, D), F32),
                pltpu.VMEM((8, FF), F32),
                pltpu.VMEM((FF, D), BF),
            ],
        ),
        out_shape=[
            pltpu.VMEM((D, LANES_TWO), BF),
            jax.ShapeDtypeStruct((CAP, TOK, D), BF),
            pltpu.VMEM((CAP, TOK, D), F32),
            pltpu.VMEM((CAP, TOK, D), BF),
            pltpu.VMEM((CAP, MOD_TWO), F32),
            pltpu.VMEM((192, LANES_TWO), BF),
            pltpu.VMEM((192, LANES_TWO), BF),
        ],
        compiler_params=params(23),
        name="feed_forward_both_ways",
        cost_estimate=pl.CostEstimate(
            flops=16_000_000_000, bytes_accessed=30_000_000, transcendentals=3_000_000
        ),
    )(info, far(latents), far(conditions), stay(mixed), far(grad_out), stay(bias), *pieces)


def run_backward(info, latents, conditions, *values):
    return pl.pallas_call(
        backward_kernel,
        grid_spec=pltpu.PrefetchScalarGridSpec(
            num_scalar_prefetch=1,
            grid=(STEPS,),
            in_specs=[slot_spec(), whole(CAP, D)] + [held()] * 11,
            out_specs=[slot_out(), whole(CAP, D), held(), held()],
            scratch_shapes=[
                pltpu.VMEM((D, QKV_W), F32),
                pltpu.VMEM((8, QKV_W), F32),
                pltpu.VMEM((CAP, MOD_ONE), F32),
            ],
        ),
        out_shape=[
            jax.ShapeDtypeStruct((CAP, TOK, D), BF),
            jax.ShapeDtypeStruct((CAP, D), BF),
            pltpu.VMEM((192, LANES_ONE), BF),
            pltpu.VMEM((192, LANES_ONE), BF),
        ],
        compiler_params=params(10),
        name="attention_backward",
        cost_estimate=pl.CostEstimate(
            flops=25_000_000_000, bytes_accessed=20_000_000, transcendentals=1_000
        ),
    )(info, far(latents), far(conditions), *map(stay, values))


def place(index):
    shard, rep = divmod(index, 16)
    return shard // 4, shard % 4, rep // 4, (rep // 2) % 2, rep % 2


def index_of(z_high, x, y, z_low, core):
    return (z_high * 4 + x) * 16 + y * 4 + z_low * 2 + core


def routes(target_of):
    return [(i, target_of(*place(i))) for i in range(TWIN)]


def fetch(k):
    def source(zh, x, y, zl, c):
        if c == 0:
            return index_of(zh, (x + k) % 4, y, zl, c)
        return index_of(1 - zh, (x + k) % 4, y, 1 - zl, c)

    return [(source(*place(i)), i) for i in range(TWIN)]


CORE_SWAP = routes(lambda zh, x, y, zl, c: index_of(zh, x, y, zl, 1 - c))
ZLOW_SWAP = routes(lambda zh, x, y, zl, c: index_of(zh, x, y, 1 - zl, c))
BOTH = ("shard", "rep")


def move(value, pairs):
    return lax.ppermute(value, BOTH, pairs)


def y_route(k):
    return routes(lambda zh, x, y, zl, c: index_of(zh, x, (y + k) % 4, zl, c))


def after(value, *earlier):
    return lax.optimization_barrier((value, *earlier))[0]


def fetch_all(block):
    return [move(block, fetch(k)) for k in range(4)]


def swap_all(pieces):
    return [move(piece, CORE_SWAP) for piece in pieces]


def small_call(kernel, name, shapes, *values, scalars=False):
    return pl.pallas_call(
        kernel,
        in_specs=[pl.BlockSpec(memory_space=pltpu.SMEM)] * scalars
        + [held()] * (len(values) - scalars),
        out_shape=[jax.ShapeDtypeStruct(shape, BF) for shape in shapes],
        compiler_params=pltpu.CompilerParams(vmem_limit_bytes=14 * MIB),
        name=name,
    )(*values)


def add_kernel(*refs):
    refs[-1][...] = sum(ref[...].astype(F32) for ref in refs[:-1]).astype(BF)


def add(*values):
    return small_call(add_kernel, "add", [values[0].shape], *values)[0]


def add_blocks_kernel(left, right, *outs):
    for k, out in enumerate(outs):
        rows = slice(48 * k, 48 * k + 48)
        out[...] = (left[rows, :].astype(F32) + right[rows, :].astype(F32)).astype(BF)


def add_blocks(left, right):
    shape = (48, left.shape[1])
    return small_call(add_blocks_kernel, "add_blocks", [shape] * 4, left, right)


def add_halves_kernel(info, *refs):
    lanes = refs[-1].shape[1]
    for out, core in ((refs[-2], info[3]), (refs[-1], 1 - info[3])):
        at = pl.ds(pl.multiple_of(core * lanes, 128), lanes)
        out[...] = sum(ref[:, at].astype(F32) for ref in refs[:-2]).astype(BF)


def add_halves(info, pieces):
    shape = (48, pieces[0].shape[1] // 2)
    return small_call(
        add_halves_kernel, "add_halves", [shape] * 2, info, *pieces, scalars=True
    )


def scatter(blocks):
    back = [[(target, source) for source, target in fetch(k)] for k in range(4)]
    return [move(block, pairs) for block, pairs in zip(blocks, back)]


def sum_replicas(arrived, info):
    mine, other = add_halves(info, arrived)
    total = add(mine, move(other, CORE_SWAP))
    total = add(total, move(total, ZLOW_SWAP))
    total = add(total, *(move(total, y_route(k)) for k in (1, 2, 3)))
    return [total, move(total, CORE_SWAP)]


def row_of(ref):
    size = ref.shape[0]
    row = ref[...].astype(F32).reshape(1, size)
    if size % 128:
        row = jnp.concatenate([row, jnp.zeros((1, -size % 128), F32)], axis=1)
    return row


def pack_one_kernel(qkv, mod, qv_bias, mod_bias, proj_bias, up_bias, down_bias, out):
    out[:, :QKV_W] = qkv[...]
    out[:, QKV_W:BIAS_ONE] = mod[:, :MOD_ONE]
    flat = [row_of(ref) for ref in (qv_bias, mod_bias, proj_bias, up_bias, down_bias)]
    flat = jnp.concatenate(flat, axis=1)
    rows = [flat[:, 128 * i : 128 * i + 128] for i in range(8)] + [jnp.zeros((40, 128), F32)]
    out[:, BIAS_ONE:] = jnp.concatenate(rows, axis=0).astype(BF)


def pack_two_kernel(up, mod, proj, down, out):
    out[:, :FF] = up[...]
    out[:, AT_MOD:AT_PROJ] = mod[:, MOD_ONE:]
    out[:, AT_PROJ:AT_DOWN] = proj[...]
    for q in range(4):
        out[:, AT_DOWN + D * q : AT_DOWN + D * q + D] = down[48 * q : 48 * q + 48, :]
    out[:, BIAS_TWO:] = jnp.zeros((48, 128), BF)


def pack(kernel, name, lanes, *values):
    def once(shape):
        return pl.BlockSpec(shape, lambda j: (0,) * len(shape))

    return pl.pallas_call(
        kernel,
        grid=(1,),
        in_specs=[once(value.shape) for value in values],
        out_specs=once((48, lanes)),
        out_shape=pltpu.VMEM((48, lanes), BF),
        compiler_params=pltpu.CompilerParams(vmem_limit_bytes=8 * MIB),
        name=name,
    )(*map(far, values))


def finish_kernel(
    info, one_a, one_b, two_a, two_b, g_mod, g_mod_bias, g_qkv, g_qv_bias, g_proj, g_proj_bias,
    g_up, g_up_bias, g_down, g_down_bias,
):
    shard, first = info[1] + 4 * info[2], info[3] == 0

    def joined(mine, other):
        mine, other = mine[...].astype(F32), other[...].astype(F32)
        return jnp.concatenate(
            [jnp.where(first, mine, other), jnp.where(first, other, mine)], axis=1
        )

    one, two = joined(one_a, one_b), joined(two_a, two_b)
    g_mod[:, :MOD_ONE] = one[:, QKV_W:BIAS_ONE]
    g_mod[:, MOD_ONE:] = two[:, AT_MOD:AT_PROJ]
    g_qkv[...] = one[:, :QKV_W]
    g_proj[...] = two[:, AT_PROJ:AT_DOWN]
    g_up[...] = two[:, :FF]
    for q in range(4):
        g_down[48 * q : 48 * q + 48, :] = two[:, AT_DOWN + D * q : AT_DOWN + D * q + D]
    bias = one[:, BIAS_ONE:] + two[:, BIAS_TWO:]

    def own(first_row, count, size, out):
        row = bias_row(bias, first_row, count)
        row = jnp.broadcast_to(row, (8, 128 * count))
        turn = lax.rem(8 * size - shard * size, 8 * size)
        out[...] = pltpu.roll(row, turn, 1)[0:1, :size].reshape(size)

    own(ROW_MOD, 18, 288, g_mod_bias)
    query, value = bias_row(bias, 0, 3), bias_row(bias, 6, 3)
    row = jnp.broadcast_to(jnp.concatenate([query, value], axis=1), (8, 2 * D))
    turn = lax.rem(2 * D - shard * 96, 2 * D)
    g_qv_bias[...] = pltpu.roll(row, turn, 1)[0:1, :96].reshape(96)
    own(ROW_PROJ, 3, 48, g_proj_bias)
    own(ROW_UP, 12, 192, g_up_bias)
    own(ROW_DOWN, 3, 48, g_down_bias)


def finish(info, parts):
    shapes = [
        (48, 6 * D), (288,), (48, QKV_W), (96,), (48, D), (48,), (48, FF), (192,), (192, D), (48,),
    ]
    return pl.pallas_call(
        finish_kernel,
        in_specs=[pl.BlockSpec(memory_space=pltpu.SMEM)] + [held()] * 4,
        out_shape=[jax.ShapeDtypeStruct(shape, F32) for shape in shapes],
        compiler_params=pltpu.CompilerParams(vmem_limit_bytes=12 * MIB),
        name="unpack_gradients",
    )(info, *parts)


def on_device(
    latents, conditions, counts, mod_weight, mod_bias, qkv_weight, qv_bias, proj_weight,
    proj_bias, up_weight, up_bias, down_weight, down_bias, grad_out,
):
    shard = lax.axis_index("shard")
    rep = lax.axis_index("rep")
    info = jnp.stack([counts[0], shard % 4, shard // 4, rep % 2]).astype(jnp.int32)
    block_one = pack(
        pack_one_kernel, "pack_attention_weights", LANES_ONE,
        after(qkv_weight, info), mod_weight, qv_bias, mod_bias, proj_bias, up_bias, down_bias,
    )
    block_two = pack(
        pack_two_kernel, "pack_feed_forward_weights", LANES_TWO,
        up_weight, mod_weight, proj_weight, down_weight,
    )
    mine_one = fetch_all(block_one)
    mine_two = [move(block_two, fetch(0))]
    other_one = swap_all([mine_one[0]] + [after(piece, block_two) for piece in mine_one[1:]])
    block_two = after(block_two, *mine_one)
    mine_two += [move(block_two, fetch(k)) for k in (1, 2, 3)]
    weights, bias, mod, qkv, expo, mixed, rinv, hidden = run_forward(
        info, latents, conditions, mine_one + other_one
    )
    mine_two = [after(piece, mod) for piece in mine_two]
    other_two = swap_all(mine_two)
    weights_two, out, grad_mid, grad_mixed, grad_mod_two, keep_two, send_two = run_middle(
        info, latents, conditions, mixed, grad_out, bias, mine_two + other_two
    )
    held_two = add_blocks(keep_two, move(send_two, CORE_SWAP))
    arrived_two = scatter(held_two)
    grad_latents, grad_cond, keep_one, send_one = run_backward(
        info, latents, conditions, qkv, expo, mixed, rinv, hidden, grad_mid, grad_mixed, mod,
        weights, weights_two, after(grad_mod_two, held_two[0]),
    )
    held_one = add_blocks(keep_one, move(after(send_one, *arrived_two), CORE_SWAP))
    arrived_one = scatter(held_one)
    two = sum_replicas([after(arrived_two[0], arrived_one[1]), *arrived_two[1:]], info)
    one = sum_replicas(arrived_one, info)
    return (out, grad_latents, grad_cond, *finish(info, one + two))


def solution(mesh):
    slots = P(("shard", "rep"), None, None)
    rows = P(("shard", "rep"), None)
    matrix, vector = P("shard", None), P("shard")
    in_specs = (slots, rows, P(("shard", "rep"))) + (matrix, vector) * 5 + (slots,)
    out_specs = (slots, slots, rows) + (matrix, vector) * 5
    return jax.shard_map(
        on_device, mesh=mesh, in_specs=in_specs, out_specs=out_specs, check_vma=False
    )
```

```python
import functools

import jax
import jax.numpy as jnp
from jax import lax
from jax.experimental import pallas as pl
from jax.experimental.pallas import tpu as pltpu
from jax.sharding import PartitionSpec as P

D = 384
HEADS = 6
HEAD_DIM = 64
FF = 1536
TOK = 256
CAP = 8
PAIR = 2
QUAD = 4
CHUNK = 768
STEPS = CAP // PAIR
TWIN = 128
BF = jnp.bfloat16
F32 = jnp.float32
MIB = 1024 * 1024

LANES_ONE = 2048
QKV_W = 3 * D
MOD_ONE = 2 * D
BIAS_ONE = QKV_W + MOD_ONE
LANES_TWO = 5120
MOD_TWO = 4 * D
AT_MOD = FF
AT_PROJ = AT_MOD + MOD_TWO
AT_DOWN = AT_PROJ + D
BIAS_TWO = AT_DOWN + FF
ROW_QKV, ROW_MOD, ROW_PROJ, ROW_UP, ROW_DOWN = 0, 9, 27, 30, 42


def dot(left, right):
    return jnp.dot(left, right, preferred_element_type=F32)


def dot_tn(left, right):
    return lax.dot_general(left, right, (((0,), (0,)), ((), ())), preferred_element_type=F32)


def dot_nt(left, right):
    return lax.dot_general(left, right, (((1,), (1,)), ((), ())), preferred_element_type=F32)


def normalize(value):
    center = jnp.mean(value, axis=-1, keepdims=True)
    centered = value - center
    spread = jnp.mean(centered * centered, axis=-1, keepdims=True)
    inverse = lax.rsqrt(spread + 1e-06)
    return centered * inverse, inverse


def norm_back(grad, normed, inverse):
    first = jnp.mean(grad, axis=-1, keepdims=True)
    second = jnp.mean(grad * normed, axis=-1, keepdims=True)
    return inverse * (grad - first - normed * second)


def spread(rows, size):
    width = 8 * size
    lane = lax.broadcasted_iota(jnp.int32, (8, width), 1)
    total = jnp.zeros((8, width), F32)
    for owner, row in enumerate(rows):
        padded = jnp.concatenate([row, jnp.zeros((1, width - row.shape[1]), F32)], axis=1)
        padded = jnp.where(lane < size, jnp.broadcast_to(padded, (8, width)), 0.0)
        total += pltpu.roll(padded, owner * size, 1) if owner else padded
    return total[0:1]


def all_biases(raw):
    def rows(first, count):
        return [
            jnp.concatenate([block[first + i : first + i + 1] for i in range(count)], axis=1)
            for block in raw
        ]

    qv = spread(rows(0, 1), 96)
    full = [qv[:, :D], jnp.zeros((1, D), F32), qv[:, D:]]
    full += [spread(rows(1, 3), 288), spread(rows(4, 1), 48)]
    full += [spread(rows(5, 2), 192), spread(rows(7, 1), 48)]
    full = jnp.concatenate(full, axis=1)
    cut = [full[:, 128 * i : 128 * i + 128] for i in range(45)]
    return jnp.concatenate(cut + [jnp.zeros((3, 128), F32)], axis=0)


def by_head(value, low):
    zero = jnp.zeros_like(value)
    return jnp.concatenate([jnp.where(low, value, zero), jnp.where(low, zero, value)], axis=0)


def bias_row(bias, first, count):
    return jnp.concatenate([bias[first + i : first + i + 1, :] for i in range(count)], axis=1)


def silu(cond):
    return cond * (1.0 / (1.0 + jnp.exp(-cond)))


def assemble(info, pieces, full):
    column, z_high, core = info[1], info[2], info[3]
    for k in range(4):
        spot = lax.rem(column + k, 4) * 48
        mine = (z_high ^ core) * 192 + spot
        other = (1 - (z_high ^ core)) * 192 + spot
        full[pl.ds(pl.multiple_of(mine, 16), 48), :] = pieces[k][...]
        full[pl.ds(pl.multiple_of(other, 16), 48), :] = pieces[4 + k][...]


def forward_kernel(
    info, latents, conditions, p0, p1, p2, p3, p4, p5, p6, p7,
    weights, bias_out, mod_out, qkv_out, expo_out, mixed_out, rinv_out, hidden_out,
):
    step = pl.program_id(0)

    @pl.when(step == 0)
    def _():
        assemble(info, (p0, p1, p2, p3, p4, p5, p6, p7), weights)
        total = all_biases(
            [
                weights[48 * k : 48 * k + 16, BIAS_ONE : BIAS_ONE + 128].astype(F32)[:8]
                for k in range(8)
            ]
        )
        bias_out[...] = total
        cond_low = silu(conditions[...].astype(F32)).astype(BF)
        mod_out[...] = dot(cond_low, weights[:, QKV_W : QKV_W + MOD_ONE]) + bias_row(
            total, ROW_MOD, 6
        )

    @pl.when(QUAD * step < info[0])
    def _():
        hidden = []
        for i in range(QUAD):
            mod = mod_out[pl.ds(QUAD * step + i, 1), :]
            normed, _ = normalize(latents[i].astype(F32))
            hidden.append((normed * (1.0 + mod[:, D : 2 * D]) + mod[:, :D]).astype(BF))
            hidden_out[QUAD * step + i] = hidden[i]
        full_bias = bias_row(bias_out[0:16, :], ROW_QKV, 9)
        qkv_all = dot(jnp.concatenate(hidden, axis=0), weights[:, :QKV_W])
        qkv_all = (qkv_all + full_bias).astype(BF)
        low = lax.broadcasted_iota(jnp.int32, (TOK, 128), 1) < HEAD_DIM
        for i in range(QUAD):
            slot = QUAD * step + i
            qkv = qkv_all[TOK * i : TOK * i + TOK]
            qkv_out[slot] = qkv
            for pair in range(HEADS // 2):
                at = 128 * pair
                query = qkv[:, at : at + 128] * jnp.asarray(HEAD_DIM**-0.5, BF)
                value = qkv[:, 2 * D + at : 2 * D + at + 128]
                scores = dot_nt(query, by_head(qkv[:, D + at : D + at + 128], low))
                expo = jnp.concatenate(
                    [
                        jnp.exp(part - jnp.max(part, axis=-1, keepdims=True)).astype(BF)
                        for part in (scores[:, :TOK], scores[:, TOK:])
                    ],
                    axis=1,
                )
                expo_out[slot, pair] = expo
                sums = by_head(jnp.ones((TOK, 128), BF), low)
                both = dot(expo, jnp.concatenate([by_head(value, low), sums], axis=1))
                inverse = 1.0 / both[:, 128:]
                rinv_out[slot, :, at : at + 128] = inverse
                mixed_out[slot, :, at : at + 128] = (both[:, :128] * inverse).astype(BF)


def middle_kernel(
    info, latents, conditions, mixed_in, grad_out, bias_in, p0, p1, p2, p3, p4, p5, p6, p7,
    weights, out, grad_mid_out, grad_mixed_out, grad_mod, keep, send,
    mod, acc_up, acc_down, acc_proj, acc_bias, down,
):
    step = pl.program_id(0)

    @pl.when(step == 0)
    def _():
        assemble(info, (p0, p1, p2, p3, p4, p5, p6, p7), weights)
        cond_low = silu(conditions[...].astype(F32)).astype(BF)
        mod[...] = dot(cond_low, weights[:, AT_MOD : AT_MOD + MOD_TWO]) + bias_row(
            bias_in[...], ROW_MOD + 6, 12
        )
        for owner in range(8):
            for q in range(4):
                at = 192 * owner + 48 * q
                down[at : at + 48, :] = weights[
                    48 * owner : 48 * owner + 48, AT_DOWN + D * q : AT_DOWN + D * q + D
                ]
        acc_up[...] = jnp.zeros_like(acc_up)
        acc_down[...] = jnp.zeros_like(acc_down)
        acc_proj[...] = jnp.zeros_like(acc_proj)
        acc_bias[...] = jnp.zeros_like(acc_bias)
        grad_mod[...] = jnp.zeros_like(grad_mod)

    @pl.when(PAIR * step >= info[0])
    def _():
        out[...] = jnp.zeros((PAIR, TOK, D), BF)
        grad_mid_out[pl.ds(PAIR * step, PAIR)] = jnp.zeros((PAIR, TOK, D), F32)
        grad_mixed_out[pl.ds(PAIR * step, PAIR)] = jnp.zeros((PAIR, TOK, D), BF)

    @pl.when(PAIR * step < info[0])
    def _():
        bias = bias_in[...]
        w_proj = weights[:, AT_PROJ : AT_PROJ + D]
        up_bias = bias_row(bias, ROW_UP, 12)
        mixed = mixed_in[pl.ds(PAIR * step, PAIR)].reshape(PAIR * TOK, D)
        branch_all = dot(mixed, w_proj) + bias_row(bias, ROW_PROJ, 3)
        rows = [mod[pl.ds(PAIR * step + i, 1), :] for i in range(PAIR)]
        span = [slice(TOK * i, TOK * i + TOK) for i in range(PAIR)]
        middle, normed, inverse, hidden, cot, g_two = [], [], [], [], [], []
        for i in range(PAIR):
            row = rows[i]
            middle.append(latents[i].astype(F32) + row[:, :D] * branch_all[span[i]])
            value, scale = normalize(middle[i])
            normed.append(value)
            inverse.append(scale)
            hidden.append((value * (1.0 + row[:, 2 * D : 3 * D]) + row[:, D : 2 * D]).astype(BF))
            held = (PAIR * step + i < info[0]).astype(F32)
            cot.append(grad_out[i].astype(F32) * held)
            g_two.append((cot[i] * row[:, 3 * D :]).astype(BF))
        hidden = jnp.concatenate(hidden, axis=0)
        g_two = jnp.concatenate(g_two, axis=0)
        branch_two = bias_row(bias, ROW_DOWN, 3)
        d_hidden = jnp.zeros((PAIR * TOK, D), F32)
        root = 0.7978845608028654
        cube = root * 0.044715
        for chunk in range(FF // CHUNK):
            at = CHUNK * chunk
            w_up = weights[:, at : at + CHUNK]
            w_down = down[at : at + CHUNK, :]
            upward = dot(hidden, w_up) + up_bias[:, at : at + CHUNK]
            square = upward * upward
            bend = jnp.tanh(upward * (root + cube * square))
            half = 0.5 + 0.5 * bend
            act = upward * half
            slope = half + act * (1.0 - bend) * (root + (3.0 * cube) * square)
            act_low = act.astype(BF)
            branch_two = branch_two + dot(act_low, w_down)
            acc_down[at : at + CHUNK, :] += dot_tn(act_low, g_two)
            g_up = (slope * dot_nt(g_two, w_down)).astype(BF)
            acc_up[:, at : at + CHUNK] += dot_tn(hidden, g_up)
            acc_bias[0:1, at : at + CHUNK] += jnp.sum(g_up.astype(F32), axis=0, keepdims=True)
            d_hidden = d_hidden + dot_nt(g_up, w_up)
        acc_bias[1:2, :D] += jnp.sum(g_two.astype(F32), axis=0, keepdims=True)
        g_one = []
        for i in range(PAIR):
            row, slot = rows[i], PAIR * step + i
            d_hid, br_two = d_hidden[span[i]], branch_two[span[i]]
            held = (slot < info[0]).astype(F32)
            out[i] = ((middle[i] + row[:, 3 * D :] * br_two) * held).astype(BF)
            grad_mod[pl.ds(slot, 1), 3 * D :] = jnp.sum(cot[i] * br_two, axis=0, keepdims=True)
            grad_mod[pl.ds(slot, 1), D : 2 * D] = jnp.sum(d_hid, axis=0, keepdims=True)
            grad_mod[pl.ds(slot, 1), 2 * D : 3 * D] = jnp.sum(
                d_hid * normed[i], axis=0, keepdims=True
            )
            grad_mid = cot[i] + norm_back(
                d_hid * (1.0 + row[:, 2 * D : 3 * D]), normed[i], inverse[i]
            )
            grad_mid_out[slot] = grad_mid
            grad_mod[pl.ds(slot, 1), :D] = jnp.sum(
                grad_mid * branch_all[span[i]], axis=0, keepdims=True
            )
            g_one.append((grad_mid * row[:, :D]).astype(BF))
        g_one = jnp.concatenate(g_one, axis=0)
        acc_bias[2:3, :D] += jnp.sum(g_one.astype(F32), axis=0, keepdims=True)
        acc_proj[...] += dot_tn(mixed, g_one)
        grad_mixed_out[pl.ds(PAIR * step, PAIR)] = (
            dot_nt(g_one, w_proj).astype(BF).reshape(PAIR, TOK, D)
        )

    @pl.when(step == STEPS - 1)
    def _():
        cond_low = silu(conditions[...].astype(F32)).astype(BF)
        g_mod = grad_mod[...].astype(BF)
        mod_grad = dot_tn(cond_low.astype(F32), g_mod.astype(F32)).astype(BF)
        z_high, core, column = info[2], info[3], info[1]
        sums = jnp.sum(g_mod.astype(F32), axis=0, keepdims=True)
        rows = [jnp.zeros((ROW_MOD + 6, 128), F32)]
        rows += [sums[:, 128 * i : 128 * i + 128] for i in range(12)]
        rows += [acc_bias[2:3, 128 * i : 128 * i + 128] for i in range(3)]
        rows += [acc_bias[0:1, 128 * i : 128 * i + 128] for i in range(12)]
        rows += [acc_bias[1:2, 128 * i : 128 * i + 128] for i in range(3)]
        rows += [jnp.zeros((3, 128), F32)]
        bias_block = jnp.concatenate(rows, axis=0).astype(BF)
        for owner in range(8):
            zh, xx = owner // 4, owner % 4
            spot = lax.rem(xx - column + 4, 4) * 48
            spot = pl.multiple_of(spot, 16)
            is_mine = (z_high ^ core) == zh
            lo = 48 * owner

            def put(ref, spot=spot, lo=lo, owner=owner):
                ref[pl.ds(spot, 48), :FF] = acc_up[lo : lo + 48, :].astype(BF)
                ref[pl.ds(spot, 48), AT_MOD : AT_MOD + MOD_TWO] = mod_grad[lo : lo + 48, :]
                ref[pl.ds(spot, 48), AT_PROJ : AT_PROJ + D] = acc_proj[lo : lo + 48, :].astype(BF)
                for q in range(4):
                    at = 192 * owner + 48 * q
                    ref[pl.ds(spot, 48), AT_DOWN + D * q : AT_DOWN + D * q + D] = acc_down[
                        at : at + 48, :
                    ].astype(BF)
                ref[pl.ds(spot, 48), BIAS_TWO : BIAS_TWO + 128] = bias_block

            pl.when(is_mine)(functools.partial(put, keep))
            pl.when(jnp.logical_not(is_mine))(functools.partial(put, send))


def backward_kernel(
    info, latents, conditions, qkv_in, expo_in, mixed_in, rinv_in, hidden_in, grad_mid_in,
    grad_mixed_in, mod_in, weights, weights_two, grad_mod_two,
    out, grad_cond, keep, send,
    acc_qkv, acc_bias, grad_mod,
):
    step = pl.program_id(0)
    slot = QUAD * step

    @pl.when(step == 0)
    def _():
        acc_qkv[...] = jnp.zeros_like(acc_qkv)
        acc_bias[...] = jnp.zeros_like(acc_bias)
        grad_mod[...] = jnp.zeros_like(grad_mod)

    @pl.when(slot >= info[0])
    def _():
        out[...] = jnp.zeros((QUAD, TOK, D), BF)

    @pl.when(slot < info[0])
    def _():
        low = lax.broadcasted_iota(jnp.int32, (TOK, 128), 1) < HEAD_DIM
        factor = HEAD_DIM**-0.5
        g_all = []
        for i in range(QUAD):
            qkv = qkv_in[slot + i]
            scaled = (grad_mixed_in[slot + i].astype(F32) * rinv_in[slot + i]).astype(BF)
            product = scaled.astype(F32) * mixed_in[slot + i].astype(F32)
            g_query, g_key, g_value = [], [], []
            for pair in range(HEADS // 2):
                at = 128 * pair
                query = qkv[:, at : at + 128]
                key = by_head(qkv[:, D + at : D + at + 128], low)
                value = by_head(qkv[:, 2 * D + at : 2 * D + at + 128], low)
                grad = scaled[:, at : at + 128]
                weighed = product[:, at : at + 128]
                expo = expo_in[slot + i, pair]
                g_probs = dot_nt(grad, value)
                g_scores = []
                for half in range(2):
                    mask = low if half == 0 else ~low
                    delta = jnp.sum(jnp.where(mask, weighed, 0.0), axis=-1, keepdims=True)
                    lanes = slice(TOK * half, TOK * half + TOK)
                    g_scores.append(
                        (expo[:, lanes].astype(F32) * (g_probs[:, lanes] - delta)).astype(BF)
                    )
                g_scores = jnp.concatenate(g_scores, axis=1)
                d_key, d_value = dot_tn(g_scores, query), dot_tn(expo, grad)
                g_query.append((dot(g_scores, key) * factor).astype(BF))
                g_key.append((jnp.where(low, d_key[:TOK], d_key[TOK:]) * factor).astype(BF))
                g_value.append(jnp.where(low, d_value[:TOK], d_value[TOK:]).astype(BF))
            g_all.append(jnp.concatenate(g_query + g_key + g_value, axis=1))
        g_qkv = jnp.concatenate(g_all, axis=0)
        hidden = hidden_in[pl.ds(slot, QUAD)].reshape(QUAD * TOK, D)
        acc_qkv[...] += dot_tn(hidden, g_qkv)
        acc_bias[0:1, :] += jnp.sum(g_qkv.astype(F32), axis=0, keepdims=True)
        d_all = dot_nt(g_qkv, weights[:, :QKV_W])
        for i in range(QUAD):
            row = mod_in[pl.ds(slot + i, 1), :]
            normed, inverse = normalize(latents[i].astype(F32))
            d_hidden = d_all[TOK * i : TOK * i + TOK]
            grad_mod[pl.ds(slot + i, 1), :D] = jnp.sum(d_hidden, axis=0, keepdims=True)
            grad_mod[pl.ds(slot + i, 1), D:] = jnp.sum(d_hidden * normed, axis=0, keepdims=True)
            back = norm_back(d_hidden * (1.0 + row[:, D : 2 * D]), normed, inverse)
            out[i] = (grad_mid_in[slot + i] + back).astype(BF)

    @pl.when(step == CAP // QUAD - 1)
    def _():
        cond = conditions[...].astype(F32)
        sig = 1.0 / (1.0 + jnp.exp(-cond))
        cond_low = (cond * sig).astype(BF)
        g_mod = grad_mod[...].astype(BF)
        g_mod_two = grad_mod_two[...].astype(BF)
        g_cond = dot_nt(g_mod, weights[:, QKV_W : QKV_W + MOD_ONE])
        g_cond += dot_nt(g_mod_two, weights_two[:, AT_MOD : AT_MOD + MOD_TWO])
        grad_cond[...] = (g_cond * (sig * (1.0 + cond * (1.0 - sig)))).astype(BF)
        mod_grad = dot_tn(cond_low.astype(F32), g_mod.astype(F32)).astype(BF)
        sums = jnp.sum(g_mod.astype(F32), axis=0, keepdims=True)
        rows = [acc_bias[0:1, 128 * i : 128 * i + 128] for i in range(9)]
        rows += [sums[:, 128 * i : 128 * i + 128] for i in range(6)]
        rows += [jnp.zeros((33, 128), F32)]
        bias_block = jnp.concatenate(rows, axis=0).astype(BF)
        z_high, core, column = info[2], info[3], info[1]
        for owner in range(8):
            zh, xx = owner // 4, owner % 4
            spot = pl.multiple_of(lax.rem(xx - column + 4, 4) * 48, 16)
            is_mine = (z_high ^ core) == zh
            lo = 48 * owner

            def put(ref, spot=spot, lo=lo):
                ref[pl.ds(spot, 48), :QKV_W] = acc_qkv[lo : lo + 48, :].astype(BF)
                ref[pl.ds(spot, 48), QKV_W : QKV_W + MOD_ONE] = mod_grad[lo : lo + 48, :]
                ref[pl.ds(spot, 48), BIAS_ONE : BIAS_ONE + 128] = bias_block

            pl.when(is_mine)(functools.partial(put, keep))
            pl.when(jnp.logical_not(is_mine))(functools.partial(put, send))


def slot_spec(group):
    def index(j, info):
        return (jnp.minimum(j, jnp.maximum((info[0] + group - 1) // group - 1, 0)), 0, 0)

    return pl.BlockSpec((group, TOK, D), index)


def slot_out(group):
    return pl.BlockSpec((group, TOK, D), lambda j, info: (j, 0, 0))


def held():
    return pl.BlockSpec(memory_space=pltpu.VMEM)


def whole(*shape):
    zeros = (0,) * len(shape)
    return pl.BlockSpec(shape, lambda j, info: zeros)


def params(mib):
    return pltpu.CompilerParams(
        dimension_semantics=("arbitrary",), vmem_limit_bytes=mib * MIB
    )


def far(value):
    return pltpu.with_memory_space_constraint(value, pltpu.HBM)


def stay(value):
    return pltpu.with_memory_space_constraint(value, pltpu.VMEM)


def run_forward(info, latents, conditions, pieces):
    return pl.pallas_call(
        forward_kernel,
        grid_spec=pltpu.PrefetchScalarGridSpec(
            num_scalar_prefetch=1,
            grid=(CAP // QUAD,),
            in_specs=[slot_spec(QUAD), whole(CAP, D)] + [held()] * 8,
            out_specs=[held()] * 8,
        ),
        out_shape=[
            pltpu.VMEM((D, LANES_ONE), BF),
            pltpu.VMEM((48, 128), F32),
            pltpu.VMEM((CAP, MOD_ONE), F32),
            pltpu.VMEM((CAP, TOK, QKV_W), BF),
            pltpu.VMEM((CAP, HEADS // 2, TOK, 2 * TOK), BF),
            pltpu.VMEM((CAP, TOK, D), BF),
            pltpu.VMEM((CAP, TOK, D), F32),
            pltpu.VMEM((CAP, TOK, D), BF),
        ],
        compiler_params=params(12),
        name="attention_forward",
        cost_estimate=pl.CostEstimate(
            flops=3_000_000_000, bytes_accessed=20_000_000, transcendentals=3_000_000
        ),
    )(info, far(latents), far(conditions), *pieces)


def run_middle(info, latents, conditions, mixed, grad_out, bias, pieces):
    return pl.pallas_call(
        middle_kernel,
        grid_spec=pltpu.PrefetchScalarGridSpec(
            num_scalar_prefetch=1,
            grid=(CAP // PAIR,),
            in_specs=[
                slot_spec(PAIR),
                whole(CAP, D),
                held(),
                slot_spec(PAIR),
                held(),
            ]
            + [held()] * 8,
            out_specs=[held(), slot_out(PAIR)] + [held()] * 5,
            scratch_shapes=[
                pltpu.VMEM((CAP, MOD_TWO), F32),
                pltpu.VMEM((D, FF), F32),
                pltpu.VMEM((FF, D), F32),
                pltpu.VMEM((D, D), F32),
                pltpu.VMEM((8, FF), F32),
                pltpu.VMEM((FF, D), BF),
            ],
        ),
        out_shape=[
            pltpu.VMEM((D, LANES_TWO), BF),
            jax.ShapeDtypeStruct((CAP, TOK, D), BF),
            pltpu.VMEM((CAP, TOK, D), F32),
            pltpu.VMEM((CAP, TOK, D), BF),
            pltpu.VMEM((CAP, MOD_TWO), F32),
            pltpu.VMEM((192, LANES_TWO), BF),
            pltpu.VMEM((192, LANES_TWO), BF),
        ],
        compiler_params=params(23),
        name="feed_forward_both_ways",
        cost_estimate=pl.CostEstimate(
            flops=16_000_000_000, bytes_accessed=30_000_000, transcendentals=3_000_000
        ),
    )(info, far(latents), far(conditions), stay(mixed), far(grad_out), stay(bias), *pieces)


def run_backward(info, latents, conditions, *values):
    return pl.pallas_call(
        backward_kernel,
        grid_spec=pltpu.PrefetchScalarGridSpec(
            num_scalar_prefetch=1,
            grid=(CAP // QUAD,),
            in_specs=[slot_spec(QUAD), whole(CAP, D)] + [held()] * 11,
            out_specs=[slot_out(QUAD), whole(CAP, D), held(), held()],
            scratch_shapes=[
                pltpu.VMEM((D, QKV_W), F32),
                pltpu.VMEM((8, QKV_W), F32),
                pltpu.VMEM((CAP, MOD_ONE), F32),
            ],
        ),
        out_shape=[
            jax.ShapeDtypeStruct((CAP, TOK, D), BF),
            jax.ShapeDtypeStruct((CAP, D), BF),
            pltpu.VMEM((192, LANES_ONE), BF),
            pltpu.VMEM((192, LANES_ONE), BF),
        ],
        compiler_params=params(12),
        name="attention_backward",
        cost_estimate=pl.CostEstimate(
            flops=25_000_000_000, bytes_accessed=20_000_000, transcendentals=1_000
        ),
    )(info, far(latents), far(conditions), *map(stay, values))


def place(index):
    shard, rep = divmod(index, 16)
    return shard // 4, shard % 4, rep // 4, (rep // 2) % 2, rep % 2


def index_of(z_high, x, y, z_low, core):
    return (z_high * 4 + x) * 16 + y * 4 + z_low * 2 + core


def routes(target_of):
    return [(i, target_of(*place(i))) for i in range(TWIN)]


def fetch(k):
    def source(zh, x, y, zl, c):
        if c == 0:
            return index_of(zh, (x + k) % 4, y, zl, c)
        return index_of(1 - zh, (x + k) % 4, y, 1 - zl, c)

    return [(source(*place(i)), i) for i in range(TWIN)]


CORE_SWAP = routes(lambda zh, x, y, zl, c: index_of(zh, x, y, zl, 1 - c))
ZLOW_SWAP = routes(lambda zh, x, y, zl, c: index_of(zh, x, y, 1 - zl, c))
BOTH = ("shard", "rep")


def move(value, pairs):
    return lax.ppermute(value, BOTH, pairs)


def y_route(k):
    return routes(lambda zh, x, y, zl, c: index_of(zh, x, (y + k) % 4, zl, c))


def after(value, *earlier):
    return lax.optimization_barrier((value, *earlier))[0]


def fetch_all(block):
    return [move(block, fetch(k)) for k in range(4)]


def swap_all(pieces):
    return [move(piece, CORE_SWAP) for piece in pieces]


def small_call(kernel, name, shapes, *values, scalars=False):
    return pl.pallas_call(
        kernel,
        in_specs=[pl.BlockSpec(memory_space=pltpu.SMEM)] * scalars
        + [held()] * (len(values) - scalars),
        out_shape=[jax.ShapeDtypeStruct(shape, BF) for shape in shapes],
        compiler_params=pltpu.CompilerParams(vmem_limit_bytes=14 * MIB),
        name=name,
    )(*values)


def add_kernel(*refs):
    refs[-1][...] = sum(ref[...].astype(F32) for ref in refs[:-1]).astype(BF)


def add(*values):
    return small_call(add_kernel, "add", [values[0].shape], *values)[0]


def add_blocks_kernel(left, right, *outs):
    for k, out in enumerate(outs):
        rows = slice(48 * k, 48 * k + 48)
        out[...] = (left[rows, :].astype(F32) + right[rows, :].astype(F32)).astype(BF)


def add_blocks(left, right):
    shape = (48, left.shape[1])
    return small_call(add_blocks_kernel, "add_blocks", [shape] * 4, left, right)


def add_halves_kernel(info, *refs):
    lanes = refs[-1].shape[1]
    for out, core in ((refs[-2], info[3]), (refs[-1], 1 - info[3])):
        at = pl.ds(pl.multiple_of(core * lanes, 128), lanes)
        out[...] = sum(ref[:, at].astype(F32) for ref in refs[:-2]).astype(BF)


def add_halves(info, pieces):
    shape = (48, pieces[0].shape[1] // 2)
    return small_call(
        add_halves_kernel, "add_halves", [shape] * 2, info, *pieces, scalars=True
    )


def scatter(blocks):
    back = [[(target, source) for source, target in fetch(k)] for k in range(4)]
    return [move(block, pairs) for block, pairs in zip(blocks, back)]


def sum_replicas(arrived, info, *earlier):
    mine, other = add_halves(info, arrived)
    total = add(mine, move(other, CORE_SWAP))
    if earlier:
        total = after(total, *earlier)
    total = add(total, move(total, ZLOW_SWAP))
    total = add(total, *(move(total, y_route(k)) for k in (1, 2, 3)))
    return [total, move(total, CORE_SWAP)]


def row_of(ref):
    size = ref.shape[0]
    row = ref[...].astype(F32).reshape(1, size)
    if size % 128:
        row = jnp.concatenate([row, jnp.zeros((1, -size % 128), F32)], axis=1)
    return row


def pack_one_kernel(qkv, mod, qv_bias, mod_bias, proj_bias, up_bias, down_bias, out):
    out[:, :QKV_W] = qkv[...]
    out[:, QKV_W:BIAS_ONE] = mod[:, :MOD_ONE]
    flat = [row_of(ref) for ref in (qv_bias, mod_bias, proj_bias, up_bias, down_bias)]
    flat = jnp.concatenate(flat, axis=1)
    rows = [flat[:, 128 * i : 128 * i + 128] for i in range(8)] + [jnp.zeros((40, 128), F32)]
    out[:, BIAS_ONE:] = jnp.concatenate(rows, axis=0).astype(BF)


def pack_two_kernel(up, mod, proj, down, out):
    out[:, :FF] = up[...]
    out[:, AT_MOD:AT_PROJ] = mod[:, MOD_ONE:]
    out[:, AT_PROJ:AT_DOWN] = proj[...]
    for q in range(4):
        out[:, AT_DOWN + D * q : AT_DOWN + D * q + D] = down[48 * q : 48 * q + 48, :]
    out[:, BIAS_TWO:] = jnp.zeros((48, 128), BF)


def pack(kernel, name, lanes, *values):
    def once(shape):
        return pl.BlockSpec(shape, lambda j: (0,) * len(shape))

    return pl.pallas_call(
        kernel,
        grid=(1,),
        in_specs=[once(value.shape) for value in values],
        out_specs=once((48, lanes)),
        out_shape=pltpu.VMEM((48, lanes), BF),
        compiler_params=pltpu.CompilerParams(vmem_limit_bytes=8 * MIB),
        name=name,
    )(*map(far, values))


def joined(info, mine, other):
    first = info[3] == 0
    mine, other = mine[...].astype(F32), other[...].astype(F32)
    return jnp.concatenate([jnp.where(first, mine, other), jnp.where(first, other, mine)], axis=1)


def unpack_two_kernel(info, mine, other, g_mod, g_proj, g_up, g_down, bias):
    two = joined(info, mine, other)
    g_mod[:, MOD_ONE:] = two[:, AT_MOD:AT_PROJ]
    g_proj[...] = two[:, AT_PROJ:AT_DOWN]
    g_up[...] = two[:, :FF]
    for q in range(4):
        g_down[48 * q : 48 * q + 48, :] = two[:, AT_DOWN + D * q : AT_DOWN + D * q + D]
    bias[...] = two[:, BIAS_TWO:]


def unpack_one_kernel(
    info, mine, other, bias_two, _, g_mod, g_mod_bias, g_qkv, g_qv_bias, g_proj_bias, g_up_bias,
    g_down_bias,
):
    shard = info[1] + 4 * info[2]
    one = joined(info, mine, other)
    g_mod[...] = one[:, QKV_W:BIAS_ONE]
    g_qkv[...] = one[:, :QKV_W]
    bias = one[:, BIAS_ONE:] + bias_two[...]

    def own(row, size, out):
        row = jnp.broadcast_to(row, (8, row.shape[1]))
        turn = lax.rem(8 * size - shard * size, 8 * size)
        out[...] = pltpu.roll(row, turn, 1)[0:1, :size].reshape(size)

    own(bias_row(bias, ROW_MOD, 18), 288, g_mod_bias)
    own(jnp.concatenate([bias_row(bias, 0, 3), bias_row(bias, 6, 3)], axis=1), 96, g_qv_bias)
    own(bias_row(bias, ROW_PROJ, 3), 48, g_proj_bias)
    own(bias_row(bias, ROW_UP, 12), 192, g_up_bias)
    own(bias_row(bias, ROW_DOWN, 3), 48, g_down_bias)


def finish(info, one, two):
    scalars = pl.BlockSpec(memory_space=pltpu.SMEM)
    shapes = [(48, 6 * D), (48, D), (48, FF), (192, D), (48, 128)]
    g_mod, g_proj, g_up, g_down, bias_two = pl.pallas_call(
        unpack_two_kernel,
        in_specs=[scalars] + [held()] * 2,
        out_shape=[jax.ShapeDtypeStruct(shape, F32) for shape in shapes],
        compiler_params=pltpu.CompilerParams(vmem_limit_bytes=12 * MIB),
        name="unpack_second_batch",
    )(info, *two)
    shapes = [(48, 6 * D), (288,), (48, QKV_W), (96,), (48,), (192,), (48,)]

    def once(shape):
        return pl.BlockSpec(shape, lambda j: (0,) * len(shape))

    g_mod, g_mod_bias, g_qkv, g_qv_bias, g_proj_bias, g_up_bias, g_down_bias = pl.pallas_call(
        unpack_one_kernel,
        grid=(1,),
        in_specs=[scalars] + [held()] * 3 + [pl.BlockSpec(memory_space=pl.ANY)],
        out_specs=[once((48, MOD_ONE))] + [once(shape) for shape in shapes[1:]],
        out_shape=[jax.ShapeDtypeStruct(shape, F32) for shape in shapes],
        input_output_aliases={4: 0},
        compiler_params=pltpu.CompilerParams(vmem_limit_bytes=8 * MIB),
        name="unpack_first_batch",
    )(info, *one, bias_two, g_mod)
    return (
        g_mod, g_mod_bias, g_qkv, g_qv_bias, g_proj, g_proj_bias, g_up, g_up_bias, g_down,
        g_down_bias,
    )


def on_device(
    latents, conditions, counts, mod_weight, mod_bias, qkv_weight, qv_bias, proj_weight,
    proj_bias, up_weight, up_bias, down_weight, down_bias, grad_out,
):
    shard = lax.axis_index("shard")
    rep = lax.axis_index("rep")
    info = jnp.stack([counts[0], shard % 4, shard // 4, rep % 2]).astype(jnp.int32)
    block_one = pack(
        pack_one_kernel, "pack_attention_weights", LANES_ONE,
        after(qkv_weight, info), mod_weight, qv_bias, mod_bias, proj_bias, up_bias, down_bias,
    )
    block_two = pack(
        pack_two_kernel, "pack_feed_forward_weights", LANES_TWO,
        up_weight, mod_weight, proj_weight, down_weight,
    )
    mine_one = fetch_all(block_one)
    mine_two = [move(block_two, fetch(0))]
    other_one = swap_all([mine_one[0]] + [after(piece, block_two) for piece in mine_one[1:]])
    block_two = after(block_two, *mine_one)
    mine_two += [move(block_two, fetch(k)) for k in (1, 2, 3)]
    weights, bias, mod, qkv, expo, mixed, rinv, hidden = run_forward(
        info, latents, conditions, mine_one + other_one
    )
    mine_two = [after(piece, mod) for piece in mine_two]
    other_two = swap_all(mine_two)
    weights_two, out, grad_mid, grad_mixed, grad_mod_two, keep_two, send_two = run_middle(
        info, latents, conditions, mixed, grad_out, bias, mine_two + other_two
    )
    held_two = add_blocks(keep_two, move(send_two, CORE_SWAP))
    arrived_two = scatter(held_two)
    grad_latents, grad_cond, keep_one, send_one = run_backward(
        info, latents, conditions, qkv, expo, mixed, rinv, hidden, grad_mid, grad_mixed, mod,
        weights, weights_two, after(grad_mod_two, held_two[0]),
    )
    held_one = add_blocks(keep_one, move(after(send_one, *arrived_two), CORE_SWAP))
    arrived_one = scatter(held_one)
    two = sum_replicas(arrived_two, info, *held_one)
    one = sum_replicas(arrived_one, info)
    return (out, grad_latents, grad_cond, *finish(info, one, two))


def solution(mesh):
    slots = P(("shard", "rep"), None, None)
    rows = P(("shard", "rep"), None)
    matrix, vector = P("shard", None), P("shard")
    in_specs = (slots, rows, P(("shard", "rep"))) + (matrix, vector) * 5 + (slots,)
    out_specs = (slots, slots, rows) + (matrix, vector) * 5
    return jax.shard_map(
        on_device, mesh=mesh, in_specs=in_specs, out_specs=out_specs, check_vma=False
    )
```

```python
import functools

import jax
import jax.numpy as jnp
from jax import lax
from jax.experimental import pallas as pl
from jax.experimental.pallas import tpu as pltpu
from jax.sharding import PartitionSpec as P

D = 384
HEADS = 6
HEAD_DIM = 64
FF = 1536
TOK = 256
CAP = 8
PAIR = 2
QUAD = 4
CHUNK = 768
STEPS = CAP // PAIR
TWIN = 128
BF = jnp.bfloat16
F32 = jnp.float32
MIB = 1024 * 1024

LANES_ONE = 2048
QKV_W = 3 * D
MOD_ONE = 2 * D
BIAS_ONE = QKV_W + MOD_ONE
LANES_TWO = 5120
MOD_TWO = 4 * D
AT_MOD = FF
AT_PROJ = AT_MOD + MOD_TWO
AT_DOWN = AT_PROJ + D
BIAS_TWO = AT_DOWN + FF
ROW_QKV, ROW_MOD, ROW_PROJ, ROW_UP, ROW_DOWN = 0, 9, 27, 30, 42


def dot(left, right):
    return jnp.dot(left, right, preferred_element_type=F32)


def dot_tn(left, right):
    return lax.dot_general(left, right, (((0,), (0,)), ((), ())), preferred_element_type=F32)


def dot_nt(left, right):
    return lax.dot_general(left, right, (((1,), (1,)), ((), ())), preferred_element_type=F32)


def normalize(value):
    center = jnp.mean(value, axis=-1, keepdims=True)
    centered = value - center
    spread = jnp.mean(centered * centered, axis=-1, keepdims=True)
    inverse = lax.rsqrt(spread + 1e-06)
    return centered * inverse, inverse


def norm_back(grad, normed, inverse):
    first = jnp.mean(grad, axis=-1, keepdims=True)
    second = jnp.mean(grad * normed, axis=-1, keepdims=True)
    return inverse * (grad - first - normed * second)


def spread(rows, size):
    width = 8 * size
    lane = lax.broadcasted_iota(jnp.int32, (8, width), 1)
    total = jnp.zeros((8, width), F32)
    for owner, row in enumerate(rows):
        padded = jnp.concatenate([row, jnp.zeros((1, width - row.shape[1]), F32)], axis=1)
        padded = jnp.where(lane < size, jnp.broadcast_to(padded, (8, width)), 0.0)
        total += pltpu.roll(padded, owner * size, 1) if owner else padded
    return total[0:1]


def all_biases(raw):
    def rows(first, count):
        return [
            jnp.concatenate([block[first + i : first + i + 1] for i in range(count)], axis=1)
            for block in raw
        ]

    qv = spread(rows(0, 1), 96)
    full = [qv[:, :D], jnp.zeros((1, D), F32), qv[:, D:]]
    full += [spread(rows(1, 3), 288), spread(rows(4, 1), 48)]
    full += [spread(rows(5, 2), 192), spread(rows(7, 1), 48)]
    full = jnp.concatenate(full, axis=1)
    cut = [full[:, 128 * i : 128 * i + 128] for i in range(45)]
    return jnp.concatenate(cut + [jnp.zeros((3, 128), F32)], axis=0)


def by_head(value, low):
    zero = jnp.zeros_like(value)
    return jnp.concatenate([jnp.where(low, value, zero), jnp.where(low, zero, value)], axis=0)


def bias_row(bias, first, count):
    return jnp.concatenate([bias[first + i : first + i + 1, :] for i in range(count)], axis=1)


def silu(cond):
    return cond * (1.0 / (1.0 + jnp.exp(-cond)))


def assemble(info, pieces, full):
    column, z_high, core = info[1], info[2], info[3]
    for k in range(4):
        spot = lax.rem(column + k, 4) * 48
        mine = (z_high ^ core) * 192 + spot
        other = (1 - (z_high ^ core)) * 192 + spot
        full[pl.ds(pl.multiple_of(mine, 16), 48), :] = pieces[k][...]
        full[pl.ds(pl.multiple_of(other, 16), 48), :] = pieces[4 + k][...]


def forward_kernel(
    info, latents, conditions, p0, p1, p2, p3, p4, p5, p6, p7,
    weights, bias_out, mod_out, qkv_out, expo_out, mixed_out, rinv_out, hidden_out,
):
    step = pl.program_id(0)

    @pl.when(step == 0)
    def _():
        assemble(info, (p0, p1, p2, p3, p4, p5, p6, p7), weights)
        total = all_biases(
            [
                weights[48 * k : 48 * k + 16, BIAS_ONE : BIAS_ONE + 128].astype(F32)[:8]
                for k in range(8)
            ]
        )
        bias_out[...] = total
        cond_low = silu(conditions[...].astype(F32)).astype(BF)
        mod_out[...] = dot(cond_low, weights[:, QKV_W : QKV_W + MOD_ONE]) + bias_row(
            total, ROW_MOD, 6
        )

    @pl.when(QUAD * step < info[0])
    def _():
        hidden = []
        for i in range(QUAD):
            mod = mod_out[pl.ds(QUAD * step + i, 1), :]
            normed, _ = normalize(latents[i].astype(F32))
            hidden.append((normed * (1.0 + mod[:, D : 2 * D]) + mod[:, :D]).astype(BF))
            hidden_out[QUAD * step + i] = hidden[i]
        full_bias = bias_row(bias_out[0:16, :], ROW_QKV, 9)
        qkv_all = dot(jnp.concatenate(hidden, axis=0), weights[:, :QKV_W])
        qkv_all = (qkv_all + full_bias).astype(BF)
        low = lax.broadcasted_iota(jnp.int32, (TOK, 128), 1) < HEAD_DIM
        for i in range(QUAD):
            slot = QUAD * step + i
            qkv = qkv_all[TOK * i : TOK * i + TOK]
            qkv_out[slot] = qkv
            for pair in range(HEADS // 2):
                at = 128 * pair
                query = qkv[:, at : at + 128] * jnp.asarray(HEAD_DIM**-0.5, BF)
                value = qkv[:, 2 * D + at : 2 * D + at + 128]
                scores = dot_nt(query, by_head(qkv[:, D + at : D + at + 128], low))
                expo = jnp.concatenate(
                    [
                        jnp.exp(part - jnp.max(part, axis=-1, keepdims=True)).astype(BF)
                        for part in (scores[:, :TOK], scores[:, TOK:])
                    ],
                    axis=1,
                )
                expo_out[slot, pair] = expo
                sums = by_head(jnp.ones((TOK, 128), BF), low)
                both = dot(expo, jnp.concatenate([by_head(value, low), sums], axis=1))
                inverse = 1.0 / both[:, 128:]
                rinv_out[slot, :, at : at + 128] = inverse
                mixed_out[slot, :, at : at + 128] = (both[:, :128] * inverse).astype(BF)


def middle_kernel(
    info, latents, conditions, mixed_in, grad_out, bias_in, p0, p1, p2, p3, p4, p5, p6, p7,
    weights, out, grad_mid_out, grad_mixed_out, grad_mod, keep, send,
    mod, acc_up, acc_down, acc_proj, acc_bias, down,
):
    step = pl.program_id(0)

    @pl.when(step == 0)
    def _():
        assemble(info, (p0, p1, p2, p3, p4, p5, p6, p7), weights)
        cond_low = silu(conditions[...].astype(F32)).astype(BF)
        mod[...] = dot(cond_low, weights[:, AT_MOD : AT_MOD + MOD_TWO]) + bias_row(
            bias_in[...], ROW_MOD + 6, 12
        )
        for owner in range(8):
            for q in range(4):
                at = 192 * owner + 48 * q
                down[at : at + 48, :] = weights[
                    48 * owner : 48 * owner + 48, AT_DOWN + D * q : AT_DOWN + D * q + D
                ]
        acc_up[...] = jnp.zeros_like(acc_up)
        acc_down[...] = jnp.zeros_like(acc_down)
        acc_proj[...] = jnp.zeros_like(acc_proj)
        acc_bias[...] = jnp.zeros_like(acc_bias)
        grad_mod[...] = jnp.zeros_like(grad_mod)

    @pl.when(PAIR * step >= info[0])
    def _():
        out[...] = jnp.zeros((PAIR, TOK, D), BF)
        grad_mid_out[pl.ds(PAIR * step, PAIR)] = jnp.zeros((PAIR, TOK, D), F32)
        grad_mixed_out[pl.ds(PAIR * step, PAIR)] = jnp.zeros((PAIR, TOK, D), BF)

    @pl.when(PAIR * step < info[0])
    def _():
        bias = bias_in[...]
        w_proj = weights[:, AT_PROJ : AT_PROJ + D]
        up_bias = bias_row(bias, ROW_UP, 12)
        mixed = mixed_in[pl.ds(PAIR * step, PAIR)].reshape(PAIR * TOK, D)
        branch_all = dot(mixed, w_proj) + bias_row(bias, ROW_PROJ, 3)
        rows = [mod[pl.ds(PAIR * step + i, 1), :] for i in range(PAIR)]
        span = [slice(TOK * i, TOK * i + TOK) for i in range(PAIR)]
        middle, normed, inverse, hidden, cot, g_two = [], [], [], [], [], []
        for i in range(PAIR):
            row = rows[i]
            middle.append(latents[i].astype(F32) + row[:, :D] * branch_all[span[i]])
            value, scale = normalize(middle[i])
            normed.append(value)
            inverse.append(scale)
            hidden.append((value * (1.0 + row[:, 2 * D : 3 * D]) + row[:, D : 2 * D]).astype(BF))
            held = (PAIR * step + i < info[0]).astype(F32)
            cot.append(grad_out[i].astype(F32) * held)
            g_two.append((cot[i] * row[:, 3 * D :]).astype(BF))
        hidden = jnp.concatenate(hidden, axis=0)
        g_two = jnp.concatenate(g_two, axis=0)
        branch_two = bias_row(bias, ROW_DOWN, 3)
        d_hidden = jnp.zeros((PAIR * TOK, D), F32)
        root = 0.7978845608028654
        cube = root * 0.044715
        for chunk in range(FF // CHUNK):
            at = CHUNK * chunk
            w_up = weights[:, at : at + CHUNK]
            w_down = down[at : at + CHUNK, :]
            upward = dot(hidden, w_up) + up_bias[:, at : at + CHUNK]
            square = upward * upward
            bend = jnp.tanh(upward * (root + cube * square))
            half = 0.5 + 0.5 * bend
            act = upward * half
            slope = half + act * (1.0 - bend) * (root + (3.0 * cube) * square)
            act_low = act.astype(BF)
            branch_two = branch_two + dot(act_low, w_down)
            acc_down[at : at + CHUNK, :] += dot_tn(act_low, g_two)
            g_up = (slope * dot_nt(g_two, w_down)).astype(BF)
            acc_up[:, at : at + CHUNK] += dot_tn(hidden, g_up)
            acc_bias[0:1, at : at + CHUNK] += jnp.sum(g_up.astype(F32), axis=0, keepdims=True)
            d_hidden = d_hidden + dot_nt(g_up, w_up)
        acc_bias[1:2, :D] += jnp.sum(g_two.astype(F32), axis=0, keepdims=True)
        g_one = []
        for i in range(PAIR):
            row, slot = rows[i], PAIR * step + i
            d_hid, br_two = d_hidden[span[i]], branch_two[span[i]]
            held = (slot < info[0]).astype(F32)
            out[i] = ((middle[i] + row[:, 3 * D :] * br_two) * held).astype(BF)
            grad_mod[pl.ds(slot, 1), 3 * D :] = jnp.sum(cot[i] * br_two, axis=0, keepdims=True)
            grad_mod[pl.ds(slot, 1), D : 2 * D] = jnp.sum(d_hid, axis=0, keepdims=True)
            grad_mod[pl.ds(slot, 1), 2 * D : 3 * D] = jnp.sum(
                d_hid * normed[i], axis=0, keepdims=True
            )
            grad_mid = cot[i] + norm_back(
                d_hid * (1.0 + row[:, 2 * D : 3 * D]), normed[i], inverse[i]
            )
            grad_mid_out[slot] = grad_mid
            grad_mod[pl.ds(slot, 1), :D] = jnp.sum(
                grad_mid * branch_all[span[i]], axis=0, keepdims=True
            )
            g_one.append((grad_mid * row[:, :D]).astype(BF))
        g_one = jnp.concatenate(g_one, axis=0)
        acc_bias[2:3, :D] += jnp.sum(g_one.astype(F32), axis=0, keepdims=True)
        acc_proj[...] += dot_tn(mixed, g_one)
        grad_mixed_out[pl.ds(PAIR * step, PAIR)] = (
            dot_nt(g_one, w_proj).astype(BF).reshape(PAIR, TOK, D)
        )

    @pl.when(step == STEPS - 1)
    def _():
        cond_low = silu(conditions[...].astype(F32)).astype(BF)
        g_mod = grad_mod[...].astype(BF)
        mod_grad = dot_tn(cond_low.astype(F32), g_mod.astype(F32)).astype(BF)
        z_high, core, column = info[2], info[3], info[1]
        sums = jnp.sum(g_mod.astype(F32), axis=0, keepdims=True)
        rows = [jnp.zeros((ROW_MOD + 6, 128), F32)]
        rows += [sums[:, 128 * i : 128 * i + 128] for i in range(12)]
        rows += [acc_bias[2:3, 128 * i : 128 * i + 128] for i in range(3)]
        rows += [acc_bias[0:1, 128 * i : 128 * i + 128] for i in range(12)]
        rows += [acc_bias[1:2, 128 * i : 128 * i + 128] for i in range(3)]
        rows += [jnp.zeros((3, 128), F32)]
        bias_block = jnp.concatenate(rows, axis=0).astype(BF)
        for owner in range(8):
            zh, xx = owner // 4, owner % 4
            spot = lax.rem(xx - column + 4, 4) * 48
            spot = pl.multiple_of(spot, 16)
            is_mine = (z_high ^ core) == zh
            lo = 48 * owner

            def put(ref, spot=spot, lo=lo, owner=owner):
                ref[pl.ds(spot, 48), :FF] = acc_up[lo : lo + 48, :].astype(BF)
                ref[pl.ds(spot, 48), AT_MOD : AT_MOD + MOD_TWO] = mod_grad[lo : lo + 48, :]
                ref[pl.ds(spot, 48), AT_PROJ : AT_PROJ + D] = acc_proj[lo : lo + 48, :].astype(BF)
                for q in range(4):
                    at = 192 * owner + 48 * q
                    ref[pl.ds(spot, 48), AT_DOWN + D * q : AT_DOWN + D * q + D] = acc_down[
                        at : at + 48, :
                    ].astype(BF)
                ref[pl.ds(spot, 48), BIAS_TWO : BIAS_TWO + 128] = bias_block

            pl.when(is_mine)(functools.partial(put, keep))
            pl.when(jnp.logical_not(is_mine))(functools.partial(put, send))


def backward_kernel(
    info, latents, conditions, qkv_in, expo_in, mixed_in, rinv_in, hidden_in, grad_mid_in,
    grad_mixed_in, mod_in, weights, weights_two, grad_mod_two,
    out, grad_cond, keep, send,
    acc_qkv, acc_bias, grad_mod,
):
    step = pl.program_id(0)
    slot = QUAD * step

    @pl.when(step == 0)
    def _():
        acc_qkv[...] = jnp.zeros_like(acc_qkv)
        acc_bias[...] = jnp.zeros_like(acc_bias)
        grad_mod[...] = jnp.zeros_like(grad_mod)

    @pl.when(slot >= info[0])
    def _():
        out[...] = jnp.zeros((QUAD, TOK, D), BF)

    @pl.when(slot < info[0])
    def _():
        low = lax.broadcasted_iota(jnp.int32, (TOK, 128), 1) < HEAD_DIM
        factor = HEAD_DIM**-0.5
        g_all = []
        for i in range(QUAD):
            qkv = qkv_in[slot + i]
            scaled = (grad_mixed_in[slot + i].astype(F32) * rinv_in[slot + i]).astype(BF)
            product = scaled.astype(F32) * mixed_in[slot + i].astype(F32)
            g_query, g_key, g_value = [], [], []
            for pair in range(HEADS // 2):
                at = 128 * pair
                query = qkv[:, at : at + 128]
                key = by_head(qkv[:, D + at : D + at + 128], low)
                value = by_head(qkv[:, 2 * D + at : 2 * D + at + 128], low)
                grad = scaled[:, at : at + 128]
                weighed = product[:, at : at + 128]
                expo = expo_in[slot + i, pair]
                g_probs = dot_nt(grad, value)
                g_scores = []
                for half in range(2):
                    mask = low if half == 0 else ~low
                    delta = jnp.sum(jnp.where(mask, weighed, 0.0), axis=-1, keepdims=True)
                    lanes = slice(TOK * half, TOK * half + TOK)
                    g_scores.append(
                        (expo[:, lanes].astype(F32) * (g_probs[:, lanes] - delta)).astype(BF)
                    )
                g_scores = jnp.concatenate(g_scores, axis=1)
                d_key, d_value = dot_tn(g_scores, query), dot_tn(expo, grad)
                g_query.append((dot(g_scores, key) * factor).astype(BF))
                g_key.append((jnp.where(low, d_key[:TOK], d_key[TOK:]) * factor).astype(BF))
                g_value.append(jnp.where(low, d_value[:TOK], d_value[TOK:]).astype(BF))
            g_all.append(jnp.concatenate(g_query + g_key + g_value, axis=1))
        g_qkv = jnp.concatenate(g_all, axis=0)
        hidden = hidden_in[pl.ds(slot, QUAD)].reshape(QUAD * TOK, D)
        acc_qkv[...] += dot_tn(hidden, g_qkv)
        acc_bias[0:1, :] += jnp.sum(g_qkv.astype(F32), axis=0, keepdims=True)
        d_all = dot_nt(g_qkv, weights[:, :QKV_W])
        for i in range(QUAD):
            row = mod_in[pl.ds(slot + i, 1), :]
            normed, inverse = normalize(latents[i].astype(F32))
            d_hidden = d_all[TOK * i : TOK * i + TOK]
            grad_mod[pl.ds(slot + i, 1), :D] = jnp.sum(d_hidden, axis=0, keepdims=True)
            grad_mod[pl.ds(slot + i, 1), D:] = jnp.sum(d_hidden * normed, axis=0, keepdims=True)
            back = norm_back(d_hidden * (1.0 + row[:, D : 2 * D]), normed, inverse)
            out[i] = (grad_mid_in[slot + i] + back).astype(BF)

    @pl.when(step == CAP // QUAD - 1)
    def _():
        cond = conditions[...].astype(F32)
        sig = 1.0 / (1.0 + jnp.exp(-cond))
        cond_low = (cond * sig).astype(BF)
        g_mod = grad_mod[...].astype(BF)
        g_mod_two = grad_mod_two[...].astype(BF)
        g_cond = dot_nt(g_mod, weights[:, QKV_W : QKV_W + MOD_ONE])
        g_cond += dot_nt(g_mod_two, weights_two[:, AT_MOD : AT_MOD + MOD_TWO])
        grad_cond[...] = (g_cond * (sig * (1.0 + cond * (1.0 - sig)))).astype(BF)
        mod_grad = dot_tn(cond_low.astype(F32), g_mod.astype(F32)).astype(BF)
        sums = jnp.sum(g_mod.astype(F32), axis=0, keepdims=True)
        rows = [acc_bias[0:1, 128 * i : 128 * i + 128] for i in range(9)]
        rows += [sums[:, 128 * i : 128 * i + 128] for i in range(6)]
        rows += [jnp.zeros((33, 128), F32)]
        bias_block = jnp.concatenate(rows, axis=0).astype(BF)
        z_high, core, column = info[2], info[3], info[1]
        for owner in range(8):
            zh, xx = owner // 4, owner % 4
            spot = pl.multiple_of(lax.rem(xx - column + 4, 4) * 48, 16)
            is_mine = (z_high ^ core) == zh
            lo = 48 * owner

            def put(ref, spot=spot, lo=lo):
                ref[pl.ds(spot, 48), :QKV_W] = acc_qkv[lo : lo + 48, :].astype(BF)
                ref[pl.ds(spot, 48), QKV_W : QKV_W + MOD_ONE] = mod_grad[lo : lo + 48, :]
                ref[pl.ds(spot, 48), BIAS_ONE : BIAS_ONE + 128] = bias_block

            pl.when(is_mine)(functools.partial(put, keep))
            pl.when(jnp.logical_not(is_mine))(functools.partial(put, send))


def slot_spec(group):
    def index(j, info):
        return (jnp.minimum(j, jnp.maximum((info[0] + group - 1) // group - 1, 0)), 0, 0)

    return pl.BlockSpec((group, TOK, D), index)


def slot_out(group):
    return pl.BlockSpec((group, TOK, D), lambda j, info: (j, 0, 0))


def held():
    return pl.BlockSpec(memory_space=pltpu.VMEM)


def whole(*shape):
    zeros = (0,) * len(shape)
    return pl.BlockSpec(shape, lambda j, info: zeros)


def params(mib):
    return pltpu.CompilerParams(
        dimension_semantics=("arbitrary",), vmem_limit_bytes=mib * MIB
    )


def far(value):
    return pltpu.with_memory_space_constraint(value, pltpu.HBM)


def stay(value):
    return pltpu.with_memory_space_constraint(value, pltpu.VMEM)


def run_forward(info, latents, conditions, pieces):
    return pl.pallas_call(
        forward_kernel,
        grid_spec=pltpu.PrefetchScalarGridSpec(
            num_scalar_prefetch=1,
            grid=(CAP // QUAD,),
            in_specs=[slot_spec(QUAD), whole(CAP, D)] + [held()] * 8,
            out_specs=[held()] * 8,
        ),
        out_shape=[
            pltpu.VMEM((D, LANES_ONE), BF),
            pltpu.VMEM((48, 128), F32),
            pltpu.VMEM((CAP, MOD_ONE), F32),
            pltpu.VMEM((CAP, TOK, QKV_W), BF),
            pltpu.VMEM((CAP, HEADS // 2, TOK, 2 * TOK), BF),
            pltpu.VMEM((CAP, TOK, D), BF),
            pltpu.VMEM((CAP, TOK, D), F32),
            pltpu.VMEM((CAP, TOK, D), BF),
        ],
        compiler_params=params(12),
        name="attention_forward",
        cost_estimate=pl.CostEstimate(
            flops=12_000_000_000, bytes_accessed=60_000_000, transcendentals=3_000_000
        ),
    )(info, far(latents), far(conditions), *pieces)


def run_middle(info, latents, conditions, mixed, grad_out, bias, pieces):
    return pl.pallas_call(
        middle_kernel,
        grid_spec=pltpu.PrefetchScalarGridSpec(
            num_scalar_prefetch=1,
            grid=(CAP // PAIR,),
            in_specs=[
                slot_spec(PAIR),
                whole(CAP, D),
                held(),
                slot_spec(PAIR),
                held(),
            ]
            + [held()] * 8,
            out_specs=[held(), slot_out(PAIR)] + [held()] * 5,
            scratch_shapes=[
                pltpu.VMEM((CAP, MOD_TWO), F32),
                pltpu.VMEM((D, FF), F32),
                pltpu.VMEM((FF, D), F32),
                pltpu.VMEM((D, D), F32),
                pltpu.VMEM((8, FF), F32),
                pltpu.VMEM((FF, D), BF),
            ],
        ),
        out_shape=[
            pltpu.VMEM((D, LANES_TWO), BF),
            jax.ShapeDtypeStruct((CAP, TOK, D), BF),
            pltpu.VMEM((CAP, TOK, D), F32),
            pltpu.VMEM((CAP, TOK, D), BF),
            pltpu.VMEM((CAP, MOD_TWO), F32),
            pltpu.VMEM((192, LANES_TWO), BF),
            pltpu.VMEM((192, LANES_TWO), BF),
        ],
        compiler_params=params(23),
        name="feed_forward_both_ways",
        cost_estimate=pl.CostEstimate(
            flops=16_000_000_000, bytes_accessed=30_000_000, transcendentals=3_000_000
        ),
    )(info, far(latents), far(conditions), stay(mixed), far(grad_out), stay(bias), *pieces)


def run_backward(info, latents, conditions, *values):
    return pl.pallas_call(
        backward_kernel,
        grid_spec=pltpu.PrefetchScalarGridSpec(
            num_scalar_prefetch=1,
            grid=(CAP // QUAD,),
            in_specs=[slot_spec(QUAD), whole(CAP, D)] + [held()] * 11,
            out_specs=[slot_out(QUAD), whole(CAP, D), held(), held()],
            scratch_shapes=[
                pltpu.VMEM((D, QKV_W), F32),
                pltpu.VMEM((8, QKV_W), F32),
                pltpu.VMEM((CAP, MOD_ONE), F32),
            ],
        ),
        out_shape=[
            jax.ShapeDtypeStruct((CAP, TOK, D), BF),
            jax.ShapeDtypeStruct((CAP, D), BF),
            pltpu.VMEM((192, LANES_ONE), BF),
            pltpu.VMEM((192, LANES_ONE), BF),
        ],
        compiler_params=params(12),
        name="attention_backward",
        cost_estimate=pl.CostEstimate(
            flops=25_000_000_000, bytes_accessed=20_000_000, transcendentals=1_000
        ),
    )(info, far(latents), far(conditions), *map(stay, values))


def place(index):
    shard, rep = divmod(index, 16)
    return shard // 4, shard % 4, rep // 4, (rep // 2) % 2, rep % 2


def index_of(z_high, x, y, z_low, core):
    return (z_high * 4 + x) * 16 + y * 4 + z_low * 2 + core


def routes(target_of):
    return [(i, target_of(*place(i))) for i in range(TWIN)]


def fetch(k):
    def source(zh, x, y, zl, c):
        if c == 0:
            return index_of(zh, (x + k) % 4, y, zl, c)
        return index_of(1 - zh, (x + k) % 4, y, 1 - zl, c)

    return [(source(*place(i)), i) for i in range(TWIN)]


CORE_SWAP = routes(lambda zh, x, y, zl, c: index_of(zh, x, y, zl, 1 - c))
ZLOW_SWAP = routes(lambda zh, x, y, zl, c: index_of(zh, x, y, 1 - zl, c))
BOTH = ("shard", "rep")


def move(value, pairs):
    return lax.ppermute(value, BOTH, pairs)


def y_route(k):
    return routes(lambda zh, x, y, zl, c: index_of(zh, x, (y + k) % 4, zl, c))


def after(value, *earlier):
    return lax.optimization_barrier((value, *earlier))[0]


def fetch_all(block):
    return [move(block, fetch(k)) for k in range(4)]


def swap_all(pieces):
    return [move(piece, CORE_SWAP) for piece in pieces]


def small_call(kernel, name, shapes, *values, scalars=False):
    return pl.pallas_call(
        kernel,
        in_specs=[pl.BlockSpec(memory_space=pltpu.SMEM)] * scalars
        + [held()] * (len(values) - scalars),
        out_shape=[jax.ShapeDtypeStruct(shape, BF) for shape in shapes],
        compiler_params=pltpu.CompilerParams(vmem_limit_bytes=14 * MIB),
        name=name,
    )(*values)


def add_kernel(*refs):
    refs[-1][...] = sum(ref[...].astype(F32) for ref in refs[:-1]).astype(BF)


def add(*values):
    return small_call(add_kernel, "add", [values[0].shape], *values)[0]


def add_blocks_kernel(left, right, *outs):
    for k, out in enumerate(outs):
        rows = slice(48 * k, 48 * k + 48)
        out[...] = (left[rows, :].astype(F32) + right[rows, :].astype(F32)).astype(BF)


def add_blocks(left, right):
    shape = (48, left.shape[1])
    return small_call(add_blocks_kernel, "add_blocks", [shape] * 4, left, right)


def add_halves_kernel(info, *refs):
    lanes = refs[-1].shape[1]
    for out, core in ((refs[-2], info[3]), (refs[-1], 1 - info[3])):
        at = pl.ds(pl.multiple_of(core * lanes, 128), lanes)
        out[...] = sum(ref[:, at].astype(F32) for ref in refs[:-2]).astype(BF)


def add_halves(info, pieces):
    shape = (48, pieces[0].shape[1] // 2)
    return small_call(
        add_halves_kernel, "add_halves", [shape] * 2, info, *pieces, scalars=True
    )


def scatter(blocks):
    back = [[(target, source) for source, target in fetch(k)] for k in range(4)]
    return [move(block, pairs) for block, pairs in zip(blocks, back)]


def sum_replicas(arrived, info, *earlier):
    mine, other = add_halves(info, arrived)
    total = add(mine, move(other, CORE_SWAP))
    if earlier:
        total = after(total, *earlier)
    total = add(total, move(total, ZLOW_SWAP))
    total = add(total, *(move(total, y_route(k)) for k in (1, 2, 3)))
    return [total, move(total, CORE_SWAP)]


def row_of(ref):
    size = ref.shape[0]
    row = ref[...].astype(F32).reshape(1, size)
    if size % 128:
        row = jnp.concatenate([row, jnp.zeros((1, -size % 128), F32)], axis=1)
    return row


def pack_one_kernel(qkv, mod, qv_bias, mod_bias, proj_bias, up_bias, down_bias, out):
    out[:, :QKV_W] = qkv[...]
    out[:, QKV_W:BIAS_ONE] = mod[:, :MOD_ONE]
    flat = [row_of(ref) for ref in (qv_bias, mod_bias, proj_bias, up_bias, down_bias)]
    flat = jnp.concatenate(flat, axis=1)
    rows = [flat[:, 128 * i : 128 * i + 128] for i in range(8)] + [jnp.zeros((40, 128), F32)]
    out[:, BIAS_ONE:] = jnp.concatenate(rows, axis=0).astype(BF)


def pack_two_kernel(up, mod, proj, down, out):
    out[:, :FF] = up[...]
    out[:, AT_MOD:AT_PROJ] = mod[:, MOD_ONE:]
    out[:, AT_PROJ:AT_DOWN] = proj[...]
    for q in range(4):
        out[:, AT_DOWN + D * q : AT_DOWN + D * q + D] = down[48 * q : 48 * q + 48, :]
    out[:, BIAS_TWO:] = jnp.zeros((48, 128), BF)


def pack(kernel, name, lanes, *values):
    def once(shape):
        return pl.BlockSpec(shape, lambda j: (0,) * len(shape))

    return pl.pallas_call(
        kernel,
        grid=(1,),
        in_specs=[once(value.shape) for value in values],
        out_specs=once((48, lanes)),
        out_shape=pltpu.VMEM((48, lanes), BF),
        compiler_params=pltpu.CompilerParams(vmem_limit_bytes=8 * MIB),
        name=name,
    )(*map(far, values))


def joined(info, mine, other):
    first = info[3] == 0
    mine, other = mine[...].astype(F32), other[...].astype(F32)
    return jnp.concatenate([jnp.where(first, mine, other), jnp.where(first, other, mine)], axis=1)


def unpack_two_kernel(info, mine, other, g_mod, g_proj, g_up, g_down, bias):
    two = joined(info, mine, other)
    g_mod[:, MOD_ONE:] = two[:, AT_MOD:AT_PROJ]
    g_proj[...] = two[:, AT_PROJ:AT_DOWN]
    g_up[...] = two[:, :FF]
    for q in range(4):
        g_down[48 * q : 48 * q + 48, :] = two[:, AT_DOWN + D * q : AT_DOWN + D * q + D]
    bias[...] = two[:, BIAS_TWO:]


def unpack_one_kernel(
    info, mine, other, bias_two, _, g_mod, g_mod_bias, g_qkv, g_qv_bias, g_proj_bias, g_up_bias,
    g_down_bias,
):
    shard = info[1] + 4 * info[2]
    one = joined(info, mine, other)
    g_mod[...] = one[:, QKV_W:BIAS_ONE]
    g_qkv[...] = one[:, :QKV_W]
    bias = one[:, BIAS_ONE:] + bias_two[...]

    def own(row, size, out):
        row = jnp.broadcast_to(row, (8, row.shape[1]))
        turn = lax.rem(8 * size - shard * size, 8 * size)
        out[...] = pltpu.roll(row, turn, 1)[0:1, :size].reshape(size)

    own(bias_row(bias, ROW_MOD, 18), 288, g_mod_bias)
    own(jnp.concatenate([bias_row(bias, 0, 3), bias_row(bias, 6, 3)], axis=1), 96, g_qv_bias)
    own(bias_row(bias, ROW_PROJ, 3), 48, g_proj_bias)
    own(bias_row(bias, ROW_UP, 12), 192, g_up_bias)
    own(bias_row(bias, ROW_DOWN, 3), 48, g_down_bias)


def finish(info, one, two):
    scalars = pl.BlockSpec(memory_space=pltpu.SMEM)
    shapes = [(48, 6 * D), (48, D), (48, FF), (192, D), (48, 128)]
    g_mod, g_proj, g_up, g_down, bias_two = pl.pallas_call(
        unpack_two_kernel,
        in_specs=[scalars] + [held()] * 2,
        out_shape=[jax.ShapeDtypeStruct(shape, F32) for shape in shapes],
        compiler_params=pltpu.CompilerParams(vmem_limit_bytes=12 * MIB),
        name="unpack_second_batch",
    )(info, *two)
    shapes = [(48, 6 * D), (288,), (48, QKV_W), (96,), (48,), (192,), (48,)]

    def once(shape):
        return pl.BlockSpec(shape, lambda j: (0,) * len(shape))

    g_mod, g_mod_bias, g_qkv, g_qv_bias, g_proj_bias, g_up_bias, g_down_bias = pl.pallas_call(
        unpack_one_kernel,
        grid=(1,),
        in_specs=[scalars] + [held()] * 3 + [pl.BlockSpec(memory_space=pl.ANY)],
        out_specs=[once((48, MOD_ONE))] + [once(shape) for shape in shapes[1:]],
        out_shape=[jax.ShapeDtypeStruct(shape, F32) for shape in shapes],
        input_output_aliases={4: 0},
        compiler_params=pltpu.CompilerParams(vmem_limit_bytes=8 * MIB),
        name="unpack_first_batch",
    )(info, *one, bias_two, g_mod)
    return (
        g_mod, g_mod_bias, g_qkv, g_qv_bias, g_proj, g_proj_bias, g_up, g_up_bias, g_down,
        g_down_bias,
    )


def on_device(
    latents, conditions, counts, mod_weight, mod_bias, qkv_weight, qv_bias, proj_weight,
    proj_bias, up_weight, up_bias, down_weight, down_bias, grad_out,
):
    shard = lax.axis_index("shard")
    rep = lax.axis_index("rep")
    info = jnp.stack([counts[0], shard % 4, shard // 4, rep % 2]).astype(jnp.int32)
    block_one = pack(
        pack_one_kernel, "pack_attention_weights", LANES_ONE,
        after(qkv_weight, info), mod_weight, qv_bias, mod_bias, proj_bias, up_bias, down_bias,
    )
    block_two = pack(
        pack_two_kernel, "pack_feed_forward_weights", LANES_TWO,
        up_weight, mod_weight, proj_weight, down_weight,
    )
    mine_one = fetch_all(block_one)
    mine_two = [move(block_two, fetch(0))]
    other_one = swap_all([mine_one[0]] + [after(piece, block_two) for piece in mine_one[1:]])
    block_two = after(block_two, *mine_one)
    mine_two += [move(block_two, fetch(k)) for k in (1, 2, 3)]
    weights, bias, mod, qkv, expo, mixed, rinv, hidden = run_forward(
        info, latents, conditions, mine_one + other_one
    )
    mine_two = [after(piece, mod) for piece in mine_two]
    other_two = swap_all([mine_two[0], mine_two[1], mine_two[3]])
    mine_two[2] = after(mine_two[2], *other_two)
    other_two.insert(2, move(mine_two[2], CORE_SWAP))
    weights_two, out, grad_mid, grad_mixed, grad_mod_two, keep_two, send_two = run_middle(
        info, latents, conditions, mixed, grad_out, bias, mine_two + other_two
    )
    held_two = add_blocks(keep_two, move(send_two, CORE_SWAP))
    arrived_two = scatter(held_two)
    grad_latents, grad_cond, keep_one, send_one = run_backward(
        info, latents, conditions, qkv, expo, mixed, rinv, hidden, grad_mid, grad_mixed, mod,
        weights, weights_two, after(grad_mod_two, held_two[0]),
    )
    held_one = add_blocks(keep_one, move(after(send_one, *arrived_two), CORE_SWAP))
    arrived_one = scatter(held_one)
    two = sum_replicas(arrived_two, info, *held_one)
    one = sum_replicas(arrived_one, info)
    return (out, grad_latents, grad_cond, *finish(info, one, two))


def solution(mesh):
    slots = P(("shard", "rep"), None, None)
    rows = P(("shard", "rep"), None)
    matrix, vector = P("shard", None), P("shard")
    in_specs = (slots, rows, P(("shard", "rep"))) + (matrix, vector) * 5 + (slots,)
    out_specs = (slots, slots, rows) + (matrix, vector) * 5
    return jax.shard_map(
        on_device, mesh=mesh, in_specs=in_specs, out_specs=out_specs, check_vma=False
    )
```

```python
import functools

import jax
import jax.numpy as jnp
from jax import lax
from jax.experimental import pallas as pl
from jax.experimental.pallas import tpu as pltpu
from jax.sharding import PartitionSpec as P

D = 384
HEADS = 6
HEAD_DIM = 64
FF = 1536
TOK = 256
CAP = 8
PAIR = 2
QUAD = 4
CHUNK = 768
STEPS = CAP // PAIR
TWIN = 128
BF = jnp.bfloat16
F32 = jnp.float32
MIB = 1024 * 1024

LANES_ONE = 2048
QKV_W = 3 * D
MOD_ONE = 2 * D
BIAS_ONE = QKV_W + MOD_ONE
LANES_TWO = 5120
MOD_TWO = 4 * D
AT_MOD = FF
AT_PROJ = AT_MOD + MOD_TWO
AT_DOWN = AT_PROJ + D
BIAS_TWO = AT_DOWN + FF
LANES_SENT = BIAS_TWO
ROW_QKV, ROW_MOD, ROW_PROJ, ROW_UP, ROW_DOWN = 0, 9, 27, 30, 42


def dot(left, right):
    return jnp.dot(left, right, preferred_element_type=F32)


def dot_tn(left, right):
    return lax.dot_general(left, right, (((0,), (0,)), ((), ())), preferred_element_type=F32)


def dot_nt(left, right):
    return lax.dot_general(left, right, (((1,), (1,)), ((), ())), preferred_element_type=F32)


def normalize(value):
    center = jnp.mean(value, axis=-1, keepdims=True)
    centered = value - center
    spread = jnp.mean(centered * centered, axis=-1, keepdims=True)
    inverse = lax.rsqrt(spread + 1e-06)
    return centered * inverse, inverse


def norm_back(grad, normed, inverse):
    first = jnp.mean(grad, axis=-1, keepdims=True)
    second = jnp.mean(grad * normed, axis=-1, keepdims=True)
    return inverse * (grad - first - normed * second)


def spread(rows, size):
    width = 8 * size
    lane = lax.broadcasted_iota(jnp.int32, (8, width), 1)
    total = jnp.zeros((8, width), F32)
    for owner, row in enumerate(rows):
        padded = jnp.concatenate([row, jnp.zeros((1, width - row.shape[1]), F32)], axis=1)
        padded = jnp.where(lane < size, jnp.broadcast_to(padded, (8, width)), 0.0)
        total += pltpu.roll(padded, owner * size, 1) if owner else padded
    return total[0:1]


def all_biases(raw):
    def rows(first, count):
        return [
            jnp.concatenate([block[first + i : first + i + 1] for i in range(count)], axis=1)
            for block in raw
        ]

    qv = spread(rows(0, 1), 96)
    full = [qv[:, :D], jnp.zeros((1, D), F32), qv[:, D:]]
    full += [spread(rows(1, 3), 288), spread(rows(4, 1), 48)]
    full += [spread(rows(5, 2), 192), spread(rows(7, 1), 48)]
    full = jnp.concatenate(full, axis=1)
    cut = [full[:, 128 * i : 128 * i + 128] for i in range(45)]
    return jnp.concatenate(cut + [jnp.zeros((3, 128), F32)], axis=0)


def by_head(value, low):
    zero = jnp.zeros_like(value)
    return jnp.concatenate([jnp.where(low, value, zero), jnp.where(low, zero, value)], axis=0)


def bias_row(bias, first, count):
    return jnp.concatenate([bias[first + i : first + i + 1, :] for i in range(count)], axis=1)


def silu(cond):
    return cond * (1.0 / (1.0 + jnp.exp(-cond)))


def assemble(info, pieces, full):
    column, z_high, core = info[1], info[2], info[3]
    for k in range(4):
        spot = lax.rem(column + k, 4) * 48
        mine = (z_high ^ core) * 192 + spot
        other = (1 - (z_high ^ core)) * 192 + spot
        full[pl.ds(pl.multiple_of(mine, 16), 48), :] = pieces[k][...]
        full[pl.ds(pl.multiple_of(other, 16), 48), :] = pieces[4 + k][...]


def forward_kernel(
    info, latents, conditions, p0, p1, p2, p3, p4, p5, p6, p7,
    weights, bias_out, mod_out, qkv_out, expo_out, mixed_out, rinv_out, hidden_out,
):
    step = pl.program_id(0)

    @pl.when(step == 0)
    def _():
        assemble(info, (p0, p1, p2, p3, p4, p5, p6, p7), weights)
        total = all_biases(
            [
                weights[48 * k : 48 * k + 16, BIAS_ONE : BIAS_ONE + 128].astype(F32)[:8]
                for k in range(8)
            ]
        )
        bias_out[...] = total
        cond_low = silu(conditions[...].astype(F32)).astype(BF)
        mod_out[...] = dot(cond_low, weights[:, QKV_W : QKV_W + MOD_ONE]) + bias_row(
            total, ROW_MOD, 6
        )

    @pl.when(QUAD * step < info[0])
    def _():
        hidden = []
        for i in range(QUAD):
            mod = mod_out[pl.ds(QUAD * step + i, 1), :]
            normed, _ = normalize(latents[i].astype(F32))
            hidden.append((normed * (1.0 + mod[:, D : 2 * D]) + mod[:, :D]).astype(BF))
            hidden_out[QUAD * step + i] = hidden[i]
        full_bias = bias_row(bias_out[0:16, :], ROW_QKV, 9)
        qkv_all = dot(jnp.concatenate(hidden, axis=0), weights[:, :QKV_W])
        qkv_all = (qkv_all + full_bias).astype(BF)
        low = lax.broadcasted_iota(jnp.int32, (TOK, 128), 1) < HEAD_DIM
        for i in range(QUAD):
            slot = QUAD * step + i
            qkv = qkv_all[TOK * i : TOK * i + TOK]
            qkv_out[slot] = qkv
            for pair in range(HEADS // 2):
                at = 128 * pair
                query = qkv[:, at : at + 128] * jnp.asarray(HEAD_DIM**-0.5, BF)
                value = qkv[:, 2 * D + at : 2 * D + at + 128]
                scores = dot_nt(query, by_head(qkv[:, D + at : D + at + 128], low))
                expo = jnp.concatenate(
                    [
                        jnp.exp(part - jnp.max(part, axis=-1, keepdims=True)).astype(BF)
                        for part in (scores[:, :TOK], scores[:, TOK:])
                    ],
                    axis=1,
                )
                expo_out[slot, pair] = expo
                sums = by_head(jnp.ones((TOK, 128), BF), low)
                both = dot(expo, jnp.concatenate([by_head(value, low), sums], axis=1))
                inverse = 1.0 / both[:, 128:]
                rinv_out[slot, :, at : at + 128] = inverse
                mixed_out[slot, :, at : at + 128] = (both[:, :128] * inverse).astype(BF)


def middle_kernel(
    info, latents, conditions, mixed_in, grad_out, bias_in, p0, p1, p2, p3, p4, p5, p6, p7,
    weights, out, grad_mid_out, grad_mixed_out, grad_mod, keep, send,
    mod, acc_up, acc_down, acc_proj, acc_bias, down,
):
    step = pl.program_id(0)

    @pl.when(step == 0)
    def _():
        pieces = (p0, p1, p2, p3, p4, p5, p6, p7)
        assemble(info, [piece.at[:, :AT_DOWN] for piece in pieces], weights)
        column, z_high, core = info[1], info[2], info[3]
        for k in range(8):
            layer = (z_high ^ core) if k < 4 else 1 - (z_high ^ core)
            first = layer * 768 + lax.rem(column + k % 4, 4) * 192
            for q in range(4):
                down[pl.ds(pl.multiple_of(first + 48 * q, 16), 48), :] = pieces[k][
                    :, AT_DOWN + D * q : AT_DOWN + D * q + D
                ]
        cond_low = silu(conditions[...].astype(F32)).astype(BF)
        mod[...] = dot(cond_low, weights[:, AT_MOD : AT_MOD + MOD_TWO]) + bias_row(
            bias_in[...], ROW_MOD + 6, 12
        )
        acc_bias[...] = jnp.zeros_like(acc_bias)
        grad_mod[...] = jnp.zeros_like(grad_mod)

    @pl.when((step == 0) & (info[0] == 0))
    def _():
        acc_up[...] = jnp.zeros_like(acc_up)
        acc_down[...] = jnp.zeros_like(acc_down)
        acc_proj[...] = jnp.zeros_like(acc_proj)

    @pl.when(PAIR * step >= info[0])
    def _():
        out[...] = jnp.zeros((PAIR, TOK, D), BF)
        grad_mid_out[pl.ds(PAIR * step, PAIR)] = jnp.zeros((PAIR, TOK, D), F32)
        grad_mixed_out[pl.ds(PAIR * step, PAIR)] = jnp.zeros((PAIR, TOK, D), BF)

    @pl.when(PAIR * step < info[0])
    def _():
        def so_far(total):
            return jnp.where(step == 0, 0.0, total)

        bias = bias_in[...]
        w_proj = weights[:, AT_PROJ : AT_PROJ + D]
        up_bias = bias_row(bias, ROW_UP, 12)
        mixed = mixed_in[pl.ds(PAIR * step, PAIR)].reshape(PAIR * TOK, D)
        branch_all = dot(mixed, w_proj) + bias_row(bias, ROW_PROJ, 3)
        rows = [mod[pl.ds(PAIR * step + i, 1), :] for i in range(PAIR)]
        span = [slice(TOK * i, TOK * i + TOK) for i in range(PAIR)]
        middle, normed, inverse, hidden, cot, g_two = [], [], [], [], [], []
        for i in range(PAIR):
            row = rows[i]
            middle.append(latents[i].astype(F32) + row[:, :D] * branch_all[span[i]])
            value, scale = normalize(middle[i])
            normed.append(value)
            inverse.append(scale)
            hidden.append((value * (1.0 + row[:, 2 * D : 3 * D]) + row[:, D : 2 * D]).astype(BF))
            held = (PAIR * step + i < info[0]).astype(F32)
            cot.append(grad_out[i].astype(F32) * held)
            g_two.append((cot[i] * row[:, 3 * D :]).astype(BF))
        hidden = jnp.concatenate(hidden, axis=0)
        g_two = jnp.concatenate(g_two, axis=0)
        branch_two = bias_row(bias, ROW_DOWN, 3)
        d_hidden = jnp.zeros((PAIR * TOK, D), F32)
        root = 0.7978845608028654
        cube = root * 0.044715
        for chunk in range(FF // CHUNK):
            at = CHUNK * chunk
            w_up = weights[:, at : at + CHUNK]
            w_down = down[at : at + CHUNK, :]
            upward = dot(hidden, w_up) + up_bias[:, at : at + CHUNK]
            square = upward * upward
            bend = jnp.tanh(upward * (root + cube * square))
            half = 0.5 + 0.5 * bend
            act = upward * half
            slope = half + act * (1.0 - bend) * (root + (3.0 * cube) * square)
            act_low = act.astype(BF)
            branch_two = branch_two + dot(act_low, w_down)
            acc_down[at : at + CHUNK, :] = so_far(acc_down[at : at + CHUNK, :]) + dot_tn(act_low, g_two)
            g_up = (slope * dot_nt(g_two, w_down)).astype(BF)
            acc_up[:, at : at + CHUNK] = so_far(acc_up[:, at : at + CHUNK]) + dot_tn(hidden, g_up)
            acc_bias[0:1, at : at + CHUNK] += jnp.sum(g_up.astype(F32), axis=0, keepdims=True)
            d_hidden = d_hidden + dot_nt(g_up, w_up)
        acc_bias[1:2, :D] += jnp.sum(g_two.astype(F32), axis=0, keepdims=True)
        g_one = []
        for i in range(PAIR):
            row, slot = rows[i], PAIR * step + i
            d_hid, br_two = d_hidden[span[i]], branch_two[span[i]]
            held = (slot < info[0]).astype(F32)
            out[i] = ((middle[i] + row[:, 3 * D :] * br_two) * held).astype(BF)
            grad_mod[pl.ds(slot, 1), 3 * D :] = jnp.sum(cot[i] * br_two, axis=0, keepdims=True)
            grad_mod[pl.ds(slot, 1), D : 2 * D] = jnp.sum(d_hid, axis=0, keepdims=True)
            grad_mod[pl.ds(slot, 1), 2 * D : 3 * D] = jnp.sum(
                d_hid * normed[i], axis=0, keepdims=True
            )
            grad_mid = cot[i] + norm_back(
                d_hid * (1.0 + row[:, 2 * D : 3 * D]), normed[i], inverse[i]
            )
            grad_mid_out[slot] = grad_mid
            grad_mod[pl.ds(slot, 1), :D] = jnp.sum(
                grad_mid * branch_all[span[i]], axis=0, keepdims=True
            )
            g_one.append((grad_mid * row[:, :D]).astype(BF))
        g_one = jnp.concatenate(g_one, axis=0)
        acc_bias[2:3, :D] += jnp.sum(g_one.astype(F32), axis=0, keepdims=True)
        acc_proj[...] = so_far(acc_proj[...]) + dot_tn(mixed, g_one)
        grad_mixed_out[pl.ds(PAIR * step, PAIR)] = (
            dot_nt(g_one, w_proj).astype(BF).reshape(PAIR, TOK, D)
        )

    @pl.when(step == STEPS - 1)
    def _():
        cond_low = silu(conditions[...].astype(F32)).astype(BF)
        g_mod = grad_mod[...].astype(BF)
        mod_grad = dot_tn(cond_low.astype(F32), g_mod.astype(F32)).astype(BF)
        z_high, core, column = info[2], info[3], info[1]
        sums = jnp.sum(g_mod.astype(F32), axis=0, keepdims=True)
        rows = [jnp.zeros((ROW_MOD + 6, 128), F32)]
        rows += [sums[:, 128 * i : 128 * i + 128] for i in range(12)]
        rows += [acc_bias[2:3, 128 * i : 128 * i + 128] for i in range(3)]
        rows += [acc_bias[0:1, 128 * i : 128 * i + 128] for i in range(12)]
        rows += [acc_bias[1:2, 128 * i : 128 * i + 128] for i in range(3)]
        rows += [jnp.zeros((3, 128), F32)]
        bias_block = jnp.concatenate(rows, axis=0).astype(BF)
        for owner in range(8):
            zh, xx = owner // 4, owner % 4
            spot = lax.rem(xx - column + 4, 4) * 48
            spot = pl.multiple_of(spot, 16)
            is_mine = (z_high ^ core) == zh
            lo = 48 * owner

            def put(ref, spot=spot, lo=lo, owner=owner):
                ref[pl.ds(spot, 48), :FF] = acc_up[lo : lo + 48, :].astype(BF)
                ref[pl.ds(spot, 48), AT_MOD : AT_MOD + MOD_TWO] = mod_grad[lo : lo + 48, :]
                ref[pl.ds(spot, 48), AT_PROJ : AT_PROJ + D] = acc_proj[lo : lo + 48, :].astype(BF)
                for q in range(4):
                    at = 192 * owner + 48 * q
                    ref[pl.ds(spot, 48), AT_DOWN + D * q : AT_DOWN + D * q + D] = acc_down[
                        at : at + 48, :
                    ].astype(BF)
                ref[pl.ds(spot, 48), BIAS_TWO : BIAS_TWO + 128] = bias_block

            pl.when(is_mine)(functools.partial(put, keep))
            pl.when(jnp.logical_not(is_mine))(functools.partial(put, send))


def backward_kernel(
    info, latents, conditions, qkv_in, expo_in, mixed_in, rinv_in, hidden_in, grad_mid_in,
    grad_mixed_in, mod_in, weights, weights_two, grad_mod_two,
    out, grad_cond, keep, send,
    acc_qkv, acc_bias, grad_mod,
):
    step = pl.program_id(0)
    slot = QUAD * step

    @pl.when(step == 0)
    def _():
        acc_qkv[...] = jnp.zeros_like(acc_qkv)
        acc_bias[...] = jnp.zeros_like(acc_bias)
        grad_mod[...] = jnp.zeros_like(grad_mod)

    @pl.when(slot >= info[0])
    def _():
        out[...] = jnp.zeros((QUAD, TOK, D), BF)

    @pl.when(slot < info[0])
    def _():
        low = lax.broadcasted_iota(jnp.int32, (TOK, 128), 1) < HEAD_DIM
        factor = HEAD_DIM**-0.5
        g_all = []
        for i in range(QUAD):
            qkv = qkv_in[slot + i]
            scaled = (grad_mixed_in[slot + i].astype(F32) * rinv_in[slot + i]).astype(BF)
            product = scaled.astype(F32) * mixed_in[slot + i].astype(F32)
            g_query, g_key, g_value = [], [], []
            for pair in range(HEADS // 2):
                at = 128 * pair
                query = qkv[:, at : at + 128]
                key = by_head(qkv[:, D + at : D + at + 128], low)
                value = by_head(qkv[:, 2 * D + at : 2 * D + at + 128], low)
                grad = scaled[:, at : at + 128]
                weighed = product[:, at : at + 128]
                expo = expo_in[slot + i, pair]
                g_probs = dot_nt(grad, value)
                g_scores = []
                for half in range(2):
                    mask = low if half == 0 else ~low
                    delta = jnp.sum(jnp.where(mask, weighed, 0.0), axis=-1, keepdims=True)
                    lanes = slice(TOK * half, TOK * half + TOK)
                    g_scores.append(
                        (expo[:, lanes].astype(F32) * (g_probs[:, lanes] - delta)).astype(BF)
                    )
                g_scores = jnp.concatenate(g_scores, axis=1)
                d_key, d_value = dot_tn(g_scores, query), dot_tn(expo, grad)
                g_query.append((dot(g_scores, key) * factor).astype(BF))
                g_key.append((jnp.where(low, d_key[:TOK], d_key[TOK:]) * factor).astype(BF))
                g_value.append(jnp.where(low, d_value[:TOK], d_value[TOK:]).astype(BF))
            g_all.append(jnp.concatenate(g_query + g_key + g_value, axis=1))
        g_qkv = jnp.concatenate(g_all, axis=0)
        hidden = hidden_in[pl.ds(slot, QUAD)].reshape(QUAD * TOK, D)
        acc_qkv[...] += dot_tn(hidden, g_qkv)
        acc_bias[0:1, :] += jnp.sum(g_qkv.astype(F32), axis=0, keepdims=True)
        d_all = dot_nt(g_qkv, weights[:, :QKV_W])
        for i in range(QUAD):
            row = mod_in[pl.ds(slot + i, 1), :]
            normed, inverse = normalize(latents[i].astype(F32))
            d_hidden = d_all[TOK * i : TOK * i + TOK]
            grad_mod[pl.ds(slot + i, 1), :D] = jnp.sum(d_hidden, axis=0, keepdims=True)
            grad_mod[pl.ds(slot + i, 1), D:] = jnp.sum(d_hidden * normed, axis=0, keepdims=True)
            back = norm_back(d_hidden * (1.0 + row[:, D : 2 * D]), normed, inverse)
            out[i] = (grad_mid_in[slot + i] + back).astype(BF)

    @pl.when(step == CAP // QUAD - 1)
    def _():
        cond = conditions[...].astype(F32)
        sig = 1.0 / (1.0 + jnp.exp(-cond))
        cond_low = (cond * sig).astype(BF)
        g_mod = grad_mod[...].astype(BF)
        g_mod_two = grad_mod_two[...].astype(BF)
        g_cond = dot_nt(g_mod, weights[:, QKV_W : QKV_W + MOD_ONE])
        g_cond += dot_nt(g_mod_two, weights_two[:, AT_MOD : AT_MOD + MOD_TWO])
        grad_cond[...] = (g_cond * (sig * (1.0 + cond * (1.0 - sig)))).astype(BF)
        mod_grad = dot_tn(cond_low.astype(F32), g_mod.astype(F32)).astype(BF)
        sums = jnp.sum(g_mod.astype(F32), axis=0, keepdims=True)
        rows = [acc_bias[0:1, 128 * i : 128 * i + 128] for i in range(9)]
        rows += [sums[:, 128 * i : 128 * i + 128] for i in range(6)]
        rows += [jnp.zeros((33, 128), F32)]
        bias_block = jnp.concatenate(rows, axis=0).astype(BF)
        z_high, core, column = info[2], info[3], info[1]
        for owner in range(8):
            zh, xx = owner // 4, owner % 4
            spot = pl.multiple_of(lax.rem(xx - column + 4, 4) * 48, 16)
            is_mine = (z_high ^ core) == zh
            lo = 48 * owner

            def put(ref, spot=spot, lo=lo):
                ref[pl.ds(spot, 48), :QKV_W] = acc_qkv[lo : lo + 48, :].astype(BF)
                ref[pl.ds(spot, 48), QKV_W : QKV_W + MOD_ONE] = mod_grad[lo : lo + 48, :]
                ref[pl.ds(spot, 48), BIAS_ONE : BIAS_ONE + 128] = bias_block

            pl.when(is_mine)(functools.partial(put, keep))
            pl.when(jnp.logical_not(is_mine))(functools.partial(put, send))


def slot_spec(group):
    def index(j, info):
        return (jnp.minimum(j, jnp.maximum((info[0] + group - 1) // group - 1, 0)), 0, 0)

    return pl.BlockSpec((group, TOK, D), index)


def slot_out(group):
    return pl.BlockSpec((group, TOK, D), lambda j, info: (j, 0, 0))


def held():
    return pl.BlockSpec(memory_space=pltpu.VMEM)


def whole(*shape):
    zeros = (0,) * len(shape)
    return pl.BlockSpec(shape, lambda j, info: zeros)


def params(mib):
    return pltpu.CompilerParams(
        dimension_semantics=("arbitrary",), vmem_limit_bytes=mib * MIB
    )


def far(value):
    return pltpu.with_memory_space_constraint(value, pltpu.HBM)


def stay(value):
    return pltpu.with_memory_space_constraint(value, pltpu.VMEM)


def run_forward(info, latents, conditions, pieces):
    return pl.pallas_call(
        forward_kernel,
        grid_spec=pltpu.PrefetchScalarGridSpec(
            num_scalar_prefetch=1,
            grid=(CAP // QUAD,),
            in_specs=[slot_spec(QUAD), whole(CAP, D)] + [held()] * 8,
            out_specs=[held()] * 8,
        ),
        out_shape=[
            pltpu.VMEM((D, LANES_ONE), BF),
            pltpu.VMEM((48, 128), F32),
            pltpu.VMEM((CAP, MOD_ONE), F32),
            pltpu.VMEM((CAP, TOK, QKV_W), BF),
            pltpu.VMEM((CAP, HEADS // 2, TOK, 2 * TOK), BF),
            pltpu.VMEM((CAP, TOK, D), BF),
            pltpu.VMEM((CAP, TOK, D), F32),
            pltpu.VMEM((CAP, TOK, D), BF),
        ],
        compiler_params=params(12),
        name="attention_forward",
        cost_estimate=pl.CostEstimate(
            flops=3_000_000_000, bytes_accessed=20_000_000, transcendentals=3_000_000
        ),
    )(info, far(latents), far(conditions), *pieces)


def run_middle(info, latents, conditions, mixed, grad_out, bias, pieces):
    return pl.pallas_call(
        middle_kernel,
        grid_spec=pltpu.PrefetchScalarGridSpec(
            num_scalar_prefetch=1,
            grid=(CAP // PAIR,),
            in_specs=[
                slot_spec(PAIR),
                whole(CAP, D),
                held(),
                slot_spec(PAIR),
                held(),
            ]
            + [held()] * 8,
            out_specs=[held(), slot_out(PAIR)] + [held()] * 5,
            scratch_shapes=[
                pltpu.VMEM((CAP, MOD_TWO), F32),
                pltpu.VMEM((D, FF), F32),
                pltpu.VMEM((FF, D), F32),
                pltpu.VMEM((D, D), F32),
                pltpu.VMEM((8, FF), F32),
                pltpu.VMEM((FF, D), BF),
            ],
        ),
        out_shape=[
            pltpu.VMEM((D, AT_DOWN), BF),
            jax.ShapeDtypeStruct((CAP, TOK, D), BF),
            pltpu.VMEM((CAP, TOK, D), F32),
            pltpu.VMEM((CAP, TOK, D), BF),
            pltpu.VMEM((CAP, MOD_TWO), F32),
            pltpu.VMEM((192, LANES_TWO), BF),
            pltpu.VMEM((192, LANES_TWO), BF),
        ],
        compiler_params=params(23),
        name="feed_forward_both_ways",
        cost_estimate=pl.CostEstimate(
            flops=16_000_000_000, bytes_accessed=30_000_000, transcendentals=3_000_000
        ),
    )(info, far(latents), far(conditions), stay(mixed), far(grad_out), stay(bias), *pieces)


def run_backward(info, latents, conditions, *values):
    return pl.pallas_call(
        backward_kernel,
        grid_spec=pltpu.PrefetchScalarGridSpec(
            num_scalar_prefetch=1,
            grid=(CAP // QUAD,),
            in_specs=[slot_spec(QUAD), whole(CAP, D)] + [held()] * 11,
            out_specs=[slot_out(QUAD), whole(CAP, D), held(), held()],
            scratch_shapes=[
                pltpu.VMEM((D, QKV_W), F32),
                pltpu.VMEM((8, QKV_W), F32),
                pltpu.VMEM((CAP, MOD_ONE), F32),
            ],
        ),
        out_shape=[
            jax.ShapeDtypeStruct((CAP, TOK, D), BF),
            jax.ShapeDtypeStruct((CAP, D), BF),
            pltpu.VMEM((192, LANES_ONE), BF),
            pltpu.VMEM((192, LANES_ONE), BF),
        ],
        compiler_params=params(12),
        name="attention_backward",
        cost_estimate=pl.CostEstimate(
            flops=25_000_000_000, bytes_accessed=20_000_000, transcendentals=1_000
        ),
    )(info, far(latents), far(conditions), *map(stay, values))


def place(index):
    shard, rep = divmod(index, 16)
    return shard // 4, shard % 4, rep // 4, (rep // 2) % 2, rep % 2


def index_of(z_high, x, y, z_low, core):
    return (z_high * 4 + x) * 16 + y * 4 + z_low * 2 + core


def routes(target_of):
    return [(i, target_of(*place(i))) for i in range(TWIN)]


def fetch(k):
    def source(zh, x, y, zl, c):
        if c == 0:
            return index_of(zh, (x + k) % 4, y, zl, c)
        return index_of(1 - zh, (x + k) % 4, y, 1 - zl, c)

    return [(source(*place(i)), i) for i in range(TWIN)]


CORE_SWAP = routes(lambda zh, x, y, zl, c: index_of(zh, x, y, zl, 1 - c))
ZLOW_SWAP = routes(lambda zh, x, y, zl, c: index_of(zh, x, y, 1 - zl, c))
BOTH = ("shard", "rep")


def move(value, pairs):
    return lax.ppermute(value, BOTH, pairs)


def y_route(k):
    return routes(lambda zh, x, y, zl, c: index_of(zh, x, (y + k) % 4, zl, c))


def after(value, *earlier):
    return lax.optimization_barrier((value, *earlier))[0]


def fetch_all(block):
    return [move(block, fetch(k)) for k in range(4)]


def swap_all(pieces):
    return [move(piece, CORE_SWAP) for piece in pieces]


def small_call(kernel, name, shapes, *values, scalars=False):
    return pl.pallas_call(
        kernel,
        in_specs=[pl.BlockSpec(memory_space=pltpu.SMEM)] * scalars
        + [held()] * (len(values) - scalars),
        out_shape=[jax.ShapeDtypeStruct(shape, BF) for shape in shapes],
        compiler_params=pltpu.CompilerParams(vmem_limit_bytes=14 * MIB),
        name=name,
    )(*values)


def add_kernel(*refs):
    refs[-1][...] = sum(ref[...].astype(F32) for ref in refs[:-1]).astype(BF)


def add(*values):
    return small_call(add_kernel, "add", [values[0].shape], *values)[0]


def add_blocks_kernel(left, right, *outs):
    for k, out in enumerate(outs):
        rows = slice(48 * k, 48 * k + 48)
        out[...] = (left[rows, :].astype(F32) + right[rows, :].astype(F32)).astype(BF)


def add_blocks(left, right):
    shape = (48, left.shape[1])
    return small_call(add_blocks_kernel, "add_blocks", [shape] * 4, left, right)


def add_halves_kernel(info, *refs):
    lanes = refs[-1].shape[1]
    for out, core in ((refs[-2], info[3]), (refs[-1], 1 - info[3])):
        at = pl.ds(pl.multiple_of(core * lanes, 128), lanes)
        out[...] = sum(ref[:, at].astype(F32) for ref in refs[:-2]).astype(BF)


def add_halves(info, pieces):
    shape = (48, pieces[0].shape[1] // 2)
    return small_call(
        add_halves_kernel, "add_halves", [shape] * 2, info, *pieces, scalars=True
    )


def scatter(blocks):
    back = [[(target, source) for source, target in fetch(k)] for k in range(4)]
    return [move(block, pairs) for block, pairs in zip(blocks, back)]


def sum_replicas(arrived, info, *earlier):
    mine, other = add_halves(info, arrived)
    total = add(mine, move(other, CORE_SWAP))
    if earlier:
        total = after(total, *earlier)
    total = add(total, move(total, ZLOW_SWAP))
    total = add(total, *(move(total, y_route(k)) for k in (1, 2, 3)))
    return [total, move(total, CORE_SWAP)]


def row_of(ref):
    size = ref.shape[0]
    row = ref[...].astype(F32).reshape(1, size)
    if size % 128:
        row = jnp.concatenate([row, jnp.zeros((1, -size % 128), F32)], axis=1)
    return row


def pack_one_kernel(qkv, mod, qv_bias, mod_bias, proj_bias, up_bias, down_bias, out):
    out[:, :QKV_W] = qkv[...]
    out[:, QKV_W:BIAS_ONE] = mod[:, :MOD_ONE]
    flat = [row_of(ref) for ref in (qv_bias, mod_bias, proj_bias, up_bias, down_bias)]
    flat = jnp.concatenate(flat, axis=1)
    rows = [flat[:, 128 * i : 128 * i + 128] for i in range(8)] + [jnp.zeros((40, 128), F32)]
    out[:, BIAS_ONE:] = jnp.concatenate(rows, axis=0).astype(BF)


def pack_two_kernel(up, mod, proj, down, out):
    out[:, :FF] = up[...]
    out[:, AT_MOD:AT_PROJ] = mod[:, MOD_ONE:]
    out[:, AT_PROJ:AT_DOWN] = proj[...]
    for q in range(4):
        out[:, AT_DOWN + D * q : AT_DOWN + D * q + D] = down[48 * q : 48 * q + 48, :]


def pack(kernel, name, lanes, *values):
    def once(shape):
        return pl.BlockSpec(shape, lambda j: (0,) * len(shape))

    return pl.pallas_call(
        kernel,
        grid=(1,),
        in_specs=[once(value.shape) for value in values],
        out_specs=once((48, lanes)),
        out_shape=pltpu.VMEM((48, lanes), BF),
        compiler_params=pltpu.CompilerParams(vmem_limit_bytes=8 * MIB),
        name=name,
    )(*map(far, values))


def joined(info, mine, other):
    first = info[3] == 0
    mine, other = mine[...].astype(F32), other[...].astype(F32)
    return jnp.concatenate([jnp.where(first, mine, other), jnp.where(first, other, mine)], axis=1)


def unpack_two_kernel(info, mine, other, g_mod, g_proj, g_up, g_down, bias):
    two = joined(info, mine, other)
    g_mod[:, MOD_ONE:] = two[:, AT_MOD:AT_PROJ]
    g_proj[...] = two[:, AT_PROJ:AT_DOWN]
    g_up[...] = two[:, :FF]
    for q in range(4):
        g_down[48 * q : 48 * q + 48, :] = two[:, AT_DOWN + D * q : AT_DOWN + D * q + D]
    bias[...] = two[:, BIAS_TWO:]


def unpack_one_kernel(
    info, mine, other, bias_two, _, g_mod, g_mod_bias, g_qkv, g_qv_bias, g_proj_bias, g_up_bias,
    g_down_bias,
):
    shard = info[1] + 4 * info[2]
    one = joined(info, mine, other)
    g_mod[...] = one[:, QKV_W:BIAS_ONE]
    g_qkv[...] = one[:, :QKV_W]
    bias = one[:, BIAS_ONE:] + bias_two[...]

    def own(row, size, out):
        row = jnp.broadcast_to(row, (8, row.shape[1]))
        turn = lax.rem(8 * size - shard * size, 8 * size)
        out[...] = pltpu.roll(row, turn, 1)[0:1, :size].reshape(size)

    own(bias_row(bias, ROW_MOD, 18), 288, g_mod_bias)
    own(jnp.concatenate([bias_row(bias, 0, 3), bias_row(bias, 6, 3)], axis=1), 96, g_qv_bias)
    own(bias_row(bias, ROW_PROJ, 3), 48, g_proj_bias)
    own(bias_row(bias, ROW_UP, 12), 192, g_up_bias)
    own(bias_row(bias, ROW_DOWN, 3), 48, g_down_bias)


def finish(info, one, two):
    scalars = pl.BlockSpec(memory_space=pltpu.SMEM)
    shapes = [(48, 6 * D), (48, D), (48, FF), (192, D), (48, 128)]
    g_mod, g_proj, g_up, g_down, bias_two = pl.pallas_call(
        unpack_two_kernel,
        in_specs=[scalars] + [held()] * 2,
        out_shape=[jax.ShapeDtypeStruct(shape, F32) for shape in shapes],
        compiler_params=pltpu.CompilerParams(vmem_limit_bytes=12 * MIB),
        name="unpack_second_batch",
    )(info, *two)
    shapes = [(48, 6 * D), (288,), (48, QKV_W), (96,), (48,), (192,), (48,)]

    def once(shape):
        return pl.BlockSpec(shape, lambda j: (0,) * len(shape))

    g_mod, g_mod_bias, g_qkv, g_qv_bias, g_proj_bias, g_up_bias, g_down_bias = pl.pallas_call(
        unpack_one_kernel,
        grid=(1,),
        in_specs=[scalars] + [held()] * 3 + [pl.BlockSpec(memory_space=pl.ANY)],
        out_specs=[once((48, MOD_ONE))] + [once(shape) for shape in shapes[1:]],
        out_shape=[jax.ShapeDtypeStruct(shape, F32) for shape in shapes],
        input_output_aliases={4: 0},
        compiler_params=pltpu.CompilerParams(vmem_limit_bytes=8 * MIB),
        name="unpack_first_batch",
    )(info, *one, bias_two, g_mod)
    return (
        g_mod, g_mod_bias, g_qkv, g_qv_bias, g_proj, g_proj_bias, g_up, g_up_bias, g_down,
        g_down_bias,
    )


def on_device(
    latents, conditions, counts, mod_weight, mod_bias, qkv_weight, qv_bias, proj_weight,
    proj_bias, up_weight, up_bias, down_weight, down_bias, grad_out,
):
    shard = lax.axis_index("shard")
    rep = lax.axis_index("rep")
    info = jnp.stack([counts[0], shard % 4, shard // 4, rep % 2]).astype(jnp.int32)
    block_one = pack(
        pack_one_kernel, "pack_attention_weights", LANES_ONE,
        after(qkv_weight, info), mod_weight, qv_bias, mod_bias, proj_bias, up_bias, down_bias,
    )
    block_two = pack(
        pack_two_kernel, "pack_feed_forward_weights", LANES_SENT,
        up_weight, mod_weight, proj_weight, down_weight,
    )
    mine_one = fetch_all(block_one)
    mine_two = [move(block_two, fetch(0))]
    other_one = swap_all([mine_one[0]] + [after(piece, block_two) for piece in mine_one[1:]])
    block_two = after(block_two, *mine_one)
    mine_two += [move(block_two, fetch(k)) for k in (1, 2, 3)]
    weights, bias, mod, qkv, expo, mixed, rinv, hidden = run_forward(
        info, latents, conditions, mine_one + other_one
    )
    mine_two = [after(piece, mod) for piece in mine_two]
    other_two = swap_all(mine_two)
    weights_two, out, grad_mid, grad_mixed, grad_mod_two, keep_two, send_two = run_middle(
        info, latents, conditions, mixed, grad_out, bias, mine_two + other_two
    )
    held_two = add_blocks(keep_two, move(send_two, CORE_SWAP))
    arrived_two = scatter(held_two)
    grad_latents, grad_cond, keep_one, send_one = run_backward(
        info, latents, conditions, qkv, expo, mixed, rinv, hidden, grad_mid, grad_mixed, mod,
        weights, weights_two, after(grad_mod_two, held_two[0]),
    )
    held_one = add_blocks(keep_one, move(after(send_one, *arrived_two), CORE_SWAP))
    arrived_one = scatter(held_one)
    two = sum_replicas(arrived_two, info, *held_one)
    one = sum_replicas(arrived_one, info)
    return (out, grad_latents, grad_cond, *finish(info, one, two))


def solution(mesh):
    slots = P(("shard", "rep"), None, None)
    rows = P(("shard", "rep"), None)
    matrix, vector = P("shard", None), P("shard")
    in_specs = (slots, rows, P(("shard", "rep"))) + (matrix, vector) * 5 + (slots,)
    out_specs = (slots, slots, rows) + (matrix, vector) * 5
    return jax.shard_map(
        on_device, mesh=mesh, in_specs=in_specs, out_specs=out_specs, check_vma=False
    )
```

```python
import functools

import jax
import jax.numpy as jnp
from jax import lax
from jax.experimental import pallas as pl
from jax.experimental.pallas import tpu as pltpu
from jax.sharding import PartitionSpec as P

D = 384
HEADS = 6
HEAD_DIM = 64
FF = 1536
TOK = 256
CAP = 8
PAIR = 2
QUAD = 4
CHUNK = 768
STEPS = CAP // PAIR
TWIN = 128
BF = jnp.bfloat16
F32 = jnp.float32
MIB = 1024 * 1024

LANES_ONE = 2048
QKV_W = 3 * D
MOD_ONE = 2 * D
BIAS_ONE = QKV_W + MOD_ONE
LANES_TWO = 5120
MOD_TWO = 4 * D
AT_MOD = FF
AT_PROJ = AT_MOD + MOD_TWO
AT_DOWN = AT_PROJ + D
BIAS_TWO = AT_DOWN + FF
LANES_SENT = BIAS_TWO
ROW_QKV, ROW_MOD, ROW_PROJ, ROW_UP, ROW_DOWN = 0, 9, 27, 30, 42


def dot(left, right):
    return jnp.dot(left, right, preferred_element_type=F32)


def dot_tn(left, right):
    return lax.dot_general(left, right, (((0,), (0,)), ((), ())), preferred_element_type=F32)


def dot_nt(left, right):
    return lax.dot_general(left, right, (((1,), (1,)), ((), ())), preferred_element_type=F32)


def normalize(value):
    center = jnp.mean(value, axis=-1, keepdims=True)
    centered = value - center
    spread = jnp.mean(centered * centered, axis=-1, keepdims=True)
    inverse = lax.rsqrt(spread + 1e-06)
    return centered * inverse, inverse


def norm_back(grad, normed, inverse):
    first = jnp.mean(grad, axis=-1, keepdims=True)
    second = jnp.mean(grad * normed, axis=-1, keepdims=True)
    return inverse * (grad - first - normed * second)


def spread(rows, size):
    width = 8 * size
    lane = lax.broadcasted_iota(jnp.int32, (8, width), 1)
    total = jnp.zeros((8, width), F32)
    for owner, row in enumerate(rows):
        padded = jnp.concatenate([row, jnp.zeros((1, width - row.shape[1]), F32)], axis=1)
        padded = jnp.where(lane < size, jnp.broadcast_to(padded, (8, width)), 0.0)
        total += pltpu.roll(padded, owner * size, 1) if owner else padded
    return total[0:1]


def all_biases(raw):
    def rows(first, count):
        return [
            jnp.concatenate([block[first + i : first + i + 1] for i in range(count)], axis=1)
            for block in raw
        ]

    qv = spread(rows(0, 1), 96)
    full = [qv[:, :D], jnp.zeros((1, D), F32), qv[:, D:]]
    full += [spread(rows(1, 3), 288), spread(rows(4, 1), 48)]
    full += [spread(rows(5, 2), 192), spread(rows(7, 1), 48)]
    full = jnp.concatenate(full, axis=1)
    cut = [full[:, 128 * i : 128 * i + 128] for i in range(45)]
    return jnp.concatenate(cut + [jnp.zeros((3, 128), F32)], axis=0)


def by_head(value, low):
    zero = jnp.zeros_like(value)
    return jnp.concatenate([jnp.where(low, value, zero), jnp.where(low, zero, value)], axis=0)


def bias_row(bias, first, count):
    return jnp.concatenate([bias[first + i : first + i + 1, :] for i in range(count)], axis=1)


def silu(cond):
    return cond * (1.0 / (1.0 + jnp.exp(-cond)))


def assemble(info, pieces, full):
    column, z_high, core = info[1], info[2], info[3]
    for k in range(4):
        spot = lax.rem(column + k, 4) * 48
        mine = (z_high ^ core) * 192 + spot
        other = (1 - (z_high ^ core)) * 192 + spot
        full[pl.ds(pl.multiple_of(mine, 16), 48), :] = pieces[k][...]
        full[pl.ds(pl.multiple_of(other, 16), 48), :] = pieces[4 + k][...]


def forward_kernel(
    info, latents, conditions, p0, p1, p2, p3, p4, p5, p6, p7,
    weights, bias_out, mod_out, qkv_out, expo_out, mixed_out, rinv_out, hidden_out,
):
    step = pl.program_id(0)

    @pl.when(step == 0)
    def _():
        assemble(info, (p0, p1, p2, p3, p4, p5, p6, p7), weights)
        total = all_biases(
            [
                weights[48 * k : 48 * k + 16, BIAS_ONE : BIAS_ONE + 128].astype(F32)[:8]
                for k in range(8)
            ]
        )
        bias_out[...] = total
        cond_low = silu(conditions[...].astype(F32)).astype(BF)
        mod_out[...] = dot(cond_low, weights[:, QKV_W : QKV_W + MOD_ONE]) + bias_row(
            total, ROW_MOD, 6
        )

    @pl.when(QUAD * step < info[0])
    def _():
        hidden = []
        for i in range(QUAD):
            mod = mod_out[pl.ds(QUAD * step + i, 1), :]
            normed, _ = normalize(latents[i].astype(F32))
            hidden.append((normed * (1.0 + mod[:, D : 2 * D]) + mod[:, :D]).astype(BF))
            hidden_out[QUAD * step + i] = hidden[i]
        full_bias = bias_row(bias_out[0:16, :], ROW_QKV, 9)
        qkv_all = dot(jnp.concatenate(hidden, axis=0), weights[:, :QKV_W])
        qkv_all = (qkv_all + full_bias).astype(BF)
        low = lax.broadcasted_iota(jnp.int32, (TOK, 128), 1) < HEAD_DIM
        for i in range(QUAD):
            slot = QUAD * step + i
            qkv = qkv_all[TOK * i : TOK * i + TOK]
            qkv_out[slot] = qkv
            for pair in range(HEADS // 2):
                at = 128 * pair
                query = qkv[:, at : at + 128] * jnp.asarray(HEAD_DIM**-0.5, BF)
                value = qkv[:, 2 * D + at : 2 * D + at + 128]
                scores = dot_nt(query, by_head(qkv[:, D + at : D + at + 128], low))
                expo = jnp.concatenate(
                    [
                        jnp.exp(part - jnp.max(part, axis=-1, keepdims=True)).astype(BF)
                        for part in (scores[:, :TOK], scores[:, TOK:])
                    ],
                    axis=1,
                )
                expo_out[slot, pair] = expo
                sums = by_head(jnp.ones((TOK, 128), BF), low)
                both = dot(expo, jnp.concatenate([by_head(value, low), sums], axis=1))
                inverse = 1.0 / both[:, 128:]
                rinv_out[slot, :, at : at + 128] = inverse
                mixed_out[slot, :, at : at + 128] = (both[:, :128] * inverse).astype(BF)


def middle_kernel(
    info, latents, conditions, mixed_in, grad_out, bias_in, p0, p1, p2, p3, p4, p5, p6, p7,
    weights, out, grad_mid_out, grad_mixed_out, grad_mod, keep, send,
    mod, acc_up, acc_down, acc_proj, acc_bias, down,
):
    step = pl.program_id(0)

    @pl.when(step == 0)
    def _():
        pieces = (p0, p1, p2, p3, p4, p5, p6, p7)
        assemble(info, [piece.at[:, :AT_DOWN] for piece in pieces], weights)
        column, z_high, core = info[1], info[2], info[3]
        for k in range(8):
            layer = (z_high ^ core) if k < 4 else 1 - (z_high ^ core)
            first = layer * 768 + lax.rem(column + k % 4, 4) * 192
            for q in range(4):
                down[pl.ds(pl.multiple_of(first + 48 * q, 16), 48), :] = pieces[k][
                    :, AT_DOWN + D * q : AT_DOWN + D * q + D
                ]
        cond_low = silu(conditions[...].astype(F32)).astype(BF)
        mod[...] = dot(cond_low, weights[:, AT_MOD : AT_MOD + MOD_TWO]) + bias_row(
            bias_in[...], ROW_MOD + 6, 12
        )
        acc_bias[...] = jnp.zeros_like(acc_bias)
        grad_mod[...] = jnp.zeros_like(grad_mod)

    @pl.when((step == 0) & (info[0] == 0))
    def _():
        acc_up[...] = jnp.zeros_like(acc_up)
        acc_down[...] = jnp.zeros_like(acc_down)
        acc_proj[...] = jnp.zeros_like(acc_proj)

    @pl.when(PAIR * step >= info[0])
    def _():
        out[...] = jnp.zeros((PAIR, TOK, D), BF)
        grad_mid_out[pl.ds(PAIR * step, PAIR)] = jnp.zeros((PAIR, TOK, D), F32)
        grad_mixed_out[pl.ds(PAIR * step, PAIR)] = jnp.zeros((PAIR, TOK, D), BF)

    @pl.when(PAIR * step < info[0])
    def _():
        def so_far(total):
            return jnp.where(step == 0, 0.0, total)

        bias = bias_in[...]
        w_proj = weights[:, AT_PROJ : AT_PROJ + D]
        up_bias = bias_row(bias, ROW_UP, 12)
        mixed = mixed_in[pl.ds(PAIR * step, PAIR)].reshape(PAIR * TOK, D)
        branch_all = dot(mixed, w_proj) + bias_row(bias, ROW_PROJ, 3)
        rows = [mod[pl.ds(PAIR * step + i, 1), :] for i in range(PAIR)]
        span = [slice(TOK * i, TOK * i + TOK) for i in range(PAIR)]
        middle, normed, inverse, hidden, cot, g_two = [], [], [], [], [], []
        for i in range(PAIR):
            row = rows[i]
            middle.append(latents[i].astype(F32) + row[:, :D] * branch_all[span[i]])
            value, scale = normalize(middle[i])
            normed.append(value)
            inverse.append(scale)
            hidden.append((value * (1.0 + row[:, 2 * D : 3 * D]) + row[:, D : 2 * D]).astype(BF))
            held = (PAIR * step + i < info[0]).astype(F32)
            cot.append(grad_out[i].astype(F32) * held)
            g_two.append((cot[i] * row[:, 3 * D :]).astype(BF))
        hidden = jnp.concatenate(hidden, axis=0)
        g_two = jnp.concatenate(g_two, axis=0)
        branch_two = bias_row(bias, ROW_DOWN, 3)
        d_hidden = jnp.zeros((PAIR * TOK, D), F32)
        root = 0.7978845608028654
        cube = root * 0.044715
        for chunk in range(FF // CHUNK):
            at = CHUNK * chunk
            w_up = weights[:, at : at + CHUNK]
            w_down = down[at : at + CHUNK, :]
            upward = dot(hidden, w_up) + up_bias[:, at : at + CHUNK]
            square = upward * upward
            bend = jnp.tanh(upward * (root + cube * square))
            half = 0.5 + 0.5 * bend
            act = upward * half
            slope = half + act * (1.0 - bend) * (root + (3.0 * cube) * square)
            act_low = act.astype(BF)
            branch_two = branch_two + dot(act_low, w_down)
            acc_down[at : at + CHUNK, :] = so_far(acc_down[at : at + CHUNK, :]) + dot_tn(act_low, g_two)
            g_up = (slope * dot_nt(g_two, w_down)).astype(BF)
            acc_up[:, at : at + CHUNK] = so_far(acc_up[:, at : at + CHUNK]) + dot_tn(hidden, g_up)
            acc_bias[0:1, at : at + CHUNK] += jnp.sum(g_up.astype(F32), axis=0, keepdims=True)
            d_hidden = d_hidden + dot_nt(g_up, w_up)
        acc_bias[1:2, :D] += jnp.sum(g_two.astype(F32), axis=0, keepdims=True)
        g_one = []
        for i in range(PAIR):
            row, slot = rows[i], PAIR * step + i
            d_hid, br_two = d_hidden[span[i]], branch_two[span[i]]
            held = (slot < info[0]).astype(F32)
            out[i] = ((middle[i] + row[:, 3 * D :] * br_two) * held).astype(BF)
            grad_mod[pl.ds(slot, 1), 3 * D :] = jnp.sum(cot[i] * br_two, axis=0, keepdims=True)
            grad_mod[pl.ds(slot, 1), D : 2 * D] = jnp.sum(d_hid, axis=0, keepdims=True)
            grad_mod[pl.ds(slot, 1), 2 * D : 3 * D] = jnp.sum(
                d_hid * normed[i], axis=0, keepdims=True
            )
            grad_mid = cot[i] + norm_back(
                d_hid * (1.0 + row[:, 2 * D : 3 * D]), normed[i], inverse[i]
            )
            grad_mid_out[slot] = grad_mid
            grad_mod[pl.ds(slot, 1), :D] = jnp.sum(
                grad_mid * branch_all[span[i]], axis=0, keepdims=True
            )
            g_one.append((grad_mid * row[:, :D]).astype(BF))
        g_one = jnp.concatenate(g_one, axis=0)
        acc_bias[2:3, :D] += jnp.sum(g_one.astype(F32), axis=0, keepdims=True)
        acc_proj[...] = so_far(acc_proj[...]) + dot_tn(mixed, g_one)
        grad_mixed_out[pl.ds(PAIR * step, PAIR)] = (
            dot_nt(g_one, w_proj).astype(BF).reshape(PAIR, TOK, D)
        )

    @pl.when(step == STEPS - 1)
    def _():
        cond_low = silu(conditions[...].astype(F32)).astype(BF)
        g_mod = grad_mod[...].astype(BF)
        mod_grad = dot_tn(cond_low.astype(F32), g_mod.astype(F32)).astype(BF)
        z_high, core, column = info[2], info[3], info[1]
        sums = jnp.sum(g_mod.astype(F32), axis=0, keepdims=True)
        rows = [jnp.zeros((ROW_MOD + 6, 128), F32)]
        rows += [sums[:, 128 * i : 128 * i + 128] for i in range(12)]
        rows += [acc_bias[2:3, 128 * i : 128 * i + 128] for i in range(3)]
        rows += [acc_bias[0:1, 128 * i : 128 * i + 128] for i in range(12)]
        rows += [acc_bias[1:2, 128 * i : 128 * i + 128] for i in range(3)]
        rows += [jnp.zeros((3, 128), F32)]
        bias_block = jnp.concatenate(rows, axis=0).astype(BF)
        for owner in range(8):
            zh, xx = owner // 4, owner % 4
            spot = lax.rem(xx - column + 4, 4) * 48
            spot = pl.multiple_of(spot, 16)
            is_mine = (z_high ^ core) == zh
            lo = 48 * owner

            def put(ref, spot=spot, lo=lo, owner=owner):
                ref[pl.ds(spot, 48), :FF] = acc_up[lo : lo + 48, :].astype(BF)
                ref[pl.ds(spot, 48), AT_MOD : AT_MOD + MOD_TWO] = mod_grad[lo : lo + 48, :]
                ref[pl.ds(spot, 48), AT_PROJ : AT_PROJ + D] = acc_proj[lo : lo + 48, :].astype(BF)
                for q in range(4):
                    at = 192 * owner + 48 * q
                    ref[pl.ds(spot, 48), AT_DOWN + D * q : AT_DOWN + D * q + D] = acc_down[
                        at : at + 48, :
                    ].astype(BF)
                ref[pl.ds(spot, 48), BIAS_TWO : BIAS_TWO + 128] = bias_block

            pl.when(is_mine)(functools.partial(put, keep))
            pl.when(jnp.logical_not(is_mine))(functools.partial(put, send))


def backward_kernel(
    info, latents, conditions, qkv_in, expo_in, mixed_in, rinv_in, hidden_in, grad_mid_in,
    grad_mixed_in, mod_in, weights, weights_two, grad_mod_two,
    out, grad_cond, keep, send,
    acc_qkv, acc_bias, grad_mod,
):
    step = pl.program_id(0)
    slot = QUAD * step

    @pl.when(step == 0)
    def _():
        acc_qkv[...] = jnp.zeros_like(acc_qkv)
        acc_bias[...] = jnp.zeros_like(acc_bias)
        grad_mod[...] = jnp.zeros_like(grad_mod)

    @pl.when(slot >= info[0])
    def _():
        out[...] = jnp.zeros((QUAD, TOK, D), BF)

    @pl.when(slot < info[0])
    def _():
        low = lax.broadcasted_iota(jnp.int32, (TOK, 128), 1) < HEAD_DIM
        factor = HEAD_DIM**-0.5
        g_all = []
        for i in range(QUAD):
            qkv = qkv_in[slot + i]
            scaled = (grad_mixed_in[slot + i].astype(F32) * rinv_in[slot + i]).astype(BF)
            product = scaled.astype(F32) * mixed_in[slot + i].astype(F32)
            g_query, g_key, g_value = [], [], []
            for pair in range(HEADS // 2):
                at = 128 * pair
                query = qkv[:, at : at + 128]
                key = by_head(qkv[:, D + at : D + at + 128], low)
                value = by_head(qkv[:, 2 * D + at : 2 * D + at + 128], low)
                grad = scaled[:, at : at + 128]
                weighed = product[:, at : at + 128]
                expo = expo_in[slot + i, pair]
                g_probs = dot_nt(grad, value)
                g_scores = []
                for half in range(2):
                    mask = low if half == 0 else ~low
                    delta = jnp.sum(jnp.where(mask, weighed, 0.0), axis=-1, keepdims=True)
                    lanes = slice(TOK * half, TOK * half + TOK)
                    g_scores.append(
                        (expo[:, lanes].astype(F32) * (g_probs[:, lanes] - delta)).astype(BF)
                    )
                g_scores = jnp.concatenate(g_scores, axis=1)
                d_key, d_value = dot_tn(g_scores, query), dot_tn(expo, grad)
                g_query.append((dot(g_scores, key) * factor).astype(BF))
                g_key.append((jnp.where(low, d_key[:TOK], d_key[TOK:]) * factor).astype(BF))
                g_value.append(jnp.where(low, d_value[:TOK], d_value[TOK:]).astype(BF))
            g_all.append(jnp.concatenate(g_query + g_key + g_value, axis=1))
        g_qkv = jnp.concatenate(g_all, axis=0)
        hidden = hidden_in[pl.ds(slot, QUAD)].reshape(QUAD * TOK, D)
        acc_qkv[...] += dot_tn(hidden, g_qkv)
        acc_bias[0:1, :] += jnp.sum(g_qkv.astype(F32), axis=0, keepdims=True)
        d_all = dot_nt(g_qkv, weights[:, :QKV_W])
        for i in range(QUAD):
            row = mod_in[pl.ds(slot + i, 1), :]
            normed, inverse = normalize(latents[i].astype(F32))
            d_hidden = d_all[TOK * i : TOK * i + TOK]
            grad_mod[pl.ds(slot + i, 1), :D] = jnp.sum(d_hidden, axis=0, keepdims=True)
            grad_mod[pl.ds(slot + i, 1), D:] = jnp.sum(d_hidden * normed, axis=0, keepdims=True)
            back = norm_back(d_hidden * (1.0 + row[:, D : 2 * D]), normed, inverse)
            out[i] = (grad_mid_in[slot + i] + back).astype(BF)

    @pl.when(step == CAP // QUAD - 1)
    def _():
        cond = conditions[...].astype(F32)
        sig = 1.0 / (1.0 + jnp.exp(-cond))
        cond_low = (cond * sig).astype(BF)
        g_mod = grad_mod[...].astype(BF)
        g_mod_two = grad_mod_two[...].astype(BF)
        g_cond = dot_nt(g_mod, weights[:, QKV_W : QKV_W + MOD_ONE])
        g_cond += dot_nt(g_mod_two, weights_two[:, AT_MOD : AT_MOD + MOD_TWO])
        grad_cond[...] = (g_cond * (sig * (1.0 + cond * (1.0 - sig)))).astype(BF)
        mod_grad = dot_tn(cond_low.astype(F32), g_mod.astype(F32)).astype(BF)
        sums = jnp.sum(g_mod.astype(F32), axis=0, keepdims=True)
        rows = [acc_bias[0:1, 128 * i : 128 * i + 128] for i in range(9)]
        rows += [sums[:, 128 * i : 128 * i + 128] for i in range(6)]
        rows += [jnp.zeros((33, 128), F32)]
        bias_block = jnp.concatenate(rows, axis=0).astype(BF)
        z_high, core, column = info[2], info[3], info[1]
        for owner in range(8):
            zh, xx = owner // 4, owner % 4
            spot = pl.multiple_of(lax.rem(xx - column + 4, 4) * 48, 16)
            is_mine = (z_high ^ core) == zh
            lo = 48 * owner

            def put(ref, spot=spot, lo=lo):
                ref[pl.ds(spot, 48), :QKV_W] = acc_qkv[lo : lo + 48, :].astype(BF)
                ref[pl.ds(spot, 48), QKV_W : QKV_W + MOD_ONE] = mod_grad[lo : lo + 48, :]
                ref[pl.ds(spot, 48), BIAS_ONE : BIAS_ONE + 128] = bias_block

            pl.when(is_mine)(functools.partial(put, keep))
            pl.when(jnp.logical_not(is_mine))(functools.partial(put, send))


def slot_spec(group):
    def index(j, info):
        return (jnp.minimum(j, jnp.maximum((info[0] + group - 1) // group - 1, 0)), 0, 0)

    return pl.BlockSpec((group, TOK, D), index)


def slot_out(group):
    return pl.BlockSpec((group, TOK, D), lambda j, info: (j, 0, 0))


def held():
    return pl.BlockSpec(memory_space=pltpu.VMEM)


def whole(*shape):
    zeros = (0,) * len(shape)
    return pl.BlockSpec(shape, lambda j, info: zeros)


def params(mib):
    return pltpu.CompilerParams(
        dimension_semantics=("arbitrary",), vmem_limit_bytes=mib * MIB
    )


def far(value):
    return pltpu.with_memory_space_constraint(value, pltpu.HBM)


def stay(value):
    return pltpu.with_memory_space_constraint(value, pltpu.VMEM)


def run_forward(info, latents, conditions, pieces):
    return pl.pallas_call(
        forward_kernel,
        grid_spec=pltpu.PrefetchScalarGridSpec(
            num_scalar_prefetch=1,
            grid=(CAP // QUAD,),
            in_specs=[slot_spec(QUAD), whole(CAP, D)] + [held()] * 8,
            out_specs=[held()] * 8,
        ),
        out_shape=[
            pltpu.VMEM((D, LANES_ONE), BF),
            pltpu.VMEM((48, 128), F32),
            pltpu.VMEM((CAP, MOD_ONE), F32),
            pltpu.VMEM((CAP, TOK, QKV_W), BF),
            pltpu.VMEM((CAP, HEADS // 2, TOK, 2 * TOK), BF),
            pltpu.VMEM((CAP, TOK, D), BF),
            pltpu.VMEM((CAP, TOK, D), F32),
            pltpu.VMEM((CAP, TOK, D), BF),
        ],
        compiler_params=params(12),
        name="attention_forward",
        cost_estimate=pl.CostEstimate(
            flops=3_000_000_000, bytes_accessed=20_000_000, transcendentals=3_000_000
        ),
    )(info, far(latents), far(conditions), *pieces)


def run_middle(info, latents, conditions, mixed, grad_out, bias, pieces):
    return pl.pallas_call(
        middle_kernel,
        grid_spec=pltpu.PrefetchScalarGridSpec(
            num_scalar_prefetch=1,
            grid=(CAP // PAIR,),
            in_specs=[
                slot_spec(PAIR),
                whole(CAP, D),
                held(),
                slot_spec(PAIR),
                held(),
            ]
            + [held()] * 8,
            out_specs=[held(), slot_out(PAIR)] + [held()] * 5,
            scratch_shapes=[
                pltpu.VMEM((CAP, MOD_TWO), F32),
                pltpu.VMEM((D, FF), F32),
                pltpu.VMEM((FF, D), F32),
                pltpu.VMEM((D, D), F32),
                pltpu.VMEM((8, FF), F32),
                pltpu.VMEM((FF, D), BF),
            ],
        ),
        out_shape=[
            pltpu.VMEM((D, AT_DOWN), BF),
            jax.ShapeDtypeStruct((CAP, TOK, D), BF),
            pltpu.VMEM((CAP, TOK, D), F32),
            pltpu.VMEM((CAP, TOK, D), BF),
            pltpu.VMEM((CAP, MOD_TWO), F32),
            pltpu.VMEM((192, LANES_TWO), BF),
            pltpu.VMEM((192, LANES_TWO), BF),
        ],
        compiler_params=params(23),
        name="feed_forward_both_ways",
        cost_estimate=pl.CostEstimate(
            flops=16_000_000_000, bytes_accessed=30_000_000, transcendentals=3_000_000
        ),
    )(info, far(latents), far(conditions), stay(mixed), far(grad_out), stay(bias), *pieces)


def run_backward(info, latents, conditions, *values):
    return pl.pallas_call(
        backward_kernel,
        grid_spec=pltpu.PrefetchScalarGridSpec(
            num_scalar_prefetch=1,
            grid=(CAP // QUAD,),
            in_specs=[slot_spec(QUAD), whole(CAP, D)] + [held()] * 11,
            out_specs=[slot_out(QUAD), whole(CAP, D), held(), held()],
            scratch_shapes=[
                pltpu.VMEM((D, QKV_W), F32),
                pltpu.VMEM((8, QKV_W), F32),
                pltpu.VMEM((CAP, MOD_ONE), F32),
            ],
        ),
        out_shape=[
            jax.ShapeDtypeStruct((CAP, TOK, D), BF),
            jax.ShapeDtypeStruct((CAP, D), BF),
            pltpu.VMEM((192, LANES_ONE), BF),
            pltpu.VMEM((192, LANES_ONE), BF),
        ],
        compiler_params=params(12),
        name="attention_backward",
        cost_estimate=pl.CostEstimate(
            flops=25_000_000_000, bytes_accessed=20_000_000, transcendentals=1_000
        ),
    )(info, far(latents), far(conditions), *map(stay, values))


def place(index):
    shard, rep = divmod(index, 16)
    return shard // 4, shard % 4, rep // 4, (rep // 2) % 2, rep % 2


def index_of(z_high, x, y, z_low, core):
    return (z_high * 4 + x) * 16 + y * 4 + z_low * 2 + core


def routes(target_of):
    return [(i, target_of(*place(i))) for i in range(TWIN)]


def fetch(k):
    def source(zh, x, y, zl, c):
        if c == 0:
            return index_of(zh, (x + k) % 4, y, zl, c)
        return index_of(1 - zh, (x + k) % 4, y, 1 - zl, c)

    return [(source(*place(i)), i) for i in range(TWIN)]


CORE_SWAP = routes(lambda zh, x, y, zl, c: index_of(zh, x, y, zl, 1 - c))
ZLOW_SWAP = routes(lambda zh, x, y, zl, c: index_of(zh, x, y, 1 - zl, c))
BOTH = ("shard", "rep")


def move(value, pairs):
    return lax.ppermute(value, BOTH, pairs)


def y_route(k):
    return routes(lambda zh, x, y, zl, c: index_of(zh, x, (y + k) % 4, zl, c))


def after(value, *earlier):
    return lax.optimization_barrier((value, *earlier))[0]


def fetch_all(block):
    return [move(block, fetch(k)) for k in range(4)]


def swap_all(pieces):
    return [move(piece, CORE_SWAP) for piece in pieces]


def small_call(kernel, name, shapes, *values, scalars=False):
    return pl.pallas_call(
        kernel,
        in_specs=[pl.BlockSpec(memory_space=pltpu.SMEM)] * scalars
        + [held()] * (len(values) - scalars),
        out_shape=[jax.ShapeDtypeStruct(shape, BF) for shape in shapes],
        compiler_params=pltpu.CompilerParams(vmem_limit_bytes=14 * MIB),
        name=name,
    )(*values)


def add_kernel(*refs):
    refs[-1][...] = sum(ref[...].astype(F32) for ref in refs[:-1]).astype(BF)


def add(*values):
    return small_call(add_kernel, "add", [values[0].shape], *values)[0]


def add_blocks_kernel(left, right, *outs):
    for k, out in enumerate(outs):
        rows = slice(48 * k, 48 * k + 48)
        out[...] = (left[rows, :].astype(F32) + right[rows, :].astype(F32)).astype(BF)


def add_blocks(left, right):
    shape = (48, left.shape[1])
    return small_call(add_blocks_kernel, "add_blocks", [shape] * 4, left, right)


def add_halves_kernel(info, *refs):
    lanes = refs[-1].shape[1]
    for out, core in ((refs[-2], info[3]), (refs[-1], 1 - info[3])):
        at = pl.ds(pl.multiple_of(core * lanes, 128), lanes)
        out[...] = sum(ref[:, at].astype(F32) for ref in refs[:-2]).astype(BF)


def add_halves(info, pieces):
    shape = (48, pieces[0].shape[1] // 2)
    return small_call(
        add_halves_kernel, "add_halves", [shape] * 2, info, *pieces, scalars=True
    )


def scatter(blocks):
    back = [[(target, source) for source, target in fetch(k)] for k in range(4)]
    return [move(block, pairs) for block, pairs in zip(blocks, back)]


def sum_low(arrived, info, *earlier):
    mine, other = add_halves(info, arrived)
    total = add(mine, move(other, CORE_SWAP))
    if earlier:
        total = after(total, *earlier)
    return add(total, move(total, ZLOW_SWAP))


def sum_rows(total, *earlier):
    rows = [move(total, y_route(k)) for k in (1, 2, 3)]
    total = add(after(total, *earlier), *rows)
    return [total, move(total, CORE_SWAP)]


def row_of(ref):
    size = ref.shape[0]
    row = ref[...].astype(F32).reshape(1, size)
    if size % 128:
        row = jnp.concatenate([row, jnp.zeros((1, -size % 128), F32)], axis=1)
    return row


def pack_one_kernel(qkv, mod, qv_bias, mod_bias, proj_bias, up_bias, down_bias, out):
    out[:, :QKV_W] = qkv[...]
    out[:, QKV_W:BIAS_ONE] = mod[:, :MOD_ONE]
    flat = [row_of(ref) for ref in (qv_bias, mod_bias, proj_bias, up_bias, down_bias)]
    flat = jnp.concatenate(flat, axis=1)
    rows = [flat[:, 128 * i : 128 * i + 128] for i in range(8)] + [jnp.zeros((40, 128), F32)]
    out[:, BIAS_ONE:] = jnp.concatenate(rows, axis=0).astype(BF)


def pack_two_kernel(up, mod, proj, down, out):
    out[:, :FF] = up[...]
    out[:, AT_MOD:AT_PROJ] = mod[:, MOD_ONE:]
    out[:, AT_PROJ:AT_DOWN] = proj[...]
    for q in range(4):
        out[:, AT_DOWN + D * q : AT_DOWN + D * q + D] = down[48 * q : 48 * q + 48, :]


def pack(kernel, name, lanes, *values):
    def once(shape):
        return pl.BlockSpec(shape, lambda j: (0,) * len(shape))

    return pl.pallas_call(
        kernel,
        grid=(1,),
        in_specs=[once(value.shape) for value in values],
        out_specs=once((48, lanes)),
        out_shape=pltpu.VMEM((48, lanes), BF),
        compiler_params=pltpu.CompilerParams(vmem_limit_bytes=8 * MIB),
        name=name,
    )(*map(far, values))


def joined(info, mine, other):
    first = info[3] == 0
    mine, other = mine[...].astype(F32), other[...].astype(F32)
    return jnp.concatenate([jnp.where(first, mine, other), jnp.where(first, other, mine)], axis=1)


def unpack_two_kernel(info, mine, other, g_mod, g_proj, g_up, g_down, bias):
    two = joined(info, mine, other)
    g_mod[:, MOD_ONE:] = two[:, AT_MOD:AT_PROJ]
    g_proj[...] = two[:, AT_PROJ:AT_DOWN]
    g_up[...] = two[:, :FF]
    for q in range(4):
        g_down[48 * q : 48 * q + 48, :] = two[:, AT_DOWN + D * q : AT_DOWN + D * q + D]
    bias[...] = two[:, BIAS_TWO:]


def unpack_one_kernel(
    info, mine, other, bias_two, _, g_mod, g_mod_bias, g_qkv, g_qv_bias, g_proj_bias, g_up_bias,
    g_down_bias,
):
    shard = info[1] + 4 * info[2]
    one = joined(info, mine, other)
    g_mod[...] = one[:, QKV_W:BIAS_ONE]
    g_qkv[...] = one[:, :QKV_W]
    bias = one[:, BIAS_ONE:] + bias_two[...]

    def own(row, size, out):
        row = jnp.broadcast_to(row, (8, row.shape[1]))
        turn = lax.rem(8 * size - shard * size, 8 * size)
        out[...] = pltpu.roll(row, turn, 1)[0:1, :size].reshape(size)

    own(bias_row(bias, ROW_MOD, 18), 288, g_mod_bias)
    own(jnp.concatenate([bias_row(bias, 0, 3), bias_row(bias, 6, 3)], axis=1), 96, g_qv_bias)
    own(bias_row(bias, ROW_PROJ, 3), 48, g_proj_bias)
    own(bias_row(bias, ROW_UP, 12), 192, g_up_bias)
    own(bias_row(bias, ROW_DOWN, 3), 48, g_down_bias)


SCALARS = pl.BlockSpec(memory_space=pltpu.SMEM)


def unpack_two(info, parts):
    shapes = [(48, 6 * D), (48, D), (48, FF), (192, D), (48, 128)]
    return pl.pallas_call(
        unpack_two_kernel,
        in_specs=[SCALARS] + [held()] * 2,
        out_shape=[jax.ShapeDtypeStruct(shape, F32) for shape in shapes],
        compiler_params=pltpu.CompilerParams(vmem_limit_bytes=12 * MIB),
        name="unpack_second_batch",
    )(info, *parts)


def unpack_one(info, parts, from_two):
    g_mod, g_proj, g_up, g_down, bias_two = from_two
    shapes = [(48, 6 * D), (288,), (48, QKV_W), (96,), (48,), (192,), (48,)]

    def once(shape):
        return pl.BlockSpec(shape, lambda j: (0,) * len(shape))

    g_mod, g_mod_bias, g_qkv, g_qv_bias, g_proj_bias, g_up_bias, g_down_bias = pl.pallas_call(
        unpack_one_kernel,
        grid=(1,),
        in_specs=[SCALARS] + [held()] * 3 + [pl.BlockSpec(memory_space=pl.ANY)],
        out_specs=[once((48, MOD_ONE))] + [once(shape) for shape in shapes[1:]],
        out_shape=[jax.ShapeDtypeStruct(shape, F32) for shape in shapes],
        input_output_aliases={4: 0},
        compiler_params=pltpu.CompilerParams(vmem_limit_bytes=8 * MIB),
        name="unpack_first_batch",
    )(info, *parts, bias_two, g_mod)
    return (
        g_mod, g_mod_bias, g_qkv, g_qv_bias, g_proj, g_proj_bias, g_up, g_up_bias, g_down,
        g_down_bias,
    )


def on_device(
    latents, conditions, counts, mod_weight, mod_bias, qkv_weight, qv_bias, proj_weight,
    proj_bias, up_weight, up_bias, down_weight, down_bias, grad_out,
):
    shard = lax.axis_index("shard")
    rep = lax.axis_index("rep")
    info = jnp.stack([counts[0], shard % 4, shard // 4, rep % 2]).astype(jnp.int32)
    block_one = pack(
        pack_one_kernel, "pack_attention_weights", LANES_ONE,
        after(qkv_weight, info), mod_weight, qv_bias, mod_bias, proj_bias, up_bias, down_bias,
    )
    block_two = pack(
        pack_two_kernel, "pack_feed_forward_weights", LANES_SENT,
        up_weight, mod_weight, proj_weight, down_weight,
    )
    mine_one = fetch_all(block_one)
    mine_two = [move(block_two, fetch(0))]
    other_one = swap_all([mine_one[0]] + [after(piece, block_two) for piece in mine_one[1:]])
    block_two = after(block_two, *mine_one)
    mine_two += [move(block_two, fetch(k)) for k in (1, 2, 3)]
    weights, bias, mod, qkv, expo, mixed, rinv, hidden = run_forward(
        info, latents, conditions, mine_one + other_one
    )
    mine_two = [after(piece, mod) for piece in mine_two]
    other_two = swap_all(mine_two)
    weights_two, out, grad_mid, grad_mixed, grad_mod_two, keep_two, send_two = run_middle(
        info, latents, conditions, mixed, grad_out, bias, mine_two + other_two
    )
    held_two = add_blocks(keep_two, move(send_two, CORE_SWAP))
    arrived_two = scatter(held_two)
    grad_latents, grad_cond, keep_one, send_one = run_backward(
        info, latents, conditions, qkv, expo, mixed, rinv, hidden, grad_mid, grad_mixed, mod,
        weights, weights_two, after(grad_mod_two, held_two[0]),
    )
    held_one = add_blocks(keep_one, move(after(send_one, *arrived_two), CORE_SWAP))
    arrived_one = scatter(held_one)
    low_two = sum_low(arrived_two, info, *held_one)
    low_one = sum_low(arrived_one, info)
    from_two = unpack_two(info, sum_rows(low_two, low_one))
    one = sum_rows(low_one, from_two[1])
    return (out, grad_latents, grad_cond, *unpack_one(info, one, from_two))


def solution(mesh):
    slots = P(("shard", "rep"), None, None)
    rows = P(("shard", "rep"), None)
    matrix, vector = P("shard", None), P("shard")
    in_specs = (slots, rows, P(("shard", "rep"))) + (matrix, vector) * 5 + (slots,)
    out_specs = (slots, slots, rows) + (matrix, vector) * 5
    return jax.shard_map(
        on_device, mesh=mesh, in_specs=in_specs, out_specs=out_specs, check_vma=False
    )
```
